512 devices in a mesh: frame: 8 (over z_lo, core), seg: 16 (over z_hi, x), coil: 4 (over y).
Axes of the slice: x: 4, y: 4, z: 16 (z_hi: 4, z_lo: 4; z = z_hi * 4 + z_lo), core: 2. Of those that a mesh axis runs over, the one named last changes fastest.
Arguments:
- cal_source: bfloat16 [128, 4608, 384], P('seg', 'frame'), may hold values from -6 to 6
- cal_target: bfloat16 [128, 32, 2, 4608], P('seg', 'coil', None, 'frame'), may hold values from -6 to 6
- app_source: bfloat16 [8, 64, 128, 384], P('frame', 'seg'), may hold values from -6 to 6
- readers: int32 [8, 64], P('frame', 'seg'), may hold values from 0 to 127
- blocks: int32 [8, 64], P('frame', 'seg'), may hold values from 0 to 15
- interp: bfloat16 [8, 64, 256, 128], P('frame', 'seg'), may hold values from -0.5 to 0.5
Outputs:
- combined: float32 [8, 4096], P('frame', 'seg')
The draws below stay inside these ranges and needn't reach their ends.
All inputs are finite; a program needn't handle non-finite values.
Results may differ from the reference program's by a relative error of at most 0.0025.
Values may be sent and summed in bfloat16 or wider, within the bound.
No kernel may reach another device: no remote copies, remote signals or barrier semaphores. Data moves between devices by JAX's collectives and lax.ppermute only.
A program may use at most 128 MiB of HBM per device.

```python
import math
import jax
import jax.numpy as jnp
import numpy as np
from jax import lax

NS = 192
NC = 32
SLOT = 128
GB = 256
SEGS = 128
CAL = 4608
APP_FR = 8
GROUPS = 64
N_SEG = 16


latent_count = 64


def shared_latents(key, spread):
    latent_key = jax.random.fold_in(key, 0)
    latents = jax.random.normal(latent_key, (SEGS, CAL, latent_count), jnp.float32)
    position = jnp.arange(latent_count, dtype=jnp.float32) / (latent_count - 1)
    latent_power = jnp.exp(-jnp.log(spread) * position)
    amplitude = jnp.sqrt(latent_power / jnp.sum(latent_power))
    return (latents, amplitude)


def draw_cal_source(key, part):
    latents, amplitude = shared_latents(key, 1000.0)
    noise_level = 0.1
    key = jax.random.fold_in(key, 3)
    mix_key, noise_key = jax.random.split(key)
    mixing = jax.random.normal(mix_key, (SEGS, latent_count, 2 * NS), jnp.float32) * amplitude[None, :, None]
    clean_part = jnp.einsum('gcr,grk->gck', latents, mixing, precision=lax.Precision.HIGHEST)
    noise_part = noise_level * jax.random.normal(noise_key, (SEGS, CAL, 2 * NS), jnp.float32)
    return jnp.clip(clean_part + noise_part, -6.0, 6.0).astype(jnp.bfloat16)


def draw_cal_target(key, part):
    latents, amplitude = shared_latents(key, 1000.0)
    noise_level = 0.05
    key = jax.random.fold_in(key, 7)
    mix_key, noise_key = jax.random.split(key)
    coupling = 0.5 * jax.random.normal(mix_key, (SEGS, NC, 2, latent_count), jnp.float32) * amplitude[None, None, None, :]
    clean_part = jnp.einsum('gcr,gjtr->gjtc', latents, coupling, precision=lax.Precision.HIGHEST)
    noise_part = noise_level * jax.random.normal(noise_key, (SEGS, NC, 2, CAL), jnp.float32)
    return jnp.clip(clean_part + noise_part, -6.0, 6.0).astype(jnp.bfloat16)


def with_ends(values, stream_key, low, largest):
    longest = values.shape.index(max(values.shape))
    spots = []
    for shift in (0, 1):
        where = [jax.random.randint(jax.random.fold_in(stream_key, axis), (), 0, length) for axis, length in enumerate(values.shape)]
        where[longest] = (where[longest] + shift) % values.shape[longest]
        spots.append(tuple(where))
    return values.at[spots[0]].set(low).at[spots[1]].set(largest)


def block_levels(stream_key, dims, shards, low, high):
    loudness = 1.0
    for axis_at, blocks in shards:
        heights = jax.random.uniform(jax.random.fold_in(jax.random.fold_in(stream_key, 6), axis_at), (blocks,), jnp.float32, low / len(shards), high / len(shards))
        loudness = loudness * jnp.repeat(jnp.exp(heights), dims[axis_at] // blocks).reshape((-1,) + (1,) * (len(dims) - 1 - axis_at))
    return loudness


def cumulative_ranks(amount, lean):
    weights = [(1 << 20) // math.isqrt(standing ** lean) + 1 for standing in range(1, amount + 1)]
    deviation = 1 + sum(weights) // (1 << 30)
    return np.cumsum(np.array([max(1, weight // deviation) for weight in weights]))


def ranked_ids(key, shape, count, slope):
    listing = cumulative_ranks(count, slope)
    ticket = jax.random.randint(jax.random.fold_in(key, 1), shape, 0, int(listing[count - 1]))
    grade = jnp.searchsorted(jnp.asarray(listing, jnp.int32), ticket, side="right")
    return jax.random.permutation(jax.random.fold_in(key, 2), count)[grade].astype(jnp.int32)


def scatter_about(stream_key, extent, scale, most, pieces=(), kind=jnp.bfloat16):
    array = scale * jax.random.normal(stream_key, extent, jnp.float32)
    if pieces:
        array = array * block_levels(stream_key, extent, pieces, -0.22, 0.18)
    return jnp.clip(array, -most, most).astype(kind)


def setup_inputs(seed: int = 0) -> dict:
    arg_keys = jax.random.split(jax.random.key(seed), 7)
    cal_source = draw_cal_source(jax.random.fold_in(arg_keys[6], 71), 0)
    cal_target = draw_cal_target(jax.random.fold_in(arg_keys[6], 71), 0)
    app_source = scatter_about(arg_keys[2], (APP_FR, GROUPS, SLOT, 2 * NS), 1.0, 6.0, ((0, 8), (1, 16)))
    readers = with_ends(ranked_ids(arg_keys[3], (APP_FR, GROUPS), SEGS, 2), jax.random.fold_in(arg_keys[3], 3), 0, SEGS - 1).astype(jnp.int32)
    blocks = with_ends(jax.random.randint(arg_keys[4], (APP_FR, GROUPS), 0, N_SEG), jax.random.fold_in(arg_keys[4], 1), 0, N_SEG - 1).astype(jnp.int32)
    interp = scatter_about(arg_keys[5], (APP_FR, GROUPS, GB, SLOT), SLOT ** -0.5, 0.5, ((0, 8), (1, 16)))
    return dict(cal_source=cal_source, cal_target=cal_target, app_source=app_source, readers=readers, blocks=blocks, interp=interp)


regular = 0.02
epsilon = 1e-06

def gram_terms(source, target):
    width = source.shape[1] // 2
    gram = jnp.dot(source.T.astype(jnp.float32), source.astype(jnp.float32), preferred_element_type=jnp.float32)
    gram_real = gram[:width, :width] + gram[width:, width:]
    gram_imag = gram[:width, width:] - gram[width:, :width]
    proj_real = jnp.dot(target[:, 0, :].astype(jnp.float32), source.astype(jnp.float32), preferred_element_type=jnp.float32)
    proj_imag = jnp.dot(target[:, 1, :].astype(jnp.float32), source.astype(jnp.float32), preferred_element_type=jnp.float32)
    rhs_real = proj_real[:, :width] + proj_imag[:, width:]
    rhs_imag = proj_imag[:, :width] - proj_real[:, width:]
    return (gram_real, gram_imag, jnp.concatenate([rhs_real, rhs_imag], axis=1))

def weights_from(gram_real, gram_imag, right_side):
    width = gram_real.shape[0]
    upper = jnp.concatenate([gram_real, -gram_imag], axis=1)
    lower = jnp.concatenate([gram_imag, gram_real], axis=1)
    system = jnp.concatenate([upper, lower], axis=0)
    shift_value = regular * jnp.trace(gram_real) / width
    system = system + shift_value * jnp.eye(2 * width, dtype=system.dtype)
    factor = jnp.linalg.cholesky(system)
    middle = jax.scipy.linalg.solve_triangular(factor, right_side.T, lower=True)
    solved = jax.scipy.linalg.solve_triangular(factor, middle, lower=True, trans=1)
    return solved.T.astype(jnp.bfloat16)

def apply_rows(chosen):
    width = chosen.shape[-1] // 2
    part_real = chosen[..., :width]
    part_imag = chosen[..., width:]
    top_rows = jnp.concatenate([part_real, -part_imag], axis=-1)
    bottom_rows = jnp.concatenate([part_imag, part_real], axis=-1)
    return jnp.concatenate([top_rows, bottom_rows], axis=-2)

def reference(cal_source, cal_target, app_source, readers, blocks, interp):

    def one_segment(packed):
        source, target = packed
        gram_real, gram_imag, right_side = gram_terms(source, target)
        return weights_from(gram_real, gram_imag, right_side)
    weights = lax.map(one_segment, (cal_source, cal_target))

    def one_frame(packed):
        source, reads, places, interp_frame = packed
        chosen = weights[reads]
        matrix = apply_rows(chosen)
        filled = jnp.einsum('gjk,gsk->gjs', matrix.astype(jnp.float32), source.astype(jnp.float32)).astype(jnp.bfloat16)
        contrib = jnp.einsum('gjs,gcs->gjc', filled.astype(jnp.float32), interp_frame.astype(jnp.float32))
        hits = (places[:, None] == jnp.arange(N_SEG, dtype=jnp.int32)[None, :]).astype(jnp.float32)
        grid = jnp.einsum('gb,gjc->bjc', hits, contrib, precision=lax.Precision.HIGHEST)
        power = lax.optimization_barrier(jnp.sum(grid * grid, axis=1))
        return jnp.sqrt(power + epsilon).reshape(-1)
    return lax.map(one_frame, (app_source, readers, blocks, interp))
```

```python
import functools

import jax
import jax.numpy as jnp
from jax import lax
from jax.experimental import pallas as pl
from jax.experimental.pallas import tpu as pltpu
from jax.sharding import PartitionSpec as P

regular = 0.02
epsilon = 1e-06
settled = 1e-7
F32 = jnp.float32
BF16 = jnp.bfloat16
LANES = 128
HIGHEST = lax.Precision.HIGHEST


def across_rows(left, right):
    return lax.dot_general(left, right, (((1,), (1,)), ((), ())), preferred_element_type=F32)


def gram_kernel(part, reads_ref, source_ref, target_ref, out_ref):
    coil = lax.axis_index("coil")
    source = source_ref[0]
    depth = source.shape[1]
    width = depth // 2
    row = lax.broadcasted_iota(jnp.int32, (2 * part, depth), 0)
    column = lax.broadcasted_iota(jnp.int32, (2 * part, depth), 1)
    wanted = coil * part + jnp.where(row < part, row, row - part + width)
    pick = jnp.where(column == wanted, 1.0, 0.0).astype(BF16)
    mine = across_rows(pick, source).astype(BF16)
    left = jnp.concatenate([mine, target_ref[0, :, 0, :], target_ref[0, :, 1, :]], axis=0)
    sums = jnp.dot(left, source, preferred_element_type=F32)
    top, bottom = sums[:part], sums[part : 2 * part]
    gram_real = top[:, :width] + bottom[:, width:]
    gram_imag = top[:, width:] - bottom[:, :width]
    across = lax.broadcasted_iota(jnp.int32, (part, width), 1)
    down = lax.broadcasted_iota(jnp.int32, (part, width), 0) + coil * part
    packed = jnp.where(across <= down, gram_real, gram_imag)
    coils = target_ref.shape[1]
    proj_real = sums[2 * part : 2 * part + coils]
    proj_imag = sums[2 * part + coils :]
    rhs_real = proj_real[:, :width] + proj_imag[:, width:]
    rhs_imag = proj_imag[:, :width] - proj_real[:, width:]
    half = part // 2
    out_ref[0, :part] = packed[:, :LANES]
    out_ref[0, part : part + half] = jnp.concatenate(
        [packed[:half, LANES:], packed[half:, LANES:]], axis=1
    )
    base = part + half
    out_ref[0, base : base + coils] = rhs_real[:, :LANES]
    out_ref[0, base + coils : base + 2 * coils] = rhs_imag[:, :LANES]
    out_ref[0, base + 2 * coils : base + 3 * coils] = jnp.concatenate(
        [rhs_real[:, LANES:], rhs_imag[:, LANES:]], axis=1
    )
    lane = lax.broadcasted_iota(jnp.int32, (8, LANES), 1)
    told = jnp.zeros((8, LANES), jnp.int32)
    for slot in range(reads_ref.shape[1]):
        told = jnp.where(lane == slot, reads_ref[0, slot], told)
    out_ref[0, base + 3 * coils :] = told.astype(F32)


def solve_kernel(part, gram_ref, rhs_ref, out_ref, real_ref, imag_ref, sol_ref):
    width = 4 * part
    half = part // 2
    coils = rhs_ref.shape[0] // 3
    pieces = []
    for coil in range(4):
        block = gram_ref[coil]
        tail = block[part:]
        pieces.append(
            jnp.concatenate(
                [block[:part], jnp.concatenate([tail[:, :64], tail[:, 64:]], axis=0)], axis=1
            )
        )
    packed = jnp.concatenate(pieces, axis=0)
    flipped = packed.T
    down = lax.broadcasted_iota(jnp.int32, (width, width), 0)
    across = lax.broadcasted_iota(jnp.int32, (width, width), 1)
    real = jnp.where(across <= down, packed, flipped)
    imag = jnp.where(across > down, packed, jnp.where(across < down, -flipped, 0.0))
    diagonal = jnp.where(across == down, packed, 0.0)
    shift = regular / width * jnp.sum(diagonal)
    high = jnp.sqrt(jnp.sum(real * real + imag * imag)) + shift
    scale = 2.0 / (high + shift)
    real_ref[...] = (real + jnp.where(across == down, shift, 0.0)) * scale
    imag_ref[...] = imag * scale
    rhs_real = jnp.concatenate([rhs_ref[:coils], rhs_ref[2 * coils :, :64]], axis=1)
    rhs_imag = jnp.concatenate([rhs_ref[coils : 2 * coils], rhs_ref[2 * coils :, 64:]], axis=1)
    sol_ref[...] = jnp.concatenate([rhs_real, rhs_imag], axis=0) * scale

    def step(spread):
        square = spread * spread
        factor = 2.0 / (2.0 - square)
        real, imag, sol = real_ref[...], imag_ref[...], sol_ref[...]
        first = jnp.dot(
            jnp.concatenate([real, sol], axis=0), imag, precision=HIGHEST, preferred_element_type=F32
        )
        second = jnp.dot(
            jnp.concatenate([real - imag, sol], axis=0),
            real + imag,
            precision=HIGHEST,
            preferred_element_type=F32,
        )
        cross, thin = first[:width], first[width:]
        turned = cross.T
        by_real = second[width:] - thin
        change = jnp.concatenate(
            [by_real[:coils] + thin[coils:], by_real[coils:] - thin[:coils]], axis=0
        )
        sol_ref[...] = factor * (2.0 * sol - change)
        real_ref[...] = factor * (2.0 * real - (second[:width] - cross - turned))
        imag_ref[...] = factor * (2.0 * imag - (cross - turned))
        return square / (2.0 - square)

    start = (high - shift) / (high + shift)
    lax.while_loop(lambda spread: spread > settled, step, start)
    sol = sol_ref[...]
    weights = jnp.concatenate([sol[:coils], sol[coils:]], axis=1).astype(BF16)
    for copy in range(out_ref.shape[0]):
        out_ref[copy] = weights


def select_kernel(seg_count, x_count, told_ref, piece_ref, out_ref):
    for frame in range(out_ref.shape[0]):
        for slot in range(out_ref.shape[1]):
            out_ref[frame, slot] = piece_ref[told_ref[frame, slot]]


def fill_kernel(reads_ref, places_ref, weights_ref, source_ref, interp_ref, out_ref, grid_ref):
    frames = weights_ref.shape[0]
    grid_ref[...] = jnp.zeros_like(grid_ref)
    for slot in range(weights_ref.shape[1]):
        chosen = weights_ref[lax.rem(reads_ref[0, slot], frames), slot].astype(F32)
        width = chosen.shape[1] // 2
        real, imag = chosen[:, :width], chosen[:, width:]
        matrix = jnp.concatenate(
            [jnp.concatenate([real, -imag], axis=1), jnp.concatenate([imag, real], axis=1)], axis=0
        ).astype(BF16)
        filled = across_rows(matrix, source_ref[0, slot]).astype(BF16)
        place = places_ref[0, slot]
        grid_ref[place] = grid_ref[place] + across_rows(filled, interp_ref[0, slot])
    out_ref[...] = grid_ref[...].astype(BF16)


def on_device(cal_source, cal_target, app_source, readers, blocks, interp):
    frames = lax.axis_size("frame")
    segs = lax.axis_size("seg")
    coil_count = lax.axis_size("coil")
    held, samples, depth = cal_source.shape
    coils = cal_target.shape[1]
    width = depth // 2
    part = width // coil_count
    gram_rows = part + part // 2
    rows = gram_rows + 3 * coils + 8
    slots = readers.shape[1]
    cells = interp.shape[2]

    partial = pl.pallas_call(
        functools.partial(gram_kernel, part),
        grid=(held,),
        in_specs=[
            pl.BlockSpec(memory_space=pltpu.SMEM),
            pl.BlockSpec((1, samples, depth), lambda g: (g, 0, 0)),
            pl.BlockSpec((1, coils, 2, samples), lambda g: (g, 0, 0, 0)),
        ],
        out_specs=pl.BlockSpec((1, rows, LANES), lambda g: (g, 0, 0)),
        out_shape=jax.ShapeDtypeStruct((held, rows, LANES), F32),
    )(readers, cal_source, cal_target)
    received = lax.all_to_all(partial, "frame", 0, 0, tiled=True)
    told = received[:, rows - 8, :slots].astype(jnp.int32) // frames
    owned = jnp.sum(received[:, : rows - 8], axis=0)
    spread = jnp.broadcast_to(owned[None, :gram_rows], (coil_count, gram_rows, LANES))
    gram = lax.all_to_all(spread, "coil", 0, 0, tiled=True)
    weights = pl.pallas_call(
        functools.partial(solve_kernel, part),
        out_shape=jax.ShapeDtypeStruct((segs, coils, depth), BF16),
        scratch_shapes=[
            pltpu.VMEM((width, width), F32),
            pltpu.VMEM((width, width), F32),
            pltpu.VMEM((2 * coils, width), F32),
        ],
    )(gram, owned[gram_rows:])
    pieces = lax.all_to_all(weights, "seg", 0, 0, tiled=True)
    sent = pl.pallas_call(
        functools.partial(select_kernel, segs, 4),
        in_specs=[
            pl.BlockSpec(memory_space=pltpu.SMEM),
            pl.BlockSpec(memory_space=pltpu.VMEM),
        ],
        out_shape=jax.ShapeDtypeStruct((frames, slots, coils, depth), BF16),
    )(told, pieces)
    chosen = lax.all_to_all(sent, "frame", 0, 0, tiled=True)
    grid = pl.pallas_call(
        fill_kernel,
        in_specs=[
            pl.BlockSpec(memory_space=pltpu.SMEM),
            pl.BlockSpec(memory_space=pltpu.SMEM),
            pl.BlockSpec(memory_space=pltpu.VMEM),
            pl.BlockSpec(memory_space=pltpu.VMEM),
            pl.BlockSpec(memory_space=pltpu.VMEM),
        ],
        out_shape=jax.ShapeDtypeStruct((segs, 2 * coils, cells), BF16),
        scratch_shapes=[pltpu.VMEM((segs, 2 * coils, cells), F32)],
    )(readers, blocks, chosen, app_source, interp)
    terms = lax.all_to_all(grid, "seg", 0, 0, tiled=True)
    total = jnp.sum(terms.astype(F32), axis=0)
    power = lax.psum(jnp.sum(total * total, axis=0, keepdims=True), "coil")
    return jnp.sqrt(power + epsilon)


def solution(mesh):
    placed = (
        P("seg", "frame", None),
        P("seg", "coil", None, "frame"),
        P("frame", "seg", None, None),
        P("frame", "seg"),
        P("frame", "seg"),
        P("frame", "seg", None, None),
    )
    return jax.shard_map(
        on_device, mesh=mesh, in_specs=placed, out_specs=P("frame", "seg"), check_vma=False
    )
```

```python
import functools

import jax
import jax.numpy as jnp
from jax import lax
from jax.experimental import pallas as pl
from jax.experimental.pallas import tpu as pltpu
from jax.sharding import PartitionSpec as P

regular = 0.02
epsilon = 1e-06
settled = 1e-7
F32 = jnp.float32
BF16 = jnp.bfloat16
LANES = 128
HIGHEST = lax.Precision.HIGHEST
SMALL = pltpu.CompilerParams(vmem_limit_bytes=16 * 1024 * 1024)


def across_rows(left, right):
    return lax.dot_general(left, right, (((1,), (1,)), ((), ())), preferred_element_type=F32)


def gram_kernel(part, frames, reads_ref, source_ref, target_ref, out_ref):
    coil = lax.axis_index("coil")
    source = source_ref[0]
    depth = source.shape[1]
    width = depth // 2
    row = lax.broadcasted_iota(jnp.int32, (2 * part, depth), 0)
    column = lax.broadcasted_iota(jnp.int32, (2 * part, depth), 1)
    wanted = coil * part + jnp.where(row < part, row, row - part + width)
    pick = jnp.where(column == wanted, 1.0, 0.0).astype(BF16)
    mine = across_rows(pick, source).astype(BF16)
    left = jnp.concatenate([mine, target_ref[0, :, 0, :], target_ref[0, :, 1, :]], axis=0)
    sums = jnp.dot(left, source, preferred_element_type=F32)
    top, bottom = sums[:part], sums[part : 2 * part]
    gram_real = top[:, :width] + bottom[:, width:]
    gram_imag = top[:, width:] - bottom[:, :width]
    across = lax.broadcasted_iota(jnp.int32, (part, width), 1)
    down = lax.broadcasted_iota(jnp.int32, (part, width), 0) + coil * part
    packed = jnp.where(across <= down, gram_real, gram_imag)
    coils = target_ref.shape[1]
    proj_real = sums[2 * part : 2 * part + coils]
    proj_imag = sums[2 * part + coils :]
    rhs_real = proj_real[:, :width] + proj_imag[:, width:]
    rhs_imag = proj_imag[:, :width] - proj_real[:, width:]
    half = part // 2
    out_ref[0, :part] = packed[:, :LANES]
    out_ref[0, part : part + half] = jnp.concatenate(
        [packed[:half, LANES:], packed[half:, LANES:]], axis=1
    )
    base = part + half
    out_ref[0, base : base + coils] = rhs_real[:, :LANES]
    out_ref[0, base + coils : base + 2 * coils] = rhs_imag[:, :LANES]
    out_ref[0, base + 2 * coils : base + 3 * coils] = jnp.concatenate(
        [rhs_real[:, LANES:], rhs_imag[:, LANES:]], axis=1
    )
    lane = lax.broadcasted_iota(jnp.int32, (8, LANES), 1)
    told = jnp.zeros((8, LANES), jnp.int32)
    for slot in range(reads_ref.shape[1]):
        told = jnp.where(lane == slot, lax.div(reads_ref[0, slot], frames), told)
    out_ref[0, base + 3 * coils :] = told.astype(F32)


def sum_kernel(gram_rows, partial_ref, spread_ref, rhs_ref, told_ref):
    rows = gram_rows + rhs_ref.shape[0]
    total = partial_ref[0, :rows]
    for frame in range(1, partial_ref.shape[0]):
        total = total + partial_ref[frame, :rows]
    for copy in range(spread_ref.shape[0]):
        spread_ref[copy] = total[:gram_rows]
    rhs_ref[...] = total[gram_rows:]
    told_ref[...] = partial_ref[:, rows, :].astype(jnp.int32)


def solve_kernel(part, gram_ref, rhs_ref, out_ref, real_ref, imag_ref, sol_ref):
    width = 4 * part
    half = part // 2
    coils = rhs_ref.shape[0] // 3
    pieces = []
    for coil in range(4):
        block = gram_ref[coil]
        tail = block[part:]
        pieces.append(
            jnp.concatenate(
                [block[:part], jnp.concatenate([tail[:, :64], tail[:, 64:]], axis=0)], axis=1
            )
        )
    packed = jnp.concatenate(pieces, axis=0)
    flipped = packed.T
    down = lax.broadcasted_iota(jnp.int32, (width, width), 0)
    across = lax.broadcasted_iota(jnp.int32, (width, width), 1)
    real = jnp.where(across <= down, packed, flipped)
    imag = jnp.where(across > down, packed, jnp.where(across < down, -flipped, 0.0))
    diagonal = jnp.where(across == down, packed, 0.0)
    shift = regular / width * jnp.sum(diagonal)
    high = jnp.sqrt(jnp.sum(real * real + imag * imag)) + shift
    scale = 2.0 / (high + shift)
    real_ref[...] = (real + jnp.where(across == down, shift, 0.0)) * scale
    imag_ref[...] = imag * scale
    rhs_real = jnp.concatenate([rhs_ref[:coils], rhs_ref[2 * coils :, :64]], axis=1)
    rhs_imag = jnp.concatenate([rhs_ref[coils : 2 * coils], rhs_ref[2 * coils :, 64:]], axis=1)
    sol_ref[...] = jnp.concatenate([rhs_real, rhs_imag], axis=0) * scale

    def step(spread):
        square = spread * spread
        factor = 2.0 / (2.0 - square)
        real, imag, sol = real_ref[...], imag_ref[...], sol_ref[...]
        first = jnp.dot(
            jnp.concatenate([real, sol], axis=0), imag, precision=HIGHEST, preferred_element_type=F32
        )
        second = jnp.dot(
            jnp.concatenate([real - imag, sol], axis=0),
            real + imag,
            precision=HIGHEST,
            preferred_element_type=F32,
        )
        cross, thin = first[:width], first[width:]
        turned = cross.T
        by_real = second[width:] - thin
        change = jnp.concatenate(
            [by_real[:coils] + thin[coils:], by_real[coils:] - thin[:coils]], axis=0
        )
        sol_ref[...] = factor * (2.0 * sol - change)
        real_ref[...] = factor * (2.0 * real - (second[:width] - cross - turned))
        imag_ref[...] = factor * (2.0 * imag - (cross - turned))
        return square / (2.0 - square)

    start = (high - shift) / (high + shift)
    lax.while_loop(lambda spread: spread > settled, step, start)
    sol = sol_ref[...]
    weights = jnp.concatenate([sol[:coils], sol[coils:]], axis=1).astype(BF16)
    for copy in range(out_ref.shape[0]):
        out_ref[copy] = weights


def select_kernel(told_ref, piece_ref, out_ref):
    for frame in range(out_ref.shape[0]):
        for slot in range(out_ref.shape[1]):
            out_ref[frame, slot] = piece_ref[told_ref[frame, slot]]


def fill_kernel(reads_ref, places_ref, weights_ref, source_ref, interp_ref, out_ref, grid_ref):
    frames = weights_ref.shape[0]
    grid_ref[...] = jnp.zeros_like(grid_ref)
    for slot in range(weights_ref.shape[1]):
        chosen = weights_ref[lax.rem(reads_ref[0, slot], frames), slot].astype(F32)
        width = chosen.shape[1] // 2
        real, imag = chosen[:, :width], chosen[:, width:]
        matrix = jnp.concatenate(
            [jnp.concatenate([real, -imag], axis=1), jnp.concatenate([imag, real], axis=1)], axis=0
        ).astype(BF16)
        filled = across_rows(matrix, source_ref[0, slot]).astype(BF16)
        place = places_ref[0, slot]
        grid_ref[place] = grid_ref[place] + across_rows(filled, interp_ref[0, slot])
    out_ref[...] = grid_ref[...].astype(BF16)


def on_device(cal_source, cal_target, app_source, readers, blocks, interp):
    frames = lax.axis_size("frame")
    segs = lax.axis_size("seg")
    coil_count = lax.axis_size("coil")
    held, samples, depth = cal_source.shape
    coils = cal_target.shape[1]
    width = depth // 2
    part = width // coil_count
    gram_rows = part + part // 2
    rows = gram_rows + 3 * coils + 8
    slots = readers.shape[1]
    cells = interp.shape[2]

    partial = pl.pallas_call(
        functools.partial(gram_kernel, part, frames),
        grid=(held,),
        in_specs=[
            pl.BlockSpec(memory_space=pltpu.SMEM),
            pl.BlockSpec((1, samples, depth), lambda g: (g, 0, 0)),
            pl.BlockSpec((1, coils, 2, samples), lambda g: (g, 0, 0, 0)),
        ],
        out_specs=pl.BlockSpec((1, rows, LANES), lambda g: (g, 0, 0)),
        out_shape=jax.ShapeDtypeStruct((held, rows, LANES), F32),
    )(readers, cal_source, cal_target)
    received = lax.all_to_all(partial, "frame", 0, 0, tiled=True)
    spread, rhs, told = pl.pallas_call(
        functools.partial(sum_kernel, gram_rows),
        out_shape=[
            jax.ShapeDtypeStruct((coil_count, gram_rows, LANES), F32),
            jax.ShapeDtypeStruct((3 * coils, LANES), F32),
            jax.ShapeDtypeStruct((frames, LANES), jnp.int32),
        ],
        compiler_params=SMALL,
    )(received)
    gram = lax.all_to_all(spread, "coil", 0, 0, tiled=True)
    weights = pl.pallas_call(
        functools.partial(solve_kernel, part),
        out_shape=jax.ShapeDtypeStruct((segs, coils, depth), BF16),
        scratch_shapes=[
            pltpu.VMEM((width, width), F32),
            pltpu.VMEM((width, width), F32),
            pltpu.VMEM((2 * coils, width), F32),
        ],
        compiler_params=SMALL,
    )(gram, rhs)
    pieces = lax.all_to_all(weights, "seg", 0, 0, tiled=True)
    sent = pl.pallas_call(
        select_kernel,
        in_specs=[
            pl.BlockSpec(memory_space=pltpu.SMEM),
            pl.BlockSpec(memory_space=pltpu.VMEM),
        ],
        out_shape=jax.ShapeDtypeStruct((frames, slots, coils, depth), BF16),
        compiler_params=SMALL,
    )(told, pieces)
    chosen = lax.all_to_all(sent, "frame", 0, 0, tiled=True)
    grid = pl.pallas_call(
        fill_kernel,
        in_specs=[
            pl.BlockSpec(memory_space=pltpu.SMEM),
            pl.BlockSpec(memory_space=pltpu.SMEM),
            pl.BlockSpec(memory_space=pltpu.VMEM),
            pl.BlockSpec(memory_space=pltpu.VMEM),
            pl.BlockSpec(memory_space=pltpu.VMEM),
        ],
        out_shape=jax.ShapeDtypeStruct((segs, 2 * coils, cells), BF16),
        scratch_shapes=[pltpu.VMEM((segs, 2 * coils, cells), F32)],
        compiler_params=SMALL,
    )(readers, blocks, chosen, app_source, interp)
    terms = lax.all_to_all(grid, "seg", 0, 0, tiled=True)
    total = jnp.sum(terms.astype(F32), axis=0)
    power = lax.psum(jnp.sum(total * total, axis=0, keepdims=True), "coil")
    return jnp.sqrt(power + epsilon)


def solution(mesh):
    placed = (
        P("seg", "frame", None),
        P("seg", "coil", None, "frame"),
        P("frame", "seg", None, None),
        P("frame", "seg"),
        P("frame", "seg"),
        P("frame", "seg", None, None),
    )
    return jax.shard_map(
        on_device, mesh=mesh, in_specs=placed, out_specs=P("frame", "seg"), check_vma=False
    )
```

```python
import functools

import jax
import jax.numpy as jnp
from jax import lax
from jax.experimental import pallas as pl
from jax.experimental.pallas import tpu as pltpu
from jax.sharding import PartitionSpec as P

regular = 0.02
epsilon = 1e-06
settled = 1e-3
F32 = jnp.float32
BF16 = jnp.bfloat16
LANES = 128
SMALL = pltpu.CompilerParams(vmem_limit_bytes=16 * 1024 * 1024)


def across_rows(left, right):
    return lax.dot_general(left, right, (((1,), (1,)), ((), ())), preferred_element_type=F32)


def pieces_of(value, count):
    out = []
    for _ in range(count):
        piece = value.astype(BF16)
        value = value - piece.astype(F32)
        out.append(piece)
    return out


def product(left, right):
    a, b = pieces_of(left, 2), pieces_of(right, 2)
    dot = functools.partial(jnp.dot, preferred_element_type=F32)
    return dot(a[0], b[0]) + (dot(a[1], b[0]) + dot(a[0], b[1]))


def fine_product(left, right):
    a, b = pieces_of(left, 3), pieces_of(right, 3)
    dot = functools.partial(jnp.dot, preferred_element_type=F32)
    return dot(a[0], b[0]) + (
        (dot(a[0], b[1]) + dot(a[1], b[0]))
        + (dot(a[1], b[1]) + (dot(a[0], b[2]) + dot(a[2], b[0])))
    )


def gram_kernel(
    part, frames, reads_ref, source_ref, target_ref, send_ref, keep_ref, held_ref, goal_ref, turned_ref, sem
):
    coil = lax.axis_index("coil")
    core = lax.rem(lax.axis_index("frame"), 2)
    count, depth, samples = turned_ref.shape
    width = depth // 2
    half = part // 2
    coils = target_ref.shape[1]
    each = count // 2
    copies = []
    for slot in range(count):
        segment = 2 * (slot % each) + (1 - core if slot < each else core)
        copies.append(
            (
                pltpu.make_async_copy(source_ref.at[segment], held_ref.at[slot], sem.at[0, slot]),
                pltpu.make_async_copy(target_ref.at[segment], goal_ref.at[slot], sem.at[1, slot]),
            )
        )
    for pair in copies:
        for copy in pair:
            copy.start()
    row = lax.broadcasted_iota(jnp.int32, (8, LANES), 0)
    lane = lax.broadcasted_iota(jnp.int32, (8, LANES), 1)
    told = jnp.zeros((8, LANES), jnp.int32)
    for place in range(reads_ref.shape[1]):
        told = jnp.where((row == core) & (lane == place), lax.div(reads_ref[0, place], frames), told)
    told = told.astype(F32)
    across = lax.broadcasted_iota(jnp.int32, (part, width), 1)
    down = lax.broadcasted_iota(jnp.int32, (part, width), 0) + coil * part
    first = pl.multiple_of(coil * part, 16)
    second = pl.multiple_of(width + coil * part, 16)
    for group in range(2):
        slots = range(group * each, (group + 1) * each)
        for slot in slots:
            for copy in copies[slot]:
                copy.wait()
        lefts = []
        for slot in slots:
            turned_ref[slot] = held_ref[slot].T
            lefts.append(
                jnp.concatenate(
                    [
                        turned_ref[slot, pl.ds(first, part)],
                        turned_ref[slot, pl.ds(second, part)],
                        goal_ref[slot, :, 0, :],
                        goal_ref[slot, :, 1, :],
                    ],
                    axis=0,
                )
            )
        products = [
            jnp.dot(left, held_ref[slot], preferred_element_type=F32)
            for left, slot in zip(lefts, slots)
        ]
        for slot, sums in zip(slots, products):
            out = (send_ref if group == 0 else keep_ref).at[slot % each]
            top, bottom = sums[:part], sums[part : 2 * part]
            gram_real = top[:, :width] + bottom[:, width:]
            gram_imag = top[:, width:] - bottom[:, :width]
            packed = jnp.where(across <= down, gram_real, gram_imag)
            proj_real = sums[2 * part : 2 * part + coils]
            proj_imag = sums[2 * part + coils :]
            rhs_real = proj_real[:, :width] + proj_imag[:, width:]
            rhs_imag = proj_imag[:, :width] - proj_real[:, width:]
            out[:part] = packed[:, :LANES]
            out[part : part + half] = jnp.concatenate(
                [packed[:half, LANES:], packed[half:, LANES:]], axis=1
            )
            base = part + half
            out[base : base + coils] = rhs_real[:, :LANES]
            out[base + coils : base + 2 * coils] = rhs_imag[:, :LANES]
            out[base + 2 * coils : base + 3 * coils] = jnp.concatenate(
                [rhs_real[:, LANES:], rhs_imag[:, LANES:]], axis=1
            )
            out[base + 3 * coils :] = told


def sum_kernel(gram_rows, partial_ref, spread_ref, rhs_ref, told_ref):
    rows = gram_rows + rhs_ref.shape[0]
    total = partial_ref[0, :rows]
    for chip in range(1, partial_ref.shape[0]):
        total = total + partial_ref[chip, :rows]
    for copy in range(spread_ref.shape[0]):
        spread_ref[copy] = total[:gram_rows]
    rhs_ref[...] = total[gram_rows:]
    for chip in range(partial_ref.shape[0]):
        told_ref[2 * chip : 2 * chip + 2] = partial_ref[chip, rows : rows + 2].astype(jnp.int32)


def solve_kernel(part, gram_ref, rhs_ref, out_ref, real_ref, imag_ref, sol_ref):
    width = 4 * part
    half = part // 2
    coils = rhs_ref.shape[0] // 3
    pieces = []
    for coil in range(4):
        block = gram_ref[coil]
        tail = block[part:]
        pieces.append(
            jnp.concatenate(
                [block[:part], jnp.concatenate([tail[:, :64], tail[:, 64:]], axis=0)], axis=1
            )
        )
    packed = jnp.concatenate(pieces, axis=0)
    flipped = packed.T
    down = lax.broadcasted_iota(jnp.int32, (width, width), 0)
    across = lax.broadcasted_iota(jnp.int32, (width, width), 1)
    real = jnp.where(across <= down, packed, flipped)
    imag = jnp.where(across > down, packed, jnp.where(across < down, -flipped, 0.0))
    diagonal = jnp.where(across == down, packed, 0.0)
    shift = regular / width * jnp.sum(diagonal)
    high = jnp.sqrt(jnp.sum(real * real + imag * imag)) + shift
    scale = 2.0 / (high + shift)
    real_ref[...] = (real + jnp.where(across == down, shift, 0.0)) * scale
    imag_ref[...] = imag * scale
    rhs_real = jnp.concatenate([rhs_ref[:coils], rhs_ref[2 * coils :, :64]], axis=1)
    rhs_imag = jnp.concatenate([rhs_ref[coils : 2 * coils], rhs_ref[2 * coils :, 64:]], axis=1)
    sol_ref[...] = jnp.concatenate([rhs_real, rhs_imag], axis=0) * scale

    def step(product, spread):
        square = spread * spread
        factor = 2.0 / (2.0 - square)
        real, imag, sol = real_ref[...], imag_ref[...], sol_ref[...]
        first = product(jnp.concatenate([real, sol], axis=0), imag)
        second = product(jnp.concatenate([real - imag, sol], axis=0), real + imag)
        cross, thin = first[:width], first[width:]
        turned = cross.T
        by_real = second[width:] - thin
        change = jnp.concatenate(
            [by_real[:coils] + thin[coils:], by_real[coils:] - thin[:coils]], axis=0
        )
        sol_ref[...] = factor * (2.0 * sol - change)
        real_ref[...] = factor * (2.0 * real - (second[:width] - cross - turned))
        imag_ref[...] = factor * (2.0 * imag - (cross - turned))
        return square / (2.0 - square)

    spread = (high - shift) / (high + shift)
    spread = lax.while_loop(
        lambda spread: spread > 0.9, functools.partial(step, fine_product), spread
    )
    spread = lax.while_loop(
        lambda spread: spread > settled, functools.partial(step, product), spread
    )
    square = spread * spread
    sol = sol_ref[...]
    by_real = product(sol, real_ref[...])
    by_imag = product(sol, imag_ref[...])
    change = jnp.concatenate(
        [by_real[:coils] + by_imag[coils:], by_real[coils:] - by_imag[:coils]], axis=0
    )
    sol = 2.0 / (2.0 - square) * (2.0 * sol - change)
    weights = jnp.concatenate([sol[:coils], sol[coils:]], axis=1).astype(BF16)
    for copy in range(out_ref.shape[0]):
        out_ref[copy] = weights


def select_kernel(told_ref, piece_ref, out_ref):
    for frame in range(out_ref.shape[0]):
        for slot in range(out_ref.shape[1]):
            out_ref[frame, slot] = piece_ref[told_ref[frame, slot]]


def fill_kernel(reads_ref, places_ref, weights_ref, source_ref, interp_ref, out_ref, grid_ref):
    frames = weights_ref.shape[0]
    grid_ref[...] = jnp.zeros_like(grid_ref)
    for slot in range(weights_ref.shape[1]):
        chosen = weights_ref[lax.rem(reads_ref[0, slot], frames), slot].astype(F32)
        width = chosen.shape[1] // 2
        real, imag = chosen[:, :width], chosen[:, width:]
        matrix = jnp.concatenate(
            [jnp.concatenate([real, -imag], axis=1), jnp.concatenate([imag, real], axis=1)], axis=0
        ).astype(BF16)
        filled = across_rows(matrix, source_ref[0, slot]).astype(BF16)
        place = places_ref[0, slot]
        grid_ref[place] = grid_ref[place] + across_rows(filled, interp_ref[0, slot])
    out_ref[...] = grid_ref[...].astype(BF16)


def on_device(cal_source, cal_target, app_source, readers, blocks, interp):
    frames = lax.axis_size("frame")
    segs = lax.axis_size("seg")
    coil_count = lax.axis_size("coil")
    held, samples, depth = cal_source.shape
    coils = cal_target.shape[1]
    width = depth // 2
    part = width // coil_count
    gram_rows = part + part // 2
    rows = gram_rows + 3 * coils + 8
    slots = readers.shape[1]
    cells = interp.shape[2]

    each = held // 2
    block = jax.ShapeDtypeStruct((each, rows, LANES), F32)
    send, keep = pl.pallas_call(
        functools.partial(gram_kernel, part, frames),
        in_specs=[
            pl.BlockSpec(memory_space=pltpu.SMEM),
            pl.BlockSpec(memory_space=pl.ANY),
            pl.BlockSpec(memory_space=pl.ANY),
        ],
        out_shape=[block, block],
        scratch_shapes=[
            pltpu.VMEM((held, samples, depth), BF16),
            pltpu.VMEM((held, coils, 2, samples), BF16),
            pltpu.VMEM((held, depth, samples), BF16),
            pltpu.SemaphoreType.DMA((2, held)),
        ],
        compiler_params=pltpu.CompilerParams(vmem_limit_bytes=32 * 1024 * 1024),
    )(readers, cal_source, cal_target)
    other = lax.ppermute(send, "frame", [(frame, frame ^ 1) for frame in range(frames)])
    chips = [[2 * chip + core for chip in range(frames // 2)] for core in range(2)]
    received = lax.all_to_all(
        keep + other, "frame", 0, 0, tiled=True, axis_index_groups=chips
    )
    spread, rhs, told = pl.pallas_call(
        functools.partial(sum_kernel, gram_rows),
        out_shape=[
            jax.ShapeDtypeStruct((coil_count, gram_rows, LANES), F32),
            jax.ShapeDtypeStruct((3 * coils, LANES), F32),
            jax.ShapeDtypeStruct((frames, LANES), jnp.int32),
        ],
        compiler_params=SMALL,
    )(received)
    gram = lax.all_to_all(spread, "coil", 0, 0, tiled=True)
    weights = pl.pallas_call(
        functools.partial(solve_kernel, part),
        out_shape=jax.ShapeDtypeStruct((segs, coils, depth), BF16),
        scratch_shapes=[
            pltpu.VMEM((width, width), F32),
            pltpu.VMEM((width, width), F32),
            pltpu.VMEM((2 * coils, width), F32),
        ],
        compiler_params=SMALL,
    )(gram, rhs)
    pieces = lax.all_to_all(weights, "seg", 0, 0, tiled=True)
    sent = pl.pallas_call(
        select_kernel,
        in_specs=[
            pl.BlockSpec(memory_space=pltpu.SMEM),
            pl.BlockSpec(memory_space=pltpu.VMEM),
        ],
        out_shape=jax.ShapeDtypeStruct((frames, slots, coils, depth), BF16),
        compiler_params=SMALL,
    )(told, pieces)
    chosen = lax.all_to_all(sent, "frame", 0, 0, tiled=True)
    grid = pl.pallas_call(
        fill_kernel,
        in_specs=[
            pl.BlockSpec(memory_space=pltpu.SMEM),
            pl.BlockSpec(memory_space=pltpu.SMEM),
            pl.BlockSpec(memory_space=pltpu.VMEM),
            pl.BlockSpec(memory_space=pltpu.VMEM),
            pl.BlockSpec(memory_space=pltpu.VMEM),
        ],
        out_shape=jax.ShapeDtypeStruct((segs, 2 * coils, cells), BF16),
        scratch_shapes=[pltpu.VMEM((segs, 2 * coils, cells), F32)],
        compiler_params=SMALL,
    )(readers, blocks, chosen, app_source, interp)
    terms = lax.all_to_all(grid, "seg", 0, 0, tiled=True)
    total = jnp.sum(terms.astype(F32), axis=0)
    power = lax.psum(jnp.sum(total * total, axis=0, keepdims=True), "coil")
    return jnp.sqrt(power + epsilon)


def solution(mesh):
    placed = (
        P("seg", "frame", None),
        P("seg", "coil", None, "frame"),
        P("frame", "seg", None, None),
        P("frame", "seg"),
        P("frame", "seg"),
        P("frame", "seg", None, None),
    )
    return jax.shard_map(
        on_device, mesh=mesh, in_specs=placed, out_specs=P("frame", "seg"), check_vma=False
    )
```

```python
import functools

import jax
import jax.numpy as jnp
from jax import lax
from jax.experimental import pallas as pl
from jax.experimental.pallas import tpu as pltpu
from jax.sharding import PartitionSpec as P

regular = 0.02
epsilon = 1e-06
settled = 1e-3
F32 = jnp.float32
BF16 = jnp.bfloat16
LANES = 128
GROUPS = ((0, 1), (2, 3))
GRANT = 60 * 1024 * 1024
SMALL = pltpu.CompilerParams(vmem_limit_bytes=16 * 1024 * 1024)


def across_rows(left, right):
    return lax.dot_general(left, right, (((1,), (1,)), ((), ())), preferred_element_type=F32)


def pieces_of(value, count):
    out = []
    for _ in range(count):
        piece = value.astype(BF16)
        value = value - piece.astype(F32)
        out.append(piece)
    return out


def product(left, right):
    a, b = pieces_of(left, 2), pieces_of(right, 2)
    dot = functools.partial(jnp.dot, preferred_element_type=F32)
    return dot(a[0], b[0]) + (dot(a[1], b[0]) + dot(a[0], b[1]))


def fine_product(left, right):
    a, b = pieces_of(left, 3), pieces_of(right, 3)
    dot = functools.partial(jnp.dot, preferred_element_type=F32)
    return dot(a[0], b[0]) + (
        (dot(a[0], b[1]) + dot(a[1], b[0]))
        + (dot(a[1], b[1]) + (dot(a[0], b[2]) + dot(a[2], b[0])))
    )


def gram_kernel(
    part, frames, kept, reads_ref, source_ref, target_ref, out_ref, held_ref, goal_ref, turned_ref, sem
):
    coil = lax.axis_index("coil")
    core = lax.rem(lax.axis_index("frame"), 2)
    count, depth, samples = turned_ref.shape
    width = depth // 2
    half = part // 2
    coils = target_ref.shape[1]
    copies = []
    for slot in range(count):
        segment = 2 * slot + (core if kept else 1 - core)
        copies.append(
            (
                pltpu.make_async_copy(source_ref.at[segment], held_ref.at[slot], sem.at[0, slot]),
                pltpu.make_async_copy(target_ref.at[segment], goal_ref.at[slot], sem.at[1, slot]),
            )
        )
    for pair in copies:
        for copy in pair:
            copy.start()
    row = lax.broadcasted_iota(jnp.int32, (8, LANES), 0)
    lane = lax.broadcasted_iota(jnp.int32, (8, LANES), 1)
    told = jnp.zeros((8, LANES), jnp.int32)
    for place in range(reads_ref.shape[1]):
        told = jnp.where((row == core) & (lane == place), lax.div(reads_ref[0, place], frames), told)
    told = told.astype(F32)
    across = lax.broadcasted_iota(jnp.int32, (part, width), 1)
    down = lax.broadcasted_iota(jnp.int32, (part, width), 0) + coil * part
    first = pl.multiple_of(coil * part, 16)
    second = pl.multiple_of(width + coil * part, 16)
    for group in GROUPS:
        slots = [slot for slot in group if slot < count]
        for slot in slots:
            for copy in copies[slot]:
                copy.wait()
        lefts = []
        for slot in slots:
            turned_ref[slot] = held_ref[slot].T
            lefts.append(
                jnp.concatenate(
                    [
                        turned_ref[slot, pl.ds(first, part)],
                        turned_ref[slot, pl.ds(second, part)],
                        goal_ref[slot, :, 0, :],
                        goal_ref[slot, :, 1, :],
                    ],
                    axis=0,
                )
            )
        products = [
            jnp.dot(left, held_ref[slot], preferred_element_type=F32)
            for left, slot in zip(lefts, slots)
        ]
        for slot, sums in zip(slots, products):
            out = out_ref.at[slot]
            top, bottom = sums[:part], sums[part : 2 * part]
            gram_real = top[:, :width] + bottom[:, width:]
            gram_imag = top[:, width:] - bottom[:, :width]
            packed = jnp.where(across <= down, gram_real, gram_imag)
            proj_real = sums[2 * part : 2 * part + coils]
            proj_imag = sums[2 * part + coils :]
            rhs_real = proj_real[:, :width] + proj_imag[:, width:]
            rhs_imag = proj_imag[:, :width] - proj_real[:, width:]
            out[:part] = packed[:, :LANES]
            out[part : part + half] = jnp.concatenate(
                [packed[:half, LANES:], packed[half:, LANES:]], axis=1
            )
            base = part + half
            out[base : base + coils] = rhs_real[:, :LANES]
            out[base + coils : base + 2 * coils] = rhs_imag[:, :LANES]
            out[base + 2 * coils : base + 3 * coils] = jnp.concatenate(
                [rhs_real[:, LANES:], rhs_imag[:, LANES:]], axis=1
            )
            out[base + 3 * coils :] = told


def sum_kernel(gram_rows, partial_ref, spread_ref, rhs_ref, told_ref):
    rows = gram_rows + rhs_ref.shape[0]
    total = partial_ref[0, :rows]
    for chip in range(1, partial_ref.shape[0]):
        total = total + partial_ref[chip, :rows]
    for copy in range(spread_ref.shape[0]):
        spread_ref[copy] = total[:gram_rows]
    rhs_ref[...] = total[gram_rows:]
    for chip in range(partial_ref.shape[0]):
        told_ref[2 * chip : 2 * chip + 2] = partial_ref[chip, rows : rows + 2].astype(jnp.int32)


def solve_kernel(part, gram_ref, rhs_ref, out_ref, real_ref, imag_ref, sol_ref):
    width = 4 * part
    half = part // 2
    coils = rhs_ref.shape[0] // 3
    pieces = []
    for coil in range(4):
        block = gram_ref[coil]
        tail = block[part:]
        pieces.append(
            jnp.concatenate(
                [block[:part], jnp.concatenate([tail[:, :64], tail[:, 64:]], axis=0)], axis=1
            )
        )
    packed = jnp.concatenate(pieces, axis=0)
    flipped = packed.T
    down = lax.broadcasted_iota(jnp.int32, (width, width), 0)
    across = lax.broadcasted_iota(jnp.int32, (width, width), 1)
    real = jnp.where(across <= down, packed, flipped)
    imag = jnp.where(across > down, packed, jnp.where(across < down, -flipped, 0.0))
    diagonal = jnp.where(across == down, packed, 0.0)
    shift = regular / width * jnp.sum(diagonal)
    high = jnp.sqrt(jnp.sum(real * real + imag * imag)) + shift
    scale = 2.0 / (high + shift)
    real_ref[...] = (real + jnp.where(across == down, shift, 0.0)) * scale
    imag_ref[...] = imag * scale
    rhs_real = jnp.concatenate([rhs_ref[:coils], rhs_ref[2 * coils :, :64]], axis=1)
    rhs_imag = jnp.concatenate([rhs_ref[coils : 2 * coils], rhs_ref[2 * coils :, 64:]], axis=1)
    sol_ref[...] = jnp.concatenate([rhs_real, rhs_imag], axis=0) * scale

    def step(product, spread):
        square = spread * spread
        factor = 2.0 / (2.0 - square)
        real, imag, sol = real_ref[...], imag_ref[...], sol_ref[...]
        first = product(jnp.concatenate([real, sol], axis=0), imag)
        second = product(jnp.concatenate([real - imag, sol], axis=0), real + imag)
        cross, thin = first[:width], first[width:]
        turned = cross.T
        by_real = second[width:] - thin
        change = jnp.concatenate(
            [by_real[:coils] + thin[coils:], by_real[coils:] - thin[:coils]], axis=0
        )
        sol_ref[...] = factor * (2.0 * sol - change)
        real_ref[...] = factor * (2.0 * real - (second[:width] - cross - turned))
        imag_ref[...] = factor * (2.0 * imag - (cross - turned))
        return square / (2.0 - square)

    spread = (high - shift) / (high + shift)
    spread = lax.while_loop(
        lambda spread: spread > 0.9, functools.partial(step, fine_product), spread
    )
    spread = lax.while_loop(
        lambda spread: spread > settled, functools.partial(step, product), spread
    )
    square = spread * spread
    sol = sol_ref[...]
    by_real = product(sol, real_ref[...])
    by_imag = product(sol, imag_ref[...])
    change = jnp.concatenate(
        [by_real[:coils] + by_imag[coils:], by_real[coils:] - by_imag[:coils]], axis=0
    )
    sol = 2.0 / (2.0 - square) * (2.0 * sol - change)
    weights = jnp.concatenate([sol[:coils], sol[coils:]], axis=1).astype(BF16)
    for copy in range(out_ref.shape[0]):
        out_ref[copy] = weights


def select_kernel(told_ref, piece_ref, out_ref):
    for frame in range(out_ref.shape[0]):
        for slot in range(out_ref.shape[1]):
            out_ref[frame, slot] = piece_ref[told_ref[frame, slot]]


def fill_kernel(reads_ref, places_ref, weights_ref, source_ref, interp_ref, out_ref, grid_ref):
    frames = weights_ref.shape[0]
    grid_ref[...] = jnp.zeros_like(grid_ref)
    for slot in range(weights_ref.shape[1]):
        chosen = weights_ref[lax.rem(reads_ref[0, slot], frames), slot].astype(F32)
        width = chosen.shape[1] // 2
        real, imag = chosen[:, :width], chosen[:, width:]
        matrix = jnp.concatenate(
            [jnp.concatenate([real, -imag], axis=1), jnp.concatenate([imag, real], axis=1)], axis=0
        ).astype(BF16)
        filled = across_rows(matrix, source_ref[0, slot]).astype(BF16)
        place = places_ref[0, slot]
        grid_ref[place] = grid_ref[place] + across_rows(filled, interp_ref[0, slot])
    out_ref[...] = grid_ref[...].astype(BF16)


def on_device(cal_source, cal_target, app_source, readers, blocks, interp):
    frames = lax.axis_size("frame")
    segs = lax.axis_size("seg")
    coil_count = lax.axis_size("coil")
    held, samples, depth = cal_source.shape
    coils = cal_target.shape[1]
    width = depth // 2
    part = width // coil_count
    gram_rows = part + part // 2
    rows = gram_rows + 3 * coils + 8
    slots = readers.shape[1]
    cells = interp.shape[2]

    each = held // 2
    partials = [
        pl.pallas_call(
            functools.partial(gram_kernel, part, frames, kept),
            in_specs=[
                pl.BlockSpec(memory_space=pltpu.SMEM),
                pl.BlockSpec(memory_space=pl.ANY),
                pl.BlockSpec(memory_space=pl.ANY),
            ],
            out_shape=jax.ShapeDtypeStruct((each, rows, LANES), F32),
            scratch_shapes=[
                pltpu.VMEM((each, samples, depth), BF16),
                pltpu.VMEM((each, coils, 2, samples), BF16),
                pltpu.VMEM((each, depth, samples), BF16),
                pltpu.SemaphoreType.DMA((2, each)),
            ],
            compiler_params=pltpu.CompilerParams(vmem_limit_bytes=GRANT),
            cost_estimate=pl.CostEstimate(
                flops=2 * each * samples * depth * (2 * part + 2 * coils),
                bytes_accessed=2 * each * samples * (depth + 2 * coils),
                transcendentals=0,
            ),
        )(readers, cal_source, cal_target)
        for kept in (False, True)
    ]
    send, keep = partials
    other = lax.ppermute(send, "frame", [(frame, frame ^ 1) for frame in range(frames)])
    chips = [[2 * chip + core for chip in range(frames // 2)] for core in range(2)]
    received = lax.all_to_all(
        keep + other, "frame", 0, 0, tiled=True, axis_index_groups=chips
    )
    spread, rhs, told = pl.pallas_call(
        functools.partial(sum_kernel, gram_rows),
        out_shape=[
            jax.ShapeDtypeStruct((coil_count, gram_rows, LANES), F32),
            jax.ShapeDtypeStruct((3 * coils, LANES), F32),
            jax.ShapeDtypeStruct((frames, LANES), jnp.int32),
        ],
        compiler_params=SMALL,
    )(received)
    gram = lax.all_to_all(spread, "coil", 0, 0, tiled=True)
    weights = pl.pallas_call(
        functools.partial(solve_kernel, part),
        out_shape=jax.ShapeDtypeStruct((segs, coils, depth), BF16),
        scratch_shapes=[
            pltpu.VMEM((width, width), F32),
            pltpu.VMEM((width, width), F32),
            pltpu.VMEM((2 * coils, width), F32),
        ],
        compiler_params=SMALL,
    )(gram, rhs)
    pieces = lax.all_to_all(weights, "seg", 0, 0, tiled=True)
    sent = pl.pallas_call(
        select_kernel,
        in_specs=[
            pl.BlockSpec(memory_space=pltpu.SMEM),
            pl.BlockSpec(memory_space=pltpu.VMEM),
        ],
        out_shape=jax.ShapeDtypeStruct((frames, slots, coils, depth), BF16),
        compiler_params=SMALL,
    )(told, pieces)
    chosen = lax.all_to_all(sent, "frame", 0, 0, tiled=True)
    grid = pl.pallas_call(
        fill_kernel,
        in_specs=[
            pl.BlockSpec(memory_space=pltpu.SMEM),
            pl.BlockSpec(memory_space=pltpu.SMEM),
            pl.BlockSpec(memory_space=pltpu.VMEM),
            pl.BlockSpec(memory_space=pltpu.VMEM),
            pl.BlockSpec(memory_space=pltpu.VMEM),
        ],
        out_shape=jax.ShapeDtypeStruct((segs, 2 * coils, cells), BF16),
        scratch_shapes=[pltpu.VMEM((segs, 2 * coils, cells), F32)],
        compiler_params=SMALL,
    )(readers, blocks, chosen, app_source, interp)
    terms = lax.all_to_all(grid, "seg", 0, 0, tiled=True)
    total = jnp.sum(terms.astype(F32), axis=0)
    power = lax.psum(jnp.sum(total * total, axis=0, keepdims=True), "coil")
    return jnp.sqrt(power + epsilon)


def solution(mesh):
    placed = (
        P("seg", "frame", None),
        P("seg", "coil", None, "frame"),
        P("frame", "seg", None, None),
        P("frame", "seg"),
        P("frame", "seg"),
        P("frame", "seg", None, None),
    )
    return jax.shard_map(
        on_device, mesh=mesh, in_specs=placed, out_specs=P("frame", "seg"), check_vma=False
    )
```

```python
import functools

import jax
import jax.numpy as jnp
from jax import lax
from jax.experimental import pallas as pl
from jax.experimental.pallas import tpu as pltpu
from jax.sharding import PartitionSpec as P

regular = 0.02
epsilon = 1e-06
settled = 1e-3
F32 = jnp.float32
BF16 = jnp.bfloat16
LANES = 128
SMALL = pltpu.CompilerParams(vmem_limit_bytes=16 * 1024 * 1024)


def across_rows(left, right):
    return lax.dot_general(left, right, (((1,), (1,)), ((), ())), preferred_element_type=F32)


def pieces_of(value, count):
    out = []
    for _ in range(count):
        piece = value.astype(BF16)
        value = value - piece.astype(F32)
        out.append(piece)
    return out


def product(left, right):
    a, b = pieces_of(left, 2), pieces_of(right, 2)
    dot = functools.partial(jnp.dot, preferred_element_type=F32)
    return dot(a[0], b[0]) + (dot(a[1], b[0]) + dot(a[0], b[1]))


def fine_product(left, right):
    a, b = pieces_of(left, 3), pieces_of(right, 3)
    dot = functools.partial(jnp.dot, preferred_element_type=F32)
    return dot(a[0], b[0]) + (
        (dot(a[0], b[1]) + dot(a[1], b[0]))
        + (dot(a[1], b[1]) + (dot(a[0], b[2]) + dot(a[2], b[0])))
    )


def gram_kernel(
    part, frames, reads_ref, source_ref, target_ref, send_ref, keep_ref, held_ref, goal_ref, turned_ref, sem
):
    coil = lax.axis_index("coil")
    core = lax.rem(lax.axis_index("frame"), 2)
    count, depth, samples = turned_ref.shape
    width = depth // 2
    half = part // 2
    coils = target_ref.shape[1]
    each = count // 2
    copies = []
    for slot in range(count):
        segment = 2 * (slot % each) + (1 - core if slot < each else core)
        copies.append(
            (
                pltpu.make_async_copy(source_ref.at[segment], held_ref.at[slot], sem.at[0, slot]),
                pltpu.make_async_copy(target_ref.at[segment], goal_ref.at[slot], sem.at[1, slot]),
            )
        )
    for pair in copies:
        for copy in pair:
            copy.start()
    row = lax.broadcasted_iota(jnp.int32, (8, LANES), 0)
    lane = lax.broadcasted_iota(jnp.int32, (8, LANES), 1)
    told = jnp.zeros((8, LANES), jnp.int32)
    for place in range(reads_ref.shape[1]):
        told = jnp.where((row == core) & (lane == place), lax.div(reads_ref[0, place], frames), told)
    told = told.astype(F32)
    across = lax.broadcasted_iota(jnp.int32, (part, width), 1)
    down = lax.broadcasted_iota(jnp.int32, (part, width), 0) + coil * part
    first = pl.multiple_of(coil * part, 16)
    second = pl.multiple_of(width + coil * part, 16)
    for group in range(2):
        slots = range(group * each, (group + 1) * each)
        for slot in slots:
            for copy in copies[slot]:
                copy.wait()
        lefts = []
        for slot in slots:
            turned_ref[slot] = held_ref[slot].T
            lefts.append(
                jnp.concatenate(
                    [
                        turned_ref[slot, pl.ds(first, part)],
                        turned_ref[slot, pl.ds(second, part)],
                        goal_ref[slot, :, 0, :],
                        goal_ref[slot, :, 1, :],
                    ],
                    axis=0,
                )
            )
        products = [
            jnp.dot(left, held_ref[slot], preferred_element_type=F32)
            for left, slot in zip(lefts, slots)
        ]
        for slot, sums in zip(slots, products):
            out = (send_ref if group == 0 else keep_ref).at[slot % each]
            top, bottom = sums[:part], sums[part : 2 * part]
            gram_real = top[:, :width] + bottom[:, width:]
            gram_imag = top[:, width:] - bottom[:, :width]
            packed = jnp.where(across <= down, gram_real, gram_imag)
            proj_real = sums[2 * part : 2 * part + coils]
            proj_imag = sums[2 * part + coils :]
            rhs_real = proj_real[:, :width] + proj_imag[:, width:]
            rhs_imag = proj_imag[:, :width] - proj_real[:, width:]
            out[:part] = packed[:, :LANES]
            out[part : part + half] = jnp.concatenate(
                [packed[:half, LANES:], packed[half:, LANES:]], axis=1
            )
            base = part + half
            out[base : base + coils] = rhs_real[:, :LANES]
            out[base + coils : base + 2 * coils] = rhs_imag[:, :LANES]
            out[base + 2 * coils : base + 3 * coils] = jnp.concatenate(
                [rhs_real[:, LANES:], rhs_imag[:, LANES:]], axis=1
            )
            out[base + 3 * coils :] = told


def sum_kernel(gram_rows, partial_ref, spread_ref, rhs_ref, told_ref):
    rows = gram_rows + rhs_ref.shape[0]
    total = partial_ref[0, :rows]
    for chip in range(1, partial_ref.shape[0]):
        total = total + partial_ref[chip, :rows]
    for copy in range(spread_ref.shape[0]):
        spread_ref[copy] = total[:gram_rows]
    rhs_ref[...] = total[gram_rows:]
    for chip in range(partial_ref.shape[0]):
        told_ref[2 * chip : 2 * chip + 2] = partial_ref[chip, rows : rows + 2].astype(jnp.int32)


def solve_kernel(part, gram_ref, rhs_ref, out_ref, real_ref, imag_ref, sol_ref):
    width = 4 * part
    half = part // 2
    coils = rhs_ref.shape[0] // 3
    pieces = []
    for coil in range(4):
        block = gram_ref[coil]
        tail = block[part:]
        pieces.append(
            jnp.concatenate(
                [block[:part], jnp.concatenate([tail[:, :64], tail[:, 64:]], axis=0)], axis=1
            )
        )
    packed = jnp.concatenate(pieces, axis=0)
    flipped = packed.T
    down = lax.broadcasted_iota(jnp.int32, (width, width), 0)
    across = lax.broadcasted_iota(jnp.int32, (width, width), 1)
    real = jnp.where(across <= down, packed, flipped)
    imag = jnp.where(across > down, packed, jnp.where(across < down, -flipped, 0.0))
    diagonal = jnp.where(across == down, packed, 0.0)
    shift = regular / width * jnp.sum(diagonal)
    high = jnp.sqrt(jnp.sum(real * real + imag * imag)) + shift
    scale = 2.0 / (high + shift)
    real_ref[...] = (real + jnp.where(across == down, shift, 0.0)) * scale
    imag_ref[...] = imag * scale
    rhs_real = jnp.concatenate([rhs_ref[:coils], rhs_ref[2 * coils :, :64]], axis=1)
    rhs_imag = jnp.concatenate([rhs_ref[coils : 2 * coils], rhs_ref[2 * coils :, 64:]], axis=1)
    sol_ref[...] = jnp.concatenate([rhs_real, rhs_imag], axis=0) * scale

    def step(product, spread):
        square = spread * spread
        factor = 2.0 / (2.0 - square)
        real, imag, sol = real_ref[...], imag_ref[...], sol_ref[...]
        first = product(jnp.concatenate([real, sol], axis=0), imag)
        second = product(jnp.concatenate([real - imag, sol], axis=0), real + imag)
        cross, thin = first[:width], first[width:]
        turned = cross.T
        by_real = second[width:] - thin
        change = jnp.concatenate(
            [by_real[:coils] + thin[coils:], by_real[coils:] - thin[:coils]], axis=0
        )
        sol_ref[...] = factor * (2.0 * sol - change)
        real_ref[...] = factor * (2.0 * real - (second[:width] - cross - turned))
        imag_ref[...] = factor * (2.0 * imag - (cross - turned))
        return square / (2.0 - square)

    spread = (high - shift) / (high + shift)
    spread = lax.while_loop(
        lambda spread: spread > 0.9, functools.partial(step, fine_product), spread
    )
    spread = lax.while_loop(
        lambda spread: spread > settled, functools.partial(step, product), spread
    )
    square = spread * spread
    sol = sol_ref[...]
    by_real = product(sol, real_ref[...])
    by_imag = product(sol, imag_ref[...])
    change = jnp.concatenate(
        [by_real[:coils] + by_imag[coils:], by_real[coils:] - by_imag[:coils]], axis=0
    )
    sol = 2.0 / (2.0 - square) * (2.0 * sol - change)
    weights = jnp.concatenate([sol[:coils], sol[coils:]], axis=1).astype(BF16)
    for copy in range(out_ref.shape[0]):
        out_ref[copy] = weights


def select_kernel(told_ref, piece_ref, out_ref):
    for frame in range(out_ref.shape[0]):
        for slot in range(out_ref.shape[1]):
            out_ref[frame, slot] = piece_ref[told_ref[frame, slot]]


def fill_kernel(reads_ref, places_ref, weights_ref, source_ref, interp_ref, out_ref, grid_ref):
    frames = weights_ref.shape[0]
    grid_ref[...] = jnp.zeros_like(grid_ref)
    for slot in range(weights_ref.shape[1]):
        chosen = weights_ref[lax.rem(reads_ref[0, slot], frames), slot].astype(F32)
        width = chosen.shape[1] // 2
        real, imag = chosen[:, :width], chosen[:, width:]
        matrix = jnp.concatenate(
            [jnp.concatenate([real, -imag], axis=1), jnp.concatenate([imag, real], axis=1)], axis=0
        ).astype(BF16)
        filled = across_rows(matrix, source_ref[0, slot]).astype(BF16)
        place = places_ref[0, slot]
        grid_ref[place] = grid_ref[place] + across_rows(filled, interp_ref[0, slot])
    out_ref[...] = grid_ref[...].astype(BF16)


def on_device(cal_source, cal_target, app_source, readers, blocks, interp):
    frames = lax.axis_size("frame")
    segs = lax.axis_size("seg")
    coil_count = lax.axis_size("coil")
    held, samples, depth = cal_source.shape
    coils = cal_target.shape[1]
    width = depth // 2
    part = width // coil_count
    gram_rows = part + part // 2
    rows = gram_rows + 3 * coils + 8
    slots = readers.shape[1]
    cells = interp.shape[2]

    each = held // 2
    block = jax.ShapeDtypeStruct((each, rows, LANES), F32)
    send, keep = pl.pallas_call(
        functools.partial(gram_kernel, part, frames),
        in_specs=[
            pl.BlockSpec(memory_space=pltpu.SMEM),
            pl.BlockSpec(memory_space=pltpu.HBM),
            pl.BlockSpec(memory_space=pltpu.HBM),
        ],
        out_shape=[block, block],
        scratch_shapes=[
            pltpu.VMEM((held, samples, depth), BF16),
            pltpu.VMEM((held, coils, 2, samples), BF16),
            pltpu.VMEM((held, depth, samples), BF16),
            pltpu.SemaphoreType.DMA((2, held)),
        ],
        compiler_params=SMALL,
    )(
        pltpu.with_memory_space_constraint(readers, pltpu.HBM),
        pltpu.with_memory_space_constraint(cal_source, pltpu.HBM),
        pltpu.with_memory_space_constraint(cal_target, pltpu.HBM),
    )
    other = lax.ppermute(send, "frame", [(frame, frame ^ 1) for frame in range(frames)])
    chips = [[2 * chip + core for chip in range(frames // 2)] for core in range(2)]
    received = lax.all_to_all(
        keep + other, "frame", 0, 0, tiled=True, axis_index_groups=chips
    )
    spread, rhs, told = pl.pallas_call(
        functools.partial(sum_kernel, gram_rows),
        out_shape=[
            jax.ShapeDtypeStruct((coil_count, gram_rows, LANES), F32),
            jax.ShapeDtypeStruct((3 * coils, LANES), F32),
            jax.ShapeDtypeStruct((frames, LANES), jnp.int32),
        ],
        compiler_params=SMALL,
    )(received)
    gram = lax.all_to_all(spread, "coil", 0, 0, tiled=True)
    weights = pl.pallas_call(
        functools.partial(solve_kernel, part),
        out_shape=jax.ShapeDtypeStruct((segs, coils, depth), BF16),
        scratch_shapes=[
            pltpu.VMEM((width, width), F32),
            pltpu.VMEM((width, width), F32),
            pltpu.VMEM((2 * coils, width), F32),
        ],
        compiler_params=SMALL,
    )(gram, rhs)
    pieces = lax.all_to_all(weights, "seg", 0, 0, tiled=True)
    sent = pl.pallas_call(
        select_kernel,
        in_specs=[
            pl.BlockSpec(memory_space=pltpu.SMEM),
            pl.BlockSpec(memory_space=pltpu.VMEM),
        ],
        out_shape=jax.ShapeDtypeStruct((frames, slots, coils, depth), BF16),
        compiler_params=SMALL,
    )(told, pieces)
    chosen = lax.all_to_all(sent, "frame", 0, 0, tiled=True)
    grid = pl.pallas_call(
        fill_kernel,
        in_specs=[
            pl.BlockSpec(memory_space=pltpu.SMEM),
            pl.BlockSpec(memory_space=pltpu.SMEM),
            pl.BlockSpec(memory_space=pltpu.VMEM),
            pl.BlockSpec(memory_space=pltpu.VMEM),
            pl.BlockSpec(memory_space=pltpu.VMEM),
        ],
        out_shape=jax.ShapeDtypeStruct((segs, 2 * coils, cells), BF16),
        scratch_shapes=[pltpu.VMEM((segs, 2 * coils, cells), F32)],
        compiler_params=SMALL,
    )(readers, blocks, chosen, app_source, interp)
    terms = lax.all_to_all(grid, "seg", 0, 0, tiled=True)
    total = jnp.sum(terms.astype(F32), axis=0)
    power = lax.psum(jnp.sum(total * total, axis=0, keepdims=True), "coil")
    return jnp.sqrt(power + epsilon)


def solution(mesh):
    placed = (
        P("seg", "frame", None),
        P("seg", "coil", None, "frame"),
        P("frame", "seg", None, None),
        P("frame", "seg"),
        P("frame", "seg"),
        P("frame", "seg", None, None),
    )
    return jax.shard_map(
        on_device, mesh=mesh, in_specs=placed, out_specs=P("frame", "seg"), check_vma=False
    )
```

```python
import functools

import jax
import jax.numpy as jnp
from jax import lax
from jax.experimental import pallas as pl
from jax.experimental.pallas import tpu as pltpu
from jax.sharding import PartitionSpec as P

regular = 0.02
epsilon = 1e-06
settled = 1e-3
F32 = jnp.float32
BF16 = jnp.bfloat16
LANES = 128
GROUPS = ((0, 1), (2, 3, 4), (5, 6, 7))
SMALL = pltpu.CompilerParams(vmem_limit_bytes=16 * 1024 * 1024)


def across_rows(left, right):
    return lax.dot_general(left, right, (((1,), (1,)), ((), ())), preferred_element_type=F32)


def pieces_of(value, count):
    out = []
    for _ in range(count):
        piece = value.astype(BF16)
        value = value - piece.astype(F32)
        out.append(piece)
    return out


def product(left, right):
    a, b = pieces_of(left, 2), pieces_of(right, 2)
    dot = functools.partial(jnp.dot, preferred_element_type=F32)
    return dot(a[0], b[0]) + (dot(a[1], b[0]) + dot(a[0], b[1]))


def fine_product(left, right):
    a, b = pieces_of(left, 3), pieces_of(right, 3)
    dot = functools.partial(jnp.dot, preferred_element_type=F32)
    return dot(a[0], b[0]) + (
        (dot(a[0], b[1]) + dot(a[1], b[0]))
        + (dot(a[1], b[1]) + (dot(a[0], b[2]) + dot(a[2], b[0])))
    )


def gram_kernel(
    part, frames, reads_ref, source_ref, target_ref, send_ref, keep_ref, held_ref, goal_ref, turned_ref, sem
):
    coil = lax.axis_index("coil")
    core = lax.rem(lax.axis_index("frame"), 2)
    count, depth, samples = turned_ref.shape
    width = depth // 2
    half = part // 2
    coils = target_ref.shape[1]
    each = count // 2
    copies = []
    for slot in range(count):
        segment = 2 * (slot % each) + (1 - core if slot < each else core)
        copies.append(
            (
                pltpu.make_async_copy(source_ref.at[segment], held_ref.at[slot], sem.at[0, slot]),
                pltpu.make_async_copy(target_ref.at[segment], goal_ref.at[slot], sem.at[1, slot]),
            )
        )
    for pair in copies:
        for copy in pair:
            copy.start()
    row = lax.broadcasted_iota(jnp.int32, (8, LANES), 0)
    lane = lax.broadcasted_iota(jnp.int32, (8, LANES), 1)
    told = jnp.zeros((8, LANES), jnp.int32)
    for place in range(reads_ref.shape[1]):
        told = jnp.where((row == core) & (lane == place), lax.div(reads_ref[0, place], frames), told)
    told = told.astype(F32)
    across = lax.broadcasted_iota(jnp.int32, (part, width), 1)
    down = lax.broadcasted_iota(jnp.int32, (part, width), 0) + coil * part
    first = pl.multiple_of(coil * part, 16)
    second = pl.multiple_of(width + coil * part, 16)
    for slots in GROUPS:
        for slot in slots:
            for copy in copies[slot]:
                copy.wait()
        lefts = []
        for slot in slots:
            turned_ref[slot] = held_ref[slot].T
            lefts.append(
                jnp.concatenate(
                    [
                        turned_ref[slot, pl.ds(first, part)],
                        turned_ref[slot, pl.ds(second, part)],
                        goal_ref[slot, :, 0, :],
                        goal_ref[slot, :, 1, :],
                    ],
                    axis=0,
                )
            )
        products = [
            jnp.dot(left, held_ref[slot], preferred_element_type=F32)
            for left, slot in zip(lefts, slots)
        ]
        for slot, sums in zip(slots, products):
            out = (send_ref if slot < each else keep_ref).at[slot % each]
            top, bottom = sums[:part], sums[part : 2 * part]
            gram_real = top[:, :width] + bottom[:, width:]
            gram_imag = top[:, width:] - bottom[:, :width]
            packed = jnp.where(across <= down, gram_real, gram_imag)
            proj_real = sums[2 * part : 2 * part + coils]
            proj_imag = sums[2 * part + coils :]
            rhs_real = proj_real[:, :width] + proj_imag[:, width:]
            rhs_imag = proj_imag[:, :width] - proj_real[:, width:]
            out[:part] = packed[:, :LANES]
            out[part : part + half] = jnp.concatenate(
                [packed[:half, LANES:], packed[half:, LANES:]], axis=1
            )
            base = part + half
            out[base : base + coils] = rhs_real[:, :LANES]
            out[base + coils : base + 2 * coils] = rhs_imag[:, :LANES]
            out[base + 2 * coils : base + 3 * coils] = jnp.concatenate(
                [rhs_real[:, LANES:], rhs_imag[:, LANES:]], axis=1
            )
            out[base + 3 * coils :] = told


def sum_kernel(gram_rows, partial_ref, spread_ref, rhs_ref, told_ref):
    rows = gram_rows + rhs_ref.shape[0]
    total = partial_ref[0, :rows]
    for chip in range(1, partial_ref.shape[0]):
        total = total + partial_ref[chip, :rows]
    for copy in range(spread_ref.shape[0]):
        spread_ref[copy] = total[:gram_rows]
    rhs_ref[...] = total[gram_rows:]
    for chip in range(partial_ref.shape[0]):
        told_ref[2 * chip : 2 * chip + 2] = partial_ref[chip, rows : rows + 2].astype(jnp.int32)


def solve_kernel(part, gram_ref, rhs_ref, out_ref, real_ref, imag_ref, sol_ref):
    width = 4 * part
    half = part // 2
    coils = rhs_ref.shape[0] // 3
    pieces = []
    for coil in range(4):
        block = gram_ref[coil]
        tail = block[part:]
        pieces.append(
            jnp.concatenate(
                [block[:part], jnp.concatenate([tail[:, :64], tail[:, 64:]], axis=0)], axis=1
            )
        )
    packed = jnp.concatenate(pieces, axis=0)
    flipped = packed.T
    down = lax.broadcasted_iota(jnp.int32, (width, width), 0)
    across = lax.broadcasted_iota(jnp.int32, (width, width), 1)
    real = jnp.where(across <= down, packed, flipped)
    imag = jnp.where(across > down, packed, jnp.where(across < down, -flipped, 0.0))
    diagonal = jnp.where(across == down, packed, 0.0)
    shift = regular / width * jnp.sum(diagonal)
    high = jnp.sqrt(jnp.sum(real * real + imag * imag)) + shift
    scale = 2.0 / (high + shift)
    real_ref[...] = (real + jnp.where(across == down, shift, 0.0)) * scale
    imag_ref[...] = imag * scale
    rhs_real = jnp.concatenate([rhs_ref[:coils], rhs_ref[2 * coils :, :64]], axis=1)
    rhs_imag = jnp.concatenate([rhs_ref[coils : 2 * coils], rhs_ref[2 * coils :, 64:]], axis=1)
    sol_ref[...] = jnp.concatenate([rhs_real, rhs_imag], axis=0) * scale

    def step(product, spread):
        square = spread * spread
        factor = 2.0 / (2.0 - square)
        real, imag, sol = real_ref[...], imag_ref[...], sol_ref[...]
        first = product(jnp.concatenate([real, sol], axis=0), imag)
        second = product(jnp.concatenate([real - imag, sol], axis=0), real + imag)
        cross, thin = first[:width], first[width:]
        turned = cross.T
        by_real = second[width:] - thin
        change = jnp.concatenate(
            [by_real[:coils] + thin[coils:], by_real[coils:] - thin[:coils]], axis=0
        )
        sol_ref[...] = factor * (2.0 * sol - change)
        real_ref[...] = factor * (2.0 * real - (second[:width] - cross - turned))
        imag_ref[...] = factor * (2.0 * imag - (cross - turned))
        return square / (2.0 - square)

    spread = (high - shift) / (high + shift)
    spread = lax.while_loop(
        lambda spread: spread > 0.9, functools.partial(step, fine_product), spread
    )
    spread = lax.while_loop(
        lambda spread: spread > settled, functools.partial(step, product), spread
    )
    square = spread * spread
    sol = sol_ref[...]
    by_real = product(sol, real_ref[...])
    by_imag = product(sol, imag_ref[...])
    change = jnp.concatenate(
        [by_real[:coils] + by_imag[coils:], by_real[coils:] - by_imag[:coils]], axis=0
    )
    sol = 2.0 / (2.0 - square) * (2.0 * sol - change)
    weights = jnp.concatenate([sol[:coils], sol[coils:]], axis=1).astype(BF16)
    for copy in range(out_ref.shape[0]):
        out_ref[copy] = weights


def select_kernel(told_ref, piece_ref, out_ref):
    for frame in range(out_ref.shape[0]):
        for slot in range(out_ref.shape[1]):
            out_ref[frame, slot] = piece_ref[told_ref[frame, slot]]


def fill_kernel(reads_ref, places_ref, weights_ref, source_ref, interp_ref, out_ref, grid_ref):
    frames = weights_ref.shape[0]
    grid_ref[...] = jnp.zeros_like(grid_ref)
    for slot in range(weights_ref.shape[1]):
        chosen = weights_ref[lax.rem(reads_ref[0, slot], frames), slot].astype(F32)
        width = chosen.shape[1] // 2
        real, imag = chosen[:, :width], chosen[:, width:]
        matrix = jnp.concatenate(
            [jnp.concatenate([real, -imag], axis=1), jnp.concatenate([imag, real], axis=1)], axis=0
        ).astype(BF16)
        filled = across_rows(matrix, source_ref[0, slot]).astype(BF16)
        place = places_ref[0, slot]
        grid_ref[place] = grid_ref[place] + across_rows(filled, interp_ref[0, slot])
    out_ref[...] = grid_ref[...].astype(BF16)


def on_device(cal_source, cal_target, app_source, readers, blocks, interp):
    frames = lax.axis_size("frame")
    segs = lax.axis_size("seg")
    coil_count = lax.axis_size("coil")
    held, samples, depth = cal_source.shape
    coils = cal_target.shape[1]
    width = depth // 2
    part = width // coil_count
    gram_rows = part + part // 2
    rows = gram_rows + 3 * coils + 8
    slots = readers.shape[1]
    cells = interp.shape[2]

    each = held // 2
    block = jax.ShapeDtypeStruct((each, rows, LANES), F32)
    send, keep = pl.pallas_call(
        functools.partial(gram_kernel, part, frames),
        in_specs=[
            pl.BlockSpec(memory_space=pltpu.SMEM),
            pl.BlockSpec(memory_space=pltpu.HBM),
            pl.BlockSpec(memory_space=pltpu.HBM),
        ],
        out_shape=[block, block],
        scratch_shapes=[
            pltpu.VMEM((held, samples, depth), BF16),
            pltpu.VMEM((held, coils, 2, samples), BF16),
            pltpu.VMEM((held, depth, samples), BF16),
            pltpu.SemaphoreType.DMA((2, held)),
        ],
        compiler_params=SMALL,
    )(
        pltpu.with_memory_space_constraint(readers, pltpu.HBM),
        pltpu.with_memory_space_constraint(cal_source, pltpu.HBM),
        pltpu.with_memory_space_constraint(cal_target, pltpu.HBM),
    )
    other = lax.ppermute(send, "frame", [(frame, frame ^ 1) for frame in range(frames)])
    chips = [[2 * chip + core for chip in range(frames // 2)] for core in range(2)]
    received = lax.all_to_all(
        keep + other, "frame", 0, 0, tiled=True, axis_index_groups=chips
    )
    spread, rhs, told = pl.pallas_call(
        functools.partial(sum_kernel, gram_rows),
        out_shape=[
            jax.ShapeDtypeStruct((coil_count, gram_rows, LANES), F32),
            jax.ShapeDtypeStruct((3 * coils, LANES), F32),
            jax.ShapeDtypeStruct((frames, LANES), jnp.int32),
        ],
        compiler_params=SMALL,
    )(received)
    gram = lax.all_to_all(spread, "coil", 0, 0, tiled=True)
    weights = pl.pallas_call(
        functools.partial(solve_kernel, part),
        out_shape=jax.ShapeDtypeStruct((segs, coils, depth), BF16),
        scratch_shapes=[
            pltpu.VMEM((width, width), F32),
            pltpu.VMEM((width, width), F32),
            pltpu.VMEM((2 * coils, width), F32),
        ],
        compiler_params=SMALL,
    )(gram, rhs)
    pieces = lax.all_to_all(weights, "seg", 0, 0, tiled=True)
    sent = pl.pallas_call(
        select_kernel,
        in_specs=[
            pl.BlockSpec(memory_space=pltpu.SMEM),
            pl.BlockSpec(memory_space=pltpu.VMEM),
        ],
        out_shape=jax.ShapeDtypeStruct((frames, slots, coils, depth), BF16),
        compiler_params=SMALL,
    )(told, pieces)
    chosen = lax.all_to_all(sent, "frame", 0, 0, tiled=True)
    grid = pl.pallas_call(
        fill_kernel,
        in_specs=[
            pl.BlockSpec(memory_space=pltpu.SMEM),
            pl.BlockSpec(memory_space=pltpu.SMEM),
            pl.BlockSpec(memory_space=pltpu.VMEM),
            pl.BlockSpec(memory_space=pltpu.VMEM),
            pl.BlockSpec(memory_space=pltpu.VMEM),
        ],
        out_shape=jax.ShapeDtypeStruct((segs, 2 * coils, cells), BF16),
        scratch_shapes=[pltpu.VMEM((segs, 2 * coils, cells), F32)],
        compiler_params=SMALL,
    )(readers, blocks, chosen, app_source, interp)
    terms = lax.all_to_all(grid, "seg", 0, 0, tiled=True)
    total = jnp.sum(terms.astype(F32), axis=0)
    power = lax.all_gather(jnp.sum(total * total, axis=0, keepdims=True), "coil", tiled=True)
    return jnp.sqrt(jnp.sum(power, axis=0, keepdims=True) + epsilon)


def solution(mesh):
    placed = (
        P("seg", "frame", None),
        P("seg", "coil", None, "frame"),
        P("frame", "seg", None, None),
        P("frame", "seg"),
        P("frame", "seg"),
        P("frame", "seg", None, None),
    )
    return jax.shard_map(
        on_device, mesh=mesh, in_specs=placed, out_specs=P("frame", "seg"), check_vma=False
    )
```

```python
import functools

import jax
import jax.numpy as jnp
from jax import lax
from jax.experimental import pallas as pl
from jax.experimental.pallas import tpu as pltpu
from jax.sharding import PartitionSpec as P

regular = 0.02
epsilon = 1e-06
settled = 1e-3
F32 = jnp.float32
BF16 = jnp.bfloat16
LANES = 128
GROUPS = ((0, 1), (2, 3, 4), (5, 6, 7))
SMALL = pltpu.CompilerParams(vmem_limit_bytes=16 * 1024 * 1024)


def across_rows(left, right):
    return lax.dot_general(left, right, (((1,), (1,)), ((), ())), preferred_element_type=F32)


def pieces_of(value, count):
    out = []
    for _ in range(count):
        piece = value.astype(BF16)
        value = value - piece.astype(F32)
        out.append(piece)
    return out


def product(left, right):
    a, b = pieces_of(left, 2), pieces_of(right, 2)
    dot = functools.partial(jnp.dot, preferred_element_type=F32)
    return dot(a[0], b[0]) + (dot(a[1], b[0]) + dot(a[0], b[1]))


def fine_product(left, right):
    a, b = pieces_of(left, 3), pieces_of(right, 3)
    dot = functools.partial(jnp.dot, preferred_element_type=F32)
    return dot(a[0], b[0]) + (
        (dot(a[0], b[1]) + dot(a[1], b[0]))
        + (dot(a[1], b[1]) + (dot(a[0], b[2]) + dot(a[2], b[0])))
    )


def gram_kernel(
    part,
    frames,
    reads_ref,
    source_ref,
    target_ref,
    send_ref,
    keep_ref,
    held_ref,
    goal_ref,
    turned_ref,
    read_ref,
    sem,
    read_sem,
):
    coil = lax.axis_index("coil")
    core = lax.rem(lax.axis_index("frame"), 2)
    count, depth, samples = turned_ref.shape
    width = depth // 2
    half = part // 2
    base = part + half
    coils = target_ref.shape[1]
    each = count // 2
    copies = []
    for slot in range(count):
        segment = 2 * (slot % each) + (1 - core if slot < each else core)
        copies.append(
            (
                pltpu.make_async_copy(source_ref.at[segment], held_ref.at[slot], sem.at[0, slot]),
                pltpu.make_async_copy(target_ref.at[segment], goal_ref.at[slot], sem.at[1, slot]),
            )
        )
    for pair in copies:
        for copy in pair:
            copy.start()
    listing = pltpu.make_async_copy(reads_ref, read_ref, read_sem)
    listing.start()
    across = lax.broadcasted_iota(jnp.int32, (part, width), 1)
    down = lax.broadcasted_iota(jnp.int32, (part, width), 0) + coil * part
    first = pl.multiple_of(coil * part, 16)
    second = pl.multiple_of(width + coil * part, 16)
    for slots in GROUPS:
        for slot in slots:
            for copy in copies[slot]:
                copy.wait()
        lefts = []
        for slot in slots:
            turned_ref[slot] = held_ref[slot].T
            lefts.append(
                jnp.concatenate(
                    [
                        turned_ref[slot, pl.ds(first, part)],
                        turned_ref[slot, pl.ds(second, part)],
                        goal_ref[slot, :, 0, :],
                        goal_ref[slot, :, 1, :],
                    ],
                    axis=0,
                )
            )
        products = [
            jnp.dot(left, held_ref[slot], preferred_element_type=F32)
            for left, slot in zip(lefts, slots)
        ]
        for slot, sums in zip(slots, products):
            out = (send_ref if slot < each else keep_ref).at[slot % each]
            top, bottom = sums[:part], sums[part : 2 * part]
            gram_real = top[:, :width] + bottom[:, width:]
            gram_imag = top[:, width:] - bottom[:, :width]
            packed = jnp.where(across <= down, gram_real, gram_imag)
            proj_real = sums[2 * part : 2 * part + coils]
            proj_imag = sums[2 * part + coils :]
            rhs_real = proj_real[:, :width] + proj_imag[:, width:]
            rhs_imag = proj_imag[:, :width] - proj_real[:, width:]
            out[:part] = packed[:, :LANES]
            out[part : part + half] = jnp.concatenate(
                [packed[:half, LANES:], packed[half:, LANES:]], axis=1
            )
            out[base : base + coils] = rhs_real[:, :LANES]
            out[base + coils : base + 2 * coils] = rhs_imag[:, :LANES]
            out[base + 2 * coils : base + 3 * coils] = jnp.concatenate(
                [rhs_real[:, LANES:], rhs_imag[:, LANES:]], axis=1
            )
    listing.wait()
    row = lax.broadcasted_iota(jnp.int32, (8, LANES), 0)
    lane = lax.broadcasted_iota(jnp.int32, (8, LANES), 1)
    told = jnp.zeros((8, LANES), jnp.int32)
    for place in range(read_ref.shape[1]):
        told = jnp.where((row == core) & (lane == place), lax.div(read_ref[0, place], frames), told)
    told = told.astype(F32)
    for slot in range(each):
        send_ref[slot, base + 3 * coils :] = told
        keep_ref[slot, base + 3 * coils :] = told


def sum_kernel(gram_rows, partial_ref, spread_ref, rhs_ref, told_ref):
    rows = gram_rows + rhs_ref.shape[0]
    total = partial_ref[0, :rows]
    for chip in range(1, partial_ref.shape[0]):
        total = total + partial_ref[chip, :rows]
    for copy in range(spread_ref.shape[0]):
        spread_ref[copy] = total[:gram_rows]
    rhs_ref[...] = total[gram_rows:]
    for chip in range(partial_ref.shape[0]):
        told_ref[2 * chip : 2 * chip + 2] = partial_ref[chip, rows : rows + 2].astype(jnp.int32)


def solve_kernel(part, gram_ref, rhs_ref, out_ref, real_ref, imag_ref, sol_ref):
    width = 4 * part
    half = part // 2
    coils = rhs_ref.shape[0] // 3
    pieces = []
    for coil in range(4):
        block = gram_ref[coil]
        tail = block[part:]
        pieces.append(
            jnp.concatenate(
                [block[:part], jnp.concatenate([tail[:, :64], tail[:, 64:]], axis=0)], axis=1
            )
        )
    packed = jnp.concatenate(pieces, axis=0)
    flipped = packed.T
    down = lax.broadcasted_iota(jnp.int32, (width, width), 0)
    across = lax.broadcasted_iota(jnp.int32, (width, width), 1)
    real = jnp.where(across <= down, packed, flipped)
    imag = jnp.where(across > down, packed, jnp.where(across < down, -flipped, 0.0))
    diagonal = jnp.where(across == down, packed, 0.0)
    shift = regular / width * jnp.sum(diagonal)
    high = jnp.sqrt(jnp.sum(real * real + imag * imag)) + shift
    scale = 2.0 / (high + shift)
    real_ref[...] = (real + jnp.where(across == down, shift, 0.0)) * scale
    imag_ref[...] = imag * scale
    rhs_real = jnp.concatenate([rhs_ref[:coils], rhs_ref[2 * coils :, :64]], axis=1)
    rhs_imag = jnp.concatenate([rhs_ref[coils : 2 * coils], rhs_ref[2 * coils :, 64:]], axis=1)
    sol_ref[...] = jnp.concatenate([rhs_real, rhs_imag], axis=0) * scale

    def step(product, spread):
        square = spread * spread
        factor = 2.0 / (2.0 - square)
        real, imag, sol = real_ref[...], imag_ref[...], sol_ref[...]
        first = product(jnp.concatenate([real, sol], axis=0), imag)
        second = product(jnp.concatenate([real - imag, sol], axis=0), real + imag)
        cross, thin = first[:width], first[width:]
        turned = cross.T
        by_real = second[width:] - thin
        change = jnp.concatenate(
            [by_real[:coils] + thin[coils:], by_real[coils:] - thin[:coils]], axis=0
        )
        sol_ref[...] = factor * (2.0 * sol - change)
        real_ref[...] = factor * (2.0 * real - (second[:width] - cross - turned))
        imag_ref[...] = factor * (2.0 * imag - (cross - turned))
        return square / (2.0 - square)

    spread = (high - shift) / (high + shift)
    spread = lax.while_loop(
        lambda spread: spread > 0.97, functools.partial(step, fine_product), spread
    )
    spread = lax.while_loop(
        lambda spread: spread > settled, functools.partial(step, product), spread
    )
    square = spread * spread
    sol = sol_ref[...]
    by_real = product(sol, real_ref[...])
    by_imag = product(sol, imag_ref[...])
    change = jnp.concatenate(
        [by_real[:coils] + by_imag[coils:], by_real[coils:] - by_imag[:coils]], axis=0
    )
    sol = 2.0 / (2.0 - square) * (2.0 * sol - change)
    weights = jnp.concatenate([sol[:coils], sol[coils:]], axis=1).astype(BF16)
    for copy in range(out_ref.shape[0]):
        out_ref[copy] = weights


def select_kernel(told_ref, piece_ref, out_ref):
    for frame in range(out_ref.shape[0]):
        for slot in range(out_ref.shape[1]):
            out_ref[frame, slot] = piece_ref[told_ref[frame, slot]]


def fill_kernel(reads_ref, places_ref, weights_ref, source_ref, interp_ref, out_ref):
    frames, slots, coils, depth = weights_ref.shape
    width = depth // 2
    terms = []
    for slot in range(slots):
        holder = jnp.broadcast_to(reads_ref[:, slot : slot + 1] & (frames - 1), (coils, depth))
        chosen = weights_ref[0, slot].astype(F32)
        for frame in range(1, frames):
            chosen = jnp.where(holder == frame, weights_ref[frame, slot].astype(F32), chosen)
        real, imag = chosen[:, :width], chosen[:, width:]
        matrix = jnp.concatenate(
            [jnp.concatenate([real, -imag], axis=1), jnp.concatenate([imag, real], axis=1)], axis=0
        ).astype(BF16)
        filled = across_rows(matrix, source_ref[0, slot]).astype(BF16)
        terms.append(across_rows(filled, interp_ref[0, slot]))
    shape = terms[0].shape
    places = [jnp.broadcast_to(places_ref[:, slot : slot + 1], shape) for slot in range(slots)]
    for block in range(out_ref.shape[0]):
        total = jnp.zeros(shape, F32)
        for place, term in zip(places, terms):
            total = total + jnp.where(place == block, term, 0.0)
        out_ref[block] = total.astype(BF16)


def on_device(cal_source, cal_target, app_source, readers, blocks, interp):
    frames = lax.axis_size("frame")
    segs = lax.axis_size("seg")
    coil_count = lax.axis_size("coil")
    held, samples, depth = cal_source.shape
    coils = cal_target.shape[1]
    width = depth // 2
    part = width // coil_count
    gram_rows = part + part // 2
    rows = gram_rows + 3 * coils + 8
    slots = readers.shape[1]
    cells = interp.shape[2]

    each = held // 2
    block = jax.ShapeDtypeStruct((each, rows, LANES), F32)
    send, keep = pl.pallas_call(
        functools.partial(gram_kernel, part, frames),
        in_specs=[
            pl.BlockSpec(memory_space=pltpu.HBM),
            pl.BlockSpec(memory_space=pltpu.HBM),
            pl.BlockSpec(memory_space=pltpu.HBM),
        ],
        out_shape=[block, block],
        scratch_shapes=[
            pltpu.VMEM((held, samples, depth), BF16),
            pltpu.VMEM((held, coils, 2, samples), BF16),
            pltpu.VMEM((held, depth, samples), BF16),
            pltpu.SMEM(readers.shape, jnp.int32),
            pltpu.SemaphoreType.DMA((2, held)),
            pltpu.SemaphoreType.DMA,
        ],
        compiler_params=SMALL,
    )(
        pltpu.with_memory_space_constraint(readers, pltpu.HBM),
        pltpu.with_memory_space_constraint(cal_source, pltpu.HBM),
        pltpu.with_memory_space_constraint(cal_target, pltpu.HBM),
    )
    other = lax.ppermute(send, "frame", [(frame, frame ^ 1) for frame in range(frames)])
    chips = [[2 * chip + core for chip in range(frames // 2)] for core in range(2)]
    received = lax.all_to_all(
        keep + other, "frame", 0, 0, tiled=True, axis_index_groups=chips
    )
    spread, rhs, told = pl.pallas_call(
        functools.partial(sum_kernel, gram_rows),
        out_shape=[
            jax.ShapeDtypeStruct((coil_count, gram_rows, LANES), F32),
            jax.ShapeDtypeStruct((3 * coils, LANES), F32),
            jax.ShapeDtypeStruct((frames, LANES), jnp.int32),
        ],
        compiler_params=SMALL,
    )(received)
    gram = lax.all_to_all(spread, "coil", 0, 0, tiled=True)
    weights = pl.pallas_call(
        functools.partial(solve_kernel, part),
        out_shape=jax.ShapeDtypeStruct((segs, coils, depth), BF16),
        scratch_shapes=[
            pltpu.VMEM((width, width), F32),
            pltpu.VMEM((width, width), F32),
            pltpu.VMEM((2 * coils, width), F32),
        ],
        compiler_params=SMALL,
    )(gram, rhs)
    pieces = lax.all_to_all(weights, "seg", 0, 0, tiled=True)
    sent = pl.pallas_call(
        select_kernel,
        in_specs=[
            pl.BlockSpec(memory_space=pltpu.SMEM),
            pl.BlockSpec(memory_space=pltpu.VMEM),
        ],
        out_shape=jax.ShapeDtypeStruct((frames, slots, coils, depth), BF16),
        compiler_params=SMALL,
    )(told, pieces)
    chosen = lax.all_to_all(sent, "frame", 0, 0, tiled=True)
    grid = pl.pallas_call(
        fill_kernel,
        out_shape=jax.ShapeDtypeStruct((segs, 2 * coils, cells), BF16),
        compiler_params=SMALL,
    )(readers, blocks, chosen, app_source, interp)
    terms = lax.all_to_all(grid, "seg", 0, 0, tiled=True)
    total = jnp.sum(terms.astype(F32), axis=0)
    power = lax.all_gather(jnp.sum(total * total, axis=0, keepdims=True), "coil", tiled=True)
    return jnp.sqrt(jnp.sum(power, axis=0, keepdims=True) + epsilon)


def solution(mesh):
    placed = (
        P("seg", "frame", None),
        P("seg", "coil", None, "frame"),
        P("frame", "seg", None, None),
        P("frame", "seg"),
        P("frame", "seg"),
        P("frame", "seg", None, None),
    )
    return jax.shard_map(
        on_device, mesh=mesh, in_specs=placed, out_specs=P("frame", "seg"), check_vma=False
    )
```

```python
import functools

import jax
import jax.numpy as jnp
from jax import lax
from jax.experimental import pallas as pl
from jax.experimental.pallas import tpu as pltpu
from jax.sharding import PartitionSpec as P

regular = 0.02
epsilon = 1e-06
settled = 1e-3
F32 = jnp.float32
BF16 = jnp.bfloat16
LANES = 128
SMALL = pltpu.CompilerParams(vmem_limit_bytes=16 * 1024 * 1024)


def across_rows(left, right):
    return lax.dot_general(left, right, (((1,), (1,)), ((), ())), preferred_element_type=F32)


def pieces_of(value, count):
    out = []
    for _ in range(count):
        piece = value.astype(BF16)
        value = value - piece.astype(F32)
        out.append(piece)
    return out


def product(left, right):
    a, b = pieces_of(left, 2), pieces_of(right, 2)
    dot = functools.partial(jnp.dot, preferred_element_type=F32)
    return dot(a[0], b[0]) + (dot(a[1], b[0]) + dot(a[0], b[1]))


def fine_product(left, right):
    a, b = pieces_of(left, 3), pieces_of(right, 3)
    dot = functools.partial(jnp.dot, preferred_element_type=F32)
    return dot(a[0], b[0]) + (
        (dot(a[0], b[1]) + dot(a[1], b[0]))
        + (dot(a[1], b[1]) + (dot(a[0], b[2]) + dot(a[2], b[0])))
    )


def gram_sums(part, groups, held_ref, goal_ref, turned_ref, out_ref, copies):
    coil = lax.axis_index("coil")
    depth = held_ref.shape[2]
    width = depth // 2
    half = part // 2
    base = part + half
    coils = goal_ref.shape[1]
    across = lax.broadcasted_iota(jnp.int32, (part, width), 1)
    down = lax.broadcasted_iota(jnp.int32, (part, width), 0) + coil * part
    first = pl.multiple_of(coil * part, 16)
    second = pl.multiple_of(width + coil * part, 16)
    for slots in groups:
        for slot in slots:
            for copy in copies[slot]:
                copy.wait()
        lefts = []
        for slot in slots:
            turned_ref[slot] = held_ref[slot].T
            lefts.append(
                jnp.concatenate(
                    [
                        turned_ref[slot, pl.ds(first, part)],
                        turned_ref[slot, pl.ds(second, part)],
                        goal_ref[slot, :, 0, :],
                        goal_ref[slot, :, 1, :],
                    ],
                    axis=0,
                )
            )
        products = [
            jnp.dot(left, held_ref[slot], preferred_element_type=F32)
            for left, slot in zip(lefts, slots)
        ]
        for slot, sums in zip(slots, products):
            out = out_ref.at[slot]
            top, bottom = sums[:part], sums[part : 2 * part]
            gram_real = top[:, :width] + bottom[:, width:]
            gram_imag = top[:, width:] - bottom[:, :width]
            packed = jnp.where(across <= down, gram_real, gram_imag)
            proj_real = sums[2 * part : 2 * part + coils]
            proj_imag = sums[2 * part + coils :]
            rhs_real = proj_real[:, :width] + proj_imag[:, width:]
            rhs_imag = proj_imag[:, :width] - proj_real[:, width:]
            out[:part] = packed[:, :LANES]
            out[part:base] = jnp.concatenate(
                [packed[:half, LANES:], packed[half:, LANES:]], axis=1
            )
            out[base : base + coils] = rhs_real[:, :LANES]
            out[base + coils : base + 2 * coils] = rhs_imag[:, :LANES]
            out[base + 2 * coils : base + 3 * coils] = jnp.concatenate(
                [rhs_real[:, LANES:], rhs_imag[:, LANES:]], axis=1
            )


def tell(frames, read_ref, out_ref):
    core = lax.rem(lax.axis_index("frame"), 2)
    row = lax.broadcasted_iota(jnp.int32, (8, LANES), 0)
    lane = lax.broadcasted_iota(jnp.int32, (8, LANES), 1)
    told = jnp.zeros((8, LANES), jnp.int32)
    for place in range(read_ref.shape[1]):
        told = jnp.where((row == core) & (lane == place), lax.div(read_ref[0, place], frames), told)
    for slot in range(out_ref.shape[0]):
        out_ref[slot, out_ref.shape[1] - 8 :] = told.astype(F32)


def other_gram_kernel(
    part,
    frames,
    reads_ref,
    source_ref,
    target_ref,
    out_ref,
    own_held_ref,
    own_goal_ref,
    held_ref,
    goal_ref,
    turned_ref,
    read_ref,
    sem,
    read_sem,
):
    core = lax.rem(lax.axis_index("frame"), 2)
    each = out_ref.shape[0]
    copies = []
    for slot in range(2 * each):
        own, place = slot // each, slot % each
        segment = 2 * place + (core if own else 1 - core)
        held = (own_held_ref if own else held_ref).at[place]
        goal = (own_goal_ref if own else goal_ref).at[place]
        copies.append(
            (
                pltpu.make_async_copy(source_ref.at[segment], held, sem.at[0, slot]),
                pltpu.make_async_copy(target_ref.at[segment], goal, sem.at[1, slot]),
            )
        )
    for pair in copies:
        for copy in pair:
            copy.start()
    listing = pltpu.make_async_copy(reads_ref, read_ref, read_sem)
    listing.start()
    gram_sums(part, ((0, 1), (2, 3)), held_ref, goal_ref, turned_ref, out_ref, copies)
    listing.wait()
    tell(frames, read_ref, out_ref)
    for pair in copies[each:]:
        for copy in pair:
            copy.wait()


def own_gram_kernel(part, frames, reads_ref, held_ref, goal_ref, out_ref, turned_ref, read_ref, read_sem):
    listing = pltpu.make_async_copy(reads_ref, read_ref, read_sem)
    listing.start()
    slots = tuple(range(out_ref.shape[0]))
    gram_sums(part, (slots,), held_ref, goal_ref, turned_ref, out_ref, [() for _ in slots])
    listing.wait()
    tell(frames, read_ref, out_ref)


def sum_kernel(gram_rows, partial_ref, spread_ref, rhs_ref, told_ref):
    rows = gram_rows + rhs_ref.shape[0]
    total = partial_ref[0, :rows]
    for chip in range(1, partial_ref.shape[0]):
        total = total + partial_ref[chip, :rows]
    for copy in range(spread_ref.shape[0]):
        spread_ref[copy] = total[:gram_rows]
    rhs_ref[...] = total[gram_rows:]
    for chip in range(partial_ref.shape[0]):
        told_ref[2 * chip : 2 * chip + 2] = partial_ref[chip, rows : rows + 2].astype(jnp.int32)


def solve_kernel(part, gram_ref, rhs_ref, out_ref, real_ref, imag_ref, sol_ref):
    width = 4 * part
    half = part // 2
    coils = rhs_ref.shape[0] // 3
    pieces = []
    for coil in range(4):
        block = gram_ref[coil]
        tail = block[part:]
        pieces.append(
            jnp.concatenate(
                [block[:part], jnp.concatenate([tail[:, :64], tail[:, 64:]], axis=0)], axis=1
            )
        )
    packed = jnp.concatenate(pieces, axis=0)
    flipped = packed.T
    down = lax.broadcasted_iota(jnp.int32, (width, width), 0)
    across = lax.broadcasted_iota(jnp.int32, (width, width), 1)
    real = jnp.where(across <= down, packed, flipped)
    imag = jnp.where(across > down, packed, jnp.where(across < down, -flipped, 0.0))
    diagonal = jnp.where(across == down, packed, 0.0)
    shift = regular / width * jnp.sum(diagonal)
    high = jnp.sqrt(jnp.sum(real * real + imag * imag)) + shift
    scale = 2.0 / (high + shift)
    real_ref[...] = (real + jnp.where(across == down, shift, 0.0)) * scale
    imag_ref[...] = imag * scale
    rhs_real = jnp.concatenate([rhs_ref[:coils], rhs_ref[2 * coils :, :64]], axis=1)
    rhs_imag = jnp.concatenate([rhs_ref[coils : 2 * coils], rhs_ref[2 * coils :, 64:]], axis=1)
    sol_ref[...] = jnp.concatenate([rhs_real, rhs_imag], axis=0) * scale

    def step(product, spread):
        square = spread * spread
        factor = 2.0 / (2.0 - square)
        real, imag, sol = real_ref[...], imag_ref[...], sol_ref[...]
        first = product(jnp.concatenate([real, sol], axis=0), imag)
        second = product(jnp.concatenate([real - imag, sol], axis=0), real + imag)
        cross, thin = first[:width], first[width:]
        turned = cross.T
        by_real = second[width:] - thin
        change = jnp.concatenate(
            [by_real[:coils] + thin[coils:], by_real[coils:] - thin[:coils]], axis=0
        )
        sol_ref[...] = factor * (2.0 * sol - change)
        real_ref[...] = factor * (2.0 * real - (second[:width] - cross - turned))
        imag_ref[...] = factor * (2.0 * imag - (cross - turned))
        return square / (2.0 - square)

    spread = (high - shift) / (high + shift)
    spread = lax.while_loop(
        lambda spread: spread > 0.97, functools.partial(step, fine_product), spread
    )
    spread = lax.while_loop(
        lambda spread: spread > settled, functools.partial(step, product), spread
    )
    square = spread * spread
    sol = sol_ref[...]
    by_real = product(sol, real_ref[...])
    by_imag = product(sol, imag_ref[...])
    change = jnp.concatenate(
        [by_real[:coils] + by_imag[coils:], by_real[coils:] - by_imag[:coils]], axis=0
    )
    sol = 2.0 / (2.0 - square) * (2.0 * sol - change)
    weights = jnp.concatenate([sol[:coils], sol[coils:]], axis=1).astype(BF16)
    for copy in range(out_ref.shape[0]):
        out_ref[copy] = weights


def select_kernel(told_ref, piece_ref, out_ref):
    for frame in range(out_ref.shape[0]):
        for slot in range(out_ref.shape[1]):
            out_ref[frame, slot] = piece_ref[told_ref[frame, slot]]


def fill_kernel(reads_ref, places_ref, weights_ref, source_ref, interp_ref, out_ref):
    frames, slots, coils, depth = weights_ref.shape
    width = depth // 2
    terms = []
    for slot in range(slots):
        holder = jnp.broadcast_to(reads_ref[:, slot : slot + 1] & (frames - 1), (coils, depth))
        chosen = weights_ref[0, slot].astype(F32)
        for frame in range(1, frames):
            chosen = jnp.where(holder == frame, weights_ref[frame, slot].astype(F32), chosen)
        real, imag = chosen[:, :width], chosen[:, width:]
        matrix = jnp.concatenate(
            [jnp.concatenate([real, -imag], axis=1), jnp.concatenate([imag, real], axis=1)], axis=0
        ).astype(BF16)
        filled = across_rows(matrix, source_ref[0, slot]).astype(BF16)
        terms.append(across_rows(filled, interp_ref[0, slot]))
    shape = terms[0].shape
    places = [jnp.broadcast_to(places_ref[:, slot : slot + 1], shape) for slot in range(slots)]
    for block in range(out_ref.shape[0]):
        total = jnp.zeros(shape, F32)
        for place, term in zip(places, terms):
            total = total + jnp.where(place == block, term, 0.0)
        out_ref[block] = total.astype(BF16)


def on_device(cal_source, cal_target, app_source, readers, blocks, interp):
    frames = lax.axis_size("frame")
    segs = lax.axis_size("seg")
    coil_count = lax.axis_size("coil")
    held, samples, depth = cal_source.shape
    coils = cal_target.shape[1]
    width = depth // 2
    part = width // coil_count
    gram_rows = part + part // 2
    rows = gram_rows + 3 * coils + 8
    slots = readers.shape[1]
    cells = interp.shape[2]

    each = held // 2
    block = jax.ShapeDtypeStruct((each, rows, LANES), F32)
    listed = pltpu.with_memory_space_constraint(readers, pltpu.HBM)
    hbm = pl.BlockSpec(memory_space=pltpu.HBM)
    vmem = pl.BlockSpec(memory_space=pltpu.VMEM)
    reading = [pltpu.SMEM(readers.shape, jnp.int32)]
    turned = pltpu.VMEM((each, depth, samples), BF16)
    cost = pl.CostEstimate(
        flops=2 * each * samples * depth * 2 * (part + coils),
        bytes_accessed=2 * each * samples * (depth + 2 * coils),
        transcendentals=0,
    )
    send, own_held, own_goal = pl.pallas_call(
        functools.partial(other_gram_kernel, part, frames),
        in_specs=[hbm, hbm, hbm],
        out_shape=[
            block,
            jax.ShapeDtypeStruct((each, samples, depth), BF16),
            jax.ShapeDtypeStruct((each, coils, 2, samples), BF16),
        ],
        scratch_shapes=[
            pltpu.VMEM((each, samples, depth), BF16),
            pltpu.VMEM((each, coils, 2, samples), BF16),
            turned,
            *reading,
            pltpu.SemaphoreType.DMA((2, held)),
            pltpu.SemaphoreType.DMA,
        ],
        compiler_params=SMALL,
        cost_estimate=cost,
    )(
        listed,
        pltpu.with_memory_space_constraint(cal_source, pltpu.HBM),
        pltpu.with_memory_space_constraint(cal_target, pltpu.HBM),
    )
    keep = pl.pallas_call(
        functools.partial(own_gram_kernel, part, frames),
        in_specs=[hbm, vmem, vmem],
        out_shape=block,
        scratch_shapes=[turned, *reading, pltpu.SemaphoreType.DMA],
        compiler_params=SMALL,
        cost_estimate=cost,
    )(listed, own_held, own_goal)
    other = lax.ppermute(send, "frame", [(frame, frame ^ 1) for frame in range(frames)])
    chips = [[2 * chip + core for chip in range(frames // 2)] for core in range(2)]
    received = lax.all_to_all(
        keep + other, "frame", 0, 0, tiled=True, axis_index_groups=chips
    )
    spread, rhs, told = pl.pallas_call(
        functools.partial(sum_kernel, gram_rows),
        out_shape=[
            jax.ShapeDtypeStruct((coil_count, gram_rows, LANES), F32),
            jax.ShapeDtypeStruct((3 * coils, LANES), F32),
            jax.ShapeDtypeStruct((frames, LANES), jnp.int32),
        ],
        compiler_params=SMALL,
    )(received)
    gram = lax.all_to_all(spread, "coil", 0, 0, tiled=True)
    weights = pl.pallas_call(
        functools.partial(solve_kernel, part),
        out_shape=jax.ShapeDtypeStruct((segs, coils, depth), BF16),
        scratch_shapes=[
            pltpu.VMEM((width, width), F32),
            pltpu.VMEM((width, width), F32),
            pltpu.VMEM((2 * coils, width), F32),
        ],
        compiler_params=SMALL,
    )(gram, rhs)
    pieces = lax.all_to_all(weights, "seg", 0, 0, tiled=True)
    sent = pl.pallas_call(
        select_kernel,
        in_specs=[
            pl.BlockSpec(memory_space=pltpu.SMEM),
            pl.BlockSpec(memory_space=pltpu.VMEM),
        ],
        out_shape=jax.ShapeDtypeStruct((frames, slots, coils, depth), BF16),
        compiler_params=SMALL,
    )(told, pieces)
    chosen = lax.all_to_all(sent, "frame", 0, 0, tiled=True)
    grid = pl.pallas_call(
        fill_kernel,
        out_shape=jax.ShapeDtypeStruct((segs, 2 * coils, cells), BF16),
        compiler_params=SMALL,
    )(readers, blocks, chosen, app_source, interp)
    terms = lax.all_to_all(grid, "seg", 0, 0, tiled=True)
    total = jnp.sum(terms.astype(F32), axis=0)
    power = lax.all_gather(jnp.sum(total * total, axis=0, keepdims=True), "coil", tiled=True)
    return jnp.sqrt(jnp.sum(power, axis=0, keepdims=True) + epsilon)


def solution(mesh):
    placed = (
        P("seg", "frame", None),
        P("seg", "coil", None, "frame"),
        P("frame", "seg", None, None),
        P("frame", "seg"),
        P("frame", "seg"),
        P("frame", "seg", None, None),
    )
    return jax.shard_map(
        on_device, mesh=mesh, in_specs=placed, out_specs=P("frame", "seg"), check_vma=False
    )
```

```python
import functools

import jax
import jax.numpy as jnp
from jax import lax
from jax.experimental import pallas as pl
from jax.experimental.pallas import tpu as pltpu
from jax.sharding import PartitionSpec as P

regular = 0.02
epsilon = 1e-06
settled = 0.0125
F32 = jnp.float32
BF16 = jnp.bfloat16
LANES = 128
SMALL = pltpu.CompilerParams(vmem_limit_bytes=16 * 1024 * 1024)


def across_rows(left, right):
    return lax.dot_general(left, right, (((1,), (1,)), ((), ())), preferred_element_type=F32)


def pieces_of(value, count):
    out = []
    for _ in range(count):
        piece = value.astype(BF16)
        value = value - piece.astype(F32)
        out.append(piece)
    return out


def product(left, right):
    rows = left.shape[0]
    a, b = pieces_of(left, 2), pieces_of(right, 2)
    dot = functools.partial(jnp.dot, preferred_element_type=F32)
    first = dot(jnp.concatenate(a, axis=0), b[0])
    return first[:rows] + (first[rows:] + dot(a[0], b[1]))


def fine_product(left, right):
    rows = left.shape[0]
    a, b = pieces_of(left, 3), pieces_of(right, 3)
    dot = functools.partial(jnp.dot, preferred_element_type=F32)
    first = dot(jnp.concatenate(a, axis=0), b[0])
    second = dot(jnp.concatenate(a[:2], axis=0), b[1])
    return first[:rows] + (
        (first[rows : 2 * rows] + second[:rows])
        + (first[2 * rows :] + (second[rows:] + dot(a[0], b[2])))
    )


def gram_sums(part, groups, held_ref, goal_ref, turned_ref, out_ref, copies):
    coil = lax.axis_index("coil")
    depth = held_ref.shape[2]
    width = depth // 2
    half = part // 2
    base = part + half
    coils = goal_ref.shape[1]
    across = lax.broadcasted_iota(jnp.int32, (part, width), 1)
    down = lax.broadcasted_iota(jnp.int32, (part, width), 0) + coil * part
    first = pl.multiple_of(coil * part, 16)
    second = pl.multiple_of(width + coil * part, 16)
    for slots in groups:
        for slot in slots:
            for copy in copies[slot]:
                copy.wait()
        lefts = []
        for slot in slots:
            turned_ref[slot] = held_ref[slot].T
            lefts.append(
                jnp.concatenate(
                    [
                        turned_ref[slot, pl.ds(first, part)],
                        turned_ref[slot, pl.ds(second, part)],
                        goal_ref[slot, :, 0, :],
                        goal_ref[slot, :, 1, :],
                    ],
                    axis=0,
                )
            )
        products = [
            jnp.dot(left, held_ref[slot], preferred_element_type=F32)
            for left, slot in zip(lefts, slots)
        ]
        for slot, sums in zip(slots, products):
            out = out_ref.at[slot]
            top, bottom = sums[:part], sums[part : 2 * part]
            gram_real = top[:, :width] + bottom[:, width:]
            gram_imag = top[:, width:] - bottom[:, :width]
            packed = jnp.where(across <= down, gram_real, gram_imag)
            proj_real = sums[2 * part : 2 * part + coils]
            proj_imag = sums[2 * part + coils :]
            rhs_real = proj_real[:, :width] + proj_imag[:, width:]
            rhs_imag = proj_imag[:, :width] - proj_real[:, width:]
            out[:part] = packed[:, :LANES]
            out[part:base] = jnp.concatenate(
                [packed[:half, LANES:], packed[half:, LANES:]], axis=1
            )
            out[base : base + coils] = rhs_real[:, :LANES]
            out[base + coils : base + 2 * coils] = rhs_imag[:, :LANES]
            out[base + 2 * coils : base + 3 * coils] = jnp.concatenate(
                [rhs_real[:, LANES:], rhs_imag[:, LANES:]], axis=1
            )


def tell(frames, read_ref, out_ref):
    core = lax.rem(lax.axis_index("frame"), 2)
    row = lax.broadcasted_iota(jnp.int32, (8, LANES), 0)
    lane = lax.broadcasted_iota(jnp.int32, (8, LANES), 1)
    told = jnp.zeros((8, LANES), jnp.int32)
    for place in range(read_ref.shape[1]):
        told = jnp.where((row == core) & (lane == place), lax.div(read_ref[0, place], frames), told)
    for slot in range(out_ref.shape[0]):
        out_ref[slot, out_ref.shape[1] - 8 :] = told.astype(F32)


def other_gram_kernel(
    part,
    frames,
    reads_ref,
    source_ref,
    target_ref,
    out_ref,
    own_held_ref,
    own_goal_ref,
    held_ref,
    goal_ref,
    turned_ref,
    read_ref,
    sem,
    read_sem,
):
    core = lax.rem(lax.axis_index("frame"), 2)
    each = out_ref.shape[0]
    copies = []
    for slot in range(2 * each):
        own, place = slot // each, slot % each
        segment = 2 * place + (core if own else 1 - core)
        held = (own_held_ref if own else held_ref).at[place]
        goal = (own_goal_ref if own else goal_ref).at[place]
        copies.append(
            (
                pltpu.make_async_copy(source_ref.at[segment], held, sem.at[0, slot]),
                pltpu.make_async_copy(target_ref.at[segment], goal, sem.at[1, slot]),
            )
        )
    for pair in copies:
        for copy in pair:
            copy.start()
    listing = pltpu.make_async_copy(reads_ref, read_ref, read_sem)
    listing.start()
    gram_sums(part, ((0, 1), (2, 3)), held_ref, goal_ref, turned_ref, out_ref, copies)
    listing.wait()
    tell(frames, read_ref, out_ref)
    for pair in copies[each:]:
        for copy in pair:
            copy.wait()


def own_gram_kernel(part, frames, reads_ref, held_ref, goal_ref, out_ref, turned_ref, read_ref, read_sem):
    listing = pltpu.make_async_copy(reads_ref, read_ref, read_sem)
    listing.start()
    slots = tuple(range(out_ref.shape[0]))
    gram_sums(part, (slots,), held_ref, goal_ref, turned_ref, out_ref, [() for _ in slots])
    listing.wait()
    tell(frames, read_ref, out_ref)


def sum_kernel(gram_rows, partial_ref, spread_ref, rhs_ref, told_ref):
    rows = gram_rows + rhs_ref.shape[0]
    total = partial_ref[0, :rows]
    for chip in range(1, partial_ref.shape[0]):
        total = total + partial_ref[chip, :rows]
    for copy in range(spread_ref.shape[0]):
        spread_ref[copy] = total[:gram_rows]
    rhs_ref[...] = total[gram_rows:]
    for chip in range(partial_ref.shape[0]):
        told_ref[2 * chip : 2 * chip + 2] = partial_ref[chip, rows : rows + 2].astype(jnp.int32)


def solve_kernel(part, gram_ref, rhs_ref, out_ref, real_ref, imag_ref, sol_ref):
    width = 4 * part
    half = part // 2
    coils = rhs_ref.shape[0] // 3
    pieces = []
    for coil in range(4):
        block = gram_ref[coil]
        tail = block[part:]
        pieces.append(
            jnp.concatenate(
                [block[:part], jnp.concatenate([tail[:, :64], tail[:, 64:]], axis=0)], axis=1
            )
        )
    packed = jnp.concatenate(pieces, axis=0)
    flipped = packed.T
    down = lax.broadcasted_iota(jnp.int32, (width, width), 0)
    across = lax.broadcasted_iota(jnp.int32, (width, width), 1)
    diagonal = jnp.where(across == down, packed, 0.0)
    shift = regular / width * jnp.sum(diagonal)
    high = jnp.sqrt(jnp.sum(2.0 * (packed * packed) - diagonal * diagonal)) + shift
    scale = 2.0 / (high + shift)
    real = jnp.where(across <= down, packed, flipped)
    imag = jnp.where(across < down, -flipped, packed)
    real_ref[...] = (real + jnp.where(across == down, shift, 0.0)) * scale
    imag_ref[...] = jnp.where(across == down, 0.0, imag) * scale
    rhs_real = jnp.concatenate([rhs_ref[:coils], rhs_ref[2 * coils :, :64]], axis=1)
    rhs_imag = jnp.concatenate([rhs_ref[coils : 2 * coils], rhs_ref[2 * coils :, 64:]], axis=1)
    sol_ref[...] = jnp.concatenate([rhs_real, rhs_imag], axis=0) * scale

    def step(product, spread):
        square = spread * spread
        factor = 2.0 / (2.0 - square)
        real, imag, sol = real_ref[...], imag_ref[...], sol_ref[...]
        first = product(jnp.concatenate([real, sol], axis=0), imag)
        second = product(jnp.concatenate([real - imag, sol], axis=0), real + imag)
        cross, thin = first[:width], first[width:]
        turned = cross.T
        by_real = second[width:] - thin
        change = jnp.concatenate(
            [by_real[:coils] + thin[coils:], by_real[coils:] - thin[:coils]], axis=0
        )
        sol_ref[...] = factor * (2.0 * sol - change)
        real_ref[...] = factor * (2.0 * real - (second[:width] - cross - turned))
        imag_ref[...] = factor * (2.0 * imag - (cross - turned))
        return square / (2.0 - square)

    spread = (high - shift) / (high + shift)
    spread = lax.while_loop(
        lambda spread: spread > 0.97, functools.partial(step, fine_product), spread
    )
    spread = lax.while_loop(
        lambda spread: spread > settled, functools.partial(step, product), spread
    )
    sol = sol_ref[...]
    total = sol
    for _ in range(2):
        by_real = product(total, real_ref[...])
        by_imag = product(total, imag_ref[...])
        change = jnp.concatenate(
            [by_real[:coils] + by_imag[coils:], by_real[coils:] - by_imag[:coils]], axis=0
        )
        total = sol + (total - change)
    sol = total
    weights = jnp.concatenate([sol[:coils], sol[coils:]], axis=1).astype(BF16)
    for copy in range(out_ref.shape[0]):
        out_ref[copy] = weights


def select_kernel(told_ref, piece_ref, out_ref):
    pieces = [piece_ref[place].astype(F32) for place in range(piece_ref.shape[0])]
    for frame in range(out_ref.shape[0]):
        for slot in range(out_ref.shape[1]):
            wanted = jnp.broadcast_to(told_ref[frame : frame + 1, slot : slot + 1], pieces[0].shape)
            chosen = pieces[0]
            for place in range(1, len(pieces)):
                chosen = jnp.where(wanted == place, pieces[place], chosen)
            out_ref[frame, slot] = chosen.astype(BF16)


def fill_kernel(reads_ref, places_ref, weights_ref, source_ref, interp_ref, out_ref):
    frames, slots, coils, depth = weights_ref.shape
    width = depth // 2
    terms = []
    for slot in range(slots):
        holder = jnp.broadcast_to(reads_ref[:, slot : slot + 1] & (frames - 1), (coils, depth))
        chosen = weights_ref[0, slot].astype(F32)
        for frame in range(1, frames):
            chosen = jnp.where(holder == frame, weights_ref[frame, slot].astype(F32), chosen)
        real, imag = chosen[:, :width], chosen[:, width:]
        matrix = jnp.concatenate(
            [jnp.concatenate([real, -imag], axis=1), jnp.concatenate([imag, real], axis=1)], axis=0
        ).astype(BF16)
        filled = across_rows(matrix, source_ref[0, slot]).astype(BF16)
        terms.append(across_rows(filled, interp_ref[0, slot]))
    shape = terms[0].shape
    places = [jnp.broadcast_to(places_ref[:, slot : slot + 1], shape) for slot in range(slots)]
    for block in range(out_ref.shape[0]):
        total = jnp.zeros(shape, F32)
        for place, term in zip(places, terms):
            total = total + jnp.where(place == block, term, 0.0)
        out_ref[block] = total.astype(BF16)


def on_device(cal_source, cal_target, app_source, readers, blocks, interp):
    frames = lax.axis_size("frame")
    segs = lax.axis_size("seg")
    coil_count = lax.axis_size("coil")
    held, samples, depth = cal_source.shape
    coils = cal_target.shape[1]
    width = depth // 2
    part = width // coil_count
    gram_rows = part + part // 2
    rows = gram_rows + 3 * coils + 8
    slots = readers.shape[1]
    cells = interp.shape[2]

    each = held // 2
    block = jax.ShapeDtypeStruct((each, rows, LANES), F32)
    listed = pltpu.with_memory_space_constraint(readers, pltpu.HBM)
    hbm = pl.BlockSpec(memory_space=pltpu.HBM)
    vmem = pl.BlockSpec(memory_space=pltpu.VMEM)
    reading = [pltpu.SMEM(readers.shape, jnp.int32)]
    turned = pltpu.VMEM((each, depth, samples), BF16)
    cost = pl.CostEstimate(
        flops=2 * each * samples * depth * 2 * (part + coils),
        bytes_accessed=2 * each * samples * (depth + 2 * coils),
        transcendentals=0,
    )
    send, own_held, own_goal = pl.pallas_call(
        functools.partial(other_gram_kernel, part, frames),
        in_specs=[hbm, hbm, hbm],
        out_shape=[
            block,
            jax.ShapeDtypeStruct((each, samples, depth), BF16),
            jax.ShapeDtypeStruct((each, coils, 2, samples), BF16),
        ],
        scratch_shapes=[
            pltpu.VMEM((each, samples, depth), BF16),
            pltpu.VMEM((each, coils, 2, samples), BF16),
            turned,
            *reading,
            pltpu.SemaphoreType.DMA((2, held)),
            pltpu.SemaphoreType.DMA,
        ],
        compiler_params=SMALL,
        cost_estimate=cost,
    )(
        listed,
        pltpu.with_memory_space_constraint(cal_source, pltpu.HBM),
        pltpu.with_memory_space_constraint(cal_target, pltpu.HBM),
    )
    keep = pl.pallas_call(
        functools.partial(own_gram_kernel, part, frames),
        in_specs=[hbm, vmem, vmem],
        out_shape=block,
        scratch_shapes=[turned, *reading, pltpu.SemaphoreType.DMA],
        compiler_params=SMALL,
        cost_estimate=cost,
    )(listed, own_held, own_goal)
    other = lax.ppermute(send, "frame", [(frame, frame ^ 1) for frame in range(frames)])
    chips = [[2 * chip + core for chip in range(frames // 2)] for core in range(2)]
    received = lax.all_to_all(
        keep + other, "frame", 0, 0, tiled=True, axis_index_groups=chips
    )
    spread, rhs, told = pl.pallas_call(
        functools.partial(sum_kernel, gram_rows),
        out_shape=[
            jax.ShapeDtypeStruct((coil_count, gram_rows, LANES), F32),
            jax.ShapeDtypeStruct((3 * coils, LANES), F32),
            jax.ShapeDtypeStruct((frames, LANES), jnp.int32),
        ],
        compiler_params=SMALL,
    )(received)
    gram = lax.all_to_all(spread, "coil", 0, 0, tiled=True)
    weights = pl.pallas_call(
        functools.partial(solve_kernel, part),
        out_shape=jax.ShapeDtypeStruct((segs, coils, depth), BF16),
        scratch_shapes=[
            pltpu.VMEM((width, width), F32),
            pltpu.VMEM((width, width), F32),
            pltpu.VMEM((2 * coils, width), F32),
        ],
        compiler_params=SMALL,
    )(gram, rhs)
    pieces = lax.all_to_all(weights, "seg", 0, 0, tiled=True)
    sent = pl.pallas_call(
        select_kernel,
        out_shape=jax.ShapeDtypeStruct((frames, slots, coils, depth), BF16),
        compiler_params=SMALL,
    )(told, pieces)
    chosen = lax.all_to_all(sent, "frame", 0, 0, tiled=True)
    grid = pl.pallas_call(
        fill_kernel,
        out_shape=jax.ShapeDtypeStruct((segs, 2 * coils, cells), BF16),
        compiler_params=SMALL,
    )(readers, blocks, chosen, app_source, interp)
    terms = lax.all_to_all(grid, "seg", 0, 0, tiled=True)
    total = jnp.sum(terms.astype(F32), axis=0)
    power = lax.all_gather(jnp.sum(total * total, axis=0, keepdims=True), "coil", tiled=True)
    return jnp.sqrt(jnp.sum(power, axis=0, keepdims=True) + epsilon)


def solution(mesh):
    placed = (
        P("seg", "frame", None),
        P("seg", "coil", None, "frame"),
        P("frame", "seg", None, None),
        P("frame", "seg"),
        P("frame", "seg"),
        P("frame", "seg", None, None),
    )
    return jax.shard_map(
        on_device, mesh=mesh, in_specs=placed, out_specs=P("frame", "seg"), check_vma=False
    )
```

```python
import functools

import jax
import jax.numpy as jnp
from jax import lax
from jax.experimental import pallas as pl
from jax.experimental.pallas import tpu as pltpu
from jax.sharding import PartitionSpec as P

regular = 0.02
epsilon = 1e-06
settled = 0.0125
F32 = jnp.float32
BF16 = jnp.bfloat16
LANES = 128
SMALL = pltpu.CompilerParams(vmem_limit_bytes=16 * 1024 * 1024)


def across_rows(left, right):
    return lax.dot_general(left, right, (((1,), (1,)), ((), ())), preferred_element_type=F32)


def pieces_of(value, count):
    out = []
    for _ in range(count):
        piece = value.astype(BF16)
        value = value - piece.astype(F32)
        out.append(piece)
    return out


def product(left, right):
    rows = left.shape[0]
    a, b = pieces_of(left, 2), pieces_of(right, 2)
    dot = functools.partial(jnp.dot, preferred_element_type=F32)
    first = dot(jnp.concatenate(a, axis=0), b[0])
    return first[:rows] + (first[rows:] + dot(a[0], b[1]))


def fine_product(left, right):
    rows = left.shape[0]
    a, b = pieces_of(left, 3), pieces_of(right, 3)
    dot = functools.partial(jnp.dot, preferred_element_type=F32)
    first = dot(jnp.concatenate(a, axis=0), b[0])
    second = dot(jnp.concatenate(a[:2], axis=0), b[1])
    return first[:rows] + (
        (first[rows : 2 * rows] + second[:rows])
        + (first[2 * rows :] + (second[rows:] + dot(a[0], b[2])))
    )


def gram_sums(part, groups, held_ref, goal_ref, turned_ref, out_ref, copies):
    coil = lax.axis_index("coil")
    depth = held_ref.shape[2]
    width = depth // 2
    half = part // 2
    base = part + half
    coils = goal_ref.shape[1]
    across = lax.broadcasted_iota(jnp.int32, (part, width), 1)
    down = lax.broadcasted_iota(jnp.int32, (part, width), 0) + coil * part
    first = pl.multiple_of(coil * part, 16)
    second = pl.multiple_of(width + coil * part, 16)
    for slots in groups:
        for slot in slots:
            for copy in copies[slot]:
                copy.wait()
        lefts = []
        for slot in slots:
            turned_ref[slot] = held_ref[slot].T
            lefts.append(
                jnp.concatenate(
                    [
                        turned_ref[slot, pl.ds(first, part)],
                        turned_ref[slot, pl.ds(second, part)],
                        goal_ref[slot, :, 0, :],
                        goal_ref[slot, :, 1, :],
                    ],
                    axis=0,
                )
            )
        products = [
            jnp.dot(left, held_ref[slot], preferred_element_type=F32)
            for left, slot in zip(lefts, slots)
        ]
        for slot, sums in zip(slots, products):
            out = out_ref.at[slot]
            top, bottom = sums[:part], sums[part : 2 * part]
            gram_real = top[:, :width] + bottom[:, width:]
            gram_imag = top[:, width:] - bottom[:, :width]
            packed = jnp.where(across <= down, gram_real, gram_imag)
            proj_real = sums[2 * part : 2 * part + coils]
            proj_imag = sums[2 * part + coils :]
            rhs_real = proj_real[:, :width] + proj_imag[:, width:]
            rhs_imag = proj_imag[:, :width] - proj_real[:, width:]
            out[:part] = packed[:, :LANES]
            out[part:base] = jnp.concatenate(
                [packed[:half, LANES:], packed[half:, LANES:]], axis=1
            )
            out[base : base + coils] = rhs_real[:, :LANES]
            out[base + coils : base + 2 * coils] = rhs_imag[:, :LANES]
            out[base + 2 * coils : base + 3 * coils] = jnp.concatenate(
                [rhs_real[:, LANES:], rhs_imag[:, LANES:]], axis=1
            )


def tell(frames, read_ref, out_ref):
    core = lax.rem(lax.axis_index("frame"), 2)
    row = lax.broadcasted_iota(jnp.int32, (8, LANES), 0)
    lane = lax.broadcasted_iota(jnp.int32, (8, LANES), 1)
    told = jnp.zeros((8, LANES), jnp.int32)
    for place in range(read_ref.shape[1]):
        told = jnp.where((row == core) & (lane == place), lax.div(read_ref[0, place], frames), told)
    for slot in range(out_ref.shape[0]):
        out_ref[slot, out_ref.shape[1] - 8 :] = told.astype(F32)


def other_gram_kernel(
    part,
    frames,
    reads_ref,
    source_ref,
    target_ref,
    out_ref,
    own_held_ref,
    own_goal_ref,
    held_ref,
    goal_ref,
    turned_ref,
    read_ref,
    sem,
    read_sem,
):
    core = lax.rem(lax.axis_index("frame"), 2)
    each = out_ref.shape[0]
    copies = []
    for slot in range(2 * each):
        own, place = slot // each, slot % each
        segment = 2 * place + (core if own else 1 - core)
        held = (own_held_ref if own else held_ref).at[place]
        goal = (own_goal_ref if own else goal_ref).at[place]
        copies.append(
            (
                pltpu.make_async_copy(source_ref.at[segment], held, sem.at[0, slot]),
                pltpu.make_async_copy(target_ref.at[segment], goal, sem.at[1, slot]),
            )
        )
    for pair in copies:
        for copy in pair:
            copy.start()
    listing = pltpu.make_async_copy(reads_ref, read_ref, read_sem)
    listing.start()
    gram_sums(part, ((0, 1), (2, 3)), held_ref, goal_ref, turned_ref, out_ref, copies)
    listing.wait()
    tell(frames, read_ref, out_ref)
    for pair in copies[each:]:
        for copy in pair:
            copy.wait()


def own_gram_kernel(part, frames, reads_ref, held_ref, goal_ref, out_ref, turned_ref, read_ref, read_sem):
    listing = pltpu.make_async_copy(reads_ref, read_ref, read_sem)
    listing.start()
    slots = tuple(range(out_ref.shape[0]))
    gram_sums(part, (slots,), held_ref, goal_ref, turned_ref, out_ref, [() for _ in slots])
    listing.wait()
    tell(frames, read_ref, out_ref)


def sum_kernel(gram_rows, partial_ref, spread_ref, rhs_ref, told_ref):
    rows = gram_rows + rhs_ref.shape[0]
    total = partial_ref[0, :rows]
    for chip in range(1, partial_ref.shape[0]):
        total = total + partial_ref[chip, :rows]
    for copy in range(spread_ref.shape[0]):
        spread_ref[copy] = total[:gram_rows]
    rhs_ref[...] = total[gram_rows:]
    for chip in range(partial_ref.shape[0]):
        told_ref[2 * chip : 2 * chip + 2] = partial_ref[chip, rows : rows + 2].astype(jnp.int32)


def solve_kernel(part, gram_ref, rhs_ref, out_ref, real_ref, imag_ref, sol_ref):
    width = 4 * part
    half = part // 2
    coils = rhs_ref.shape[0] // 3
    pieces = []
    for coil in range(4):
        block = gram_ref[coil]
        tail = block[part:]
        pieces.append(
            jnp.concatenate(
                [block[:part], jnp.concatenate([tail[:, :64], tail[:, 64:]], axis=0)], axis=1
            )
        )
    packed = jnp.concatenate(pieces, axis=0)
    flipped = packed.T
    down = lax.broadcasted_iota(jnp.int32, (width, width), 0)
    across = lax.broadcasted_iota(jnp.int32, (width, width), 1)
    diagonal = jnp.where(across == down, packed, 0.0)
    shift = regular / width * jnp.sum(diagonal)
    high = jnp.sqrt(jnp.sum(2.0 * (packed * packed) - diagonal * diagonal)) + shift
    scale = 2.0 / (high + shift)
    real = jnp.where(across <= down, packed, flipped)
    imag = jnp.where(across < down, -flipped, packed)
    real_ref[...] = (real + jnp.where(across == down, shift, 0.0)) * scale
    imag_ref[...] = jnp.where(across == down, 0.0, imag) * scale
    rhs_real = jnp.concatenate([rhs_ref[:coils], rhs_ref[2 * coils :, :64]], axis=1)
    rhs_imag = jnp.concatenate([rhs_ref[coils : 2 * coils], rhs_ref[2 * coils :, 64:]], axis=1)
    sol_ref[...] = jnp.concatenate([rhs_real, rhs_imag], axis=0) * scale

    def step(product, spread):
        square = spread * spread
        factor = 2.0 / (2.0 - square)
        real, imag, sol = real_ref[...], imag_ref[...], sol_ref[...]
        first = product(jnp.concatenate([real, sol], axis=0), imag)
        second = product(jnp.concatenate([real - imag, sol], axis=0), real + imag)
        cross, thin = first[:width], first[width:]
        turned = cross.T
        by_real = second[width:] - thin
        change = jnp.concatenate(
            [by_real[:coils] + thin[coils:], by_real[coils:] - thin[:coils]], axis=0
        )
        sol_ref[...] = factor * (2.0 * sol - change)
        real_ref[...] = factor * (2.0 * real - (second[:width] - cross - turned))
        imag_ref[...] = factor * (2.0 * imag - (cross - turned))
        return square / (2.0 - square)

    spread = (high - shift) / (high + shift)
    spread = lax.while_loop(
        lambda spread: spread > 0.97, functools.partial(step, fine_product), spread
    )
    spread = lax.while_loop(
        lambda spread: spread > settled, functools.partial(step, product), spread
    )
    sol = sol_ref[...]
    total = sol
    for _ in range(2):
        by_real = product(total, real_ref[...])
        by_imag = product(total, imag_ref[...])
        change = jnp.concatenate(
            [by_real[:coils] + by_imag[coils:], by_real[coils:] - by_imag[:coils]], axis=0
        )
        total = sol + (total - change)
    sol = total
    weights = jnp.concatenate([sol[:coils], sol[coils:]], axis=1).astype(BF16)
    for copy in range(out_ref.shape[0]):
        out_ref[copy] = weights


def select_kernel(told_ref, piece_ref, out_ref):
    pieces = [piece_ref[place].astype(F32) for place in range(piece_ref.shape[0])]
    for frame in range(out_ref.shape[0]):
        for slot in range(out_ref.shape[1]):
            wanted = jnp.broadcast_to(told_ref[frame : frame + 1, slot : slot + 1], pieces[0].shape)
            chosen = pieces[0]
            for place in range(1, len(pieces)):
                chosen = jnp.where(wanted == place, pieces[place], chosen)
            out_ref[frame, slot] = chosen.astype(BF16)


def fill_kernel(reads_ref, places_ref, weights_ref, source_ref, interp_ref, out_ref):
    frames, slots, coils, depth = weights_ref.shape
    width = depth // 2
    terms = []
    for slot in range(slots):
        holder = jnp.broadcast_to(reads_ref[:, slot : slot + 1] & (frames - 1), (coils, depth))
        chosen = weights_ref[0, slot].astype(F32)
        for frame in range(1, frames):
            chosen = jnp.where(holder == frame, weights_ref[frame, slot].astype(F32), chosen)
        real, imag = chosen[:, :width], chosen[:, width:]
        matrix = jnp.concatenate(
            [jnp.concatenate([real, -imag], axis=1), jnp.concatenate([imag, real], axis=1)], axis=0
        ).astype(BF16)
        filled = across_rows(matrix, source_ref[0, slot]).astype(BF16)
        terms.append(across_rows(filled, interp_ref[0, slot]))
    shape = terms[0].shape
    places = [jnp.broadcast_to(places_ref[:, slot : slot + 1], shape) for slot in range(slots)]
    for block in range(out_ref.shape[0]):
        total = jnp.zeros(shape, F32)
        for place, term in zip(places, terms):
            total = total + jnp.where(place == block, term, 0.0)
        out_ref[block] = total.astype(BF16)


def near_kernel(coil_count, terms_ref, out_ref):
    blocks = out_ref.shape[0] // coil_count
    for block in range(blocks):
        total = terms_ref[block].astype(F32)
        for run in range(1, terms_ref.shape[0] // blocks):
            total = total + terms_ref[run * blocks + block].astype(F32)
        for coil in range(coil_count):
            out_ref[block * coil_count + coil] = total.astype(BF16)


def root_kernel(coil_count, terms_ref, out_ref):
    power = None
    for coil in range(coil_count):
        total = terms_ref[coil].astype(F32)
        for place in range(1, terms_ref.shape[0] // coil_count):
            total = total + terms_ref[place * coil_count + coil].astype(F32)
        power = total * total if power is None else power + total * total
    out_ref[...] = jnp.sqrt(jnp.sum(power, axis=0, keepdims=True) + epsilon)


def on_device(cal_source, cal_target, app_source, readers, blocks, interp):
    frames = lax.axis_size("frame")
    segs = lax.axis_size("seg")
    coil_count = lax.axis_size("coil")
    held, samples, depth = cal_source.shape
    coils = cal_target.shape[1]
    width = depth // 2
    part = width // coil_count
    gram_rows = part + part // 2
    rows = gram_rows + 3 * coils + 8
    slots = readers.shape[1]
    cells = interp.shape[2]

    each = held // 2
    block = jax.ShapeDtypeStruct((each, rows, LANES), F32)
    listed = pltpu.with_memory_space_constraint(readers, pltpu.HBM)
    hbm = pl.BlockSpec(memory_space=pltpu.HBM)
    vmem = pl.BlockSpec(memory_space=pltpu.VMEM)
    reading = [pltpu.SMEM(readers.shape, jnp.int32)]
    turned = pltpu.VMEM((each, depth, samples), BF16)
    cost = pl.CostEstimate(
        flops=2 * each * samples * depth * 2 * (part + coils),
        bytes_accessed=2 * each * samples * (depth + 2 * coils),
        transcendentals=0,
    )
    send, own_held, own_goal = pl.pallas_call(
        functools.partial(other_gram_kernel, part, frames),
        in_specs=[hbm, hbm, hbm],
        out_shape=[
            block,
            jax.ShapeDtypeStruct((each, samples, depth), BF16),
            jax.ShapeDtypeStruct((each, coils, 2, samples), BF16),
        ],
        scratch_shapes=[
            pltpu.VMEM((each, samples, depth), BF16),
            pltpu.VMEM((each, coils, 2, samples), BF16),
            turned,
            *reading,
            pltpu.SemaphoreType.DMA((2, held)),
            pltpu.SemaphoreType.DMA,
        ],
        compiler_params=SMALL,
        cost_estimate=cost,
    )(
        listed,
        pltpu.with_memory_space_constraint(cal_source, pltpu.HBM),
        pltpu.with_memory_space_constraint(cal_target, pltpu.HBM),
    )
    keep = pl.pallas_call(
        functools.partial(own_gram_kernel, part, frames),
        in_specs=[hbm, vmem, vmem],
        out_shape=block,
        scratch_shapes=[turned, *reading, pltpu.SemaphoreType.DMA],
        compiler_params=SMALL,
        cost_estimate=cost,
    )(listed, own_held, own_goal)
    other = lax.ppermute(send, "frame", [(frame, frame ^ 1) for frame in range(frames)])
    chips = [[2 * chip + core for chip in range(frames // 2)] for core in range(2)]
    received = lax.all_to_all(
        keep + other, "frame", 0, 0, tiled=True, axis_index_groups=chips
    )
    spread, rhs, told = pl.pallas_call(
        functools.partial(sum_kernel, gram_rows),
        out_shape=[
            jax.ShapeDtypeStruct((coil_count, gram_rows, LANES), F32),
            jax.ShapeDtypeStruct((3 * coils, LANES), F32),
            jax.ShapeDtypeStruct((frames, LANES), jnp.int32),
        ],
        compiler_params=SMALL,
    )(received)
    gram = lax.all_to_all(spread, "coil", 0, 0, tiled=True)
    weights = pl.pallas_call(
        functools.partial(solve_kernel, part),
        out_shape=jax.ShapeDtypeStruct((segs, coils, depth), BF16),
        scratch_shapes=[
            pltpu.VMEM((width, width), F32),
            pltpu.VMEM((width, width), F32),
            pltpu.VMEM((2 * coils, width), F32),
        ],
        compiler_params=SMALL,
    )(gram, rhs)
    pieces = lax.all_to_all(weights, "seg", 0, 0, tiled=True)
    sent = pl.pallas_call(
        select_kernel,
        out_shape=jax.ShapeDtypeStruct((frames, slots, coils, depth), BF16),
        compiler_params=SMALL,
    )(told, pieces)
    chosen = lax.all_to_all(sent, "frame", 0, 0, tiled=True)
    grid = pl.pallas_call(
        fill_kernel,
        out_shape=jax.ShapeDtypeStruct((segs, 2 * coils, cells), BF16),
        compiler_params=SMALL,
    )(readers, blocks, chosen, app_source, interp)
    columns = segs // 4
    far = [[column + 4 * run for run in range(columns)] for column in range(4)]
    terms = lax.all_to_all(grid, "seg", 0, 0, tiled=True, axis_index_groups=far)
    spread = pl.pallas_call(
        functools.partial(near_kernel, coil_count),
        out_shape=jax.ShapeDtypeStruct((4 * coil_count, 2 * coils, cells), BF16),
        compiler_params=SMALL,
    )(terms)
    near = [
        [run * 4 * coil_count + member for member in range(4 * coil_count)] for run in range(columns)
    ]
    terms = lax.all_to_all(spread, ("seg", "coil"), 0, 0, tiled=True, axis_index_groups=near)
    return pl.pallas_call(
        functools.partial(root_kernel, coil_count),
        out_shape=jax.ShapeDtypeStruct((1, cells), F32),
        compiler_params=SMALL,
    )(terms)


def solution(mesh):
    placed = (
        P("seg", "frame", None),
        P("seg", "coil", None, "frame"),
        P("frame", "seg", None, None),
        P("frame", "seg"),
        P("frame", "seg"),
        P("frame", "seg", None, None),
    )
    return jax.shard_map(
        on_device, mesh=mesh, in_specs=placed, out_specs=P("frame", "seg"), check_vma=False
    )
```

```python
import functools

import jax
import jax.numpy as jnp
from jax import lax
from jax.experimental import pallas as pl
from jax.experimental.pallas import tpu as pltpu
from jax.sharding import PartitionSpec as P

regular = 0.02
epsilon = 1e-06
settled = 0.0125
F32 = jnp.float32
BF16 = jnp.bfloat16
LANES = 128
SMALL = pltpu.CompilerParams(vmem_limit_bytes=16 * 1024 * 1024)


def across_rows(left, right):
    return lax.dot_general(left, right, (((1,), (1,)), ((), ())), preferred_element_type=F32)


def pieces_of(value, count):
    out = []
    for _ in range(count):
        piece = value.astype(BF16)
        value = value - piece.astype(F32)
        out.append(piece)
    return out


def product(left, right):
    rows = left.shape[0]
    a, b = pieces_of(left, 2), pieces_of(right, 2)
    dot = functools.partial(jnp.dot, preferred_element_type=F32)
    first = dot(jnp.concatenate(a, axis=0), b[0])
    return first[:rows] + (first[rows:] + dot(a[0], b[1]))


def fine_product(left, right):
    rows = left.shape[0]
    a, b = pieces_of(left, 3), pieces_of(right, 3)
    dot = functools.partial(jnp.dot, preferred_element_type=F32)
    first = dot(jnp.concatenate(a, axis=0), b[0])
    second = dot(jnp.concatenate(a[:2], axis=0), b[1])
    return first[:rows] + (
        (first[rows : 2 * rows] + second[:rows])
        + (first[2 * rows :] + (second[rows:] + dot(a[0], b[2])))
    )


def gram_sums(part, groups, held_ref, goal_ref, turned_ref, out_ref, copies):
    coil = lax.axis_index("coil")
    depth = held_ref.shape[2]
    width = depth // 2
    half = part // 2
    base = part + half
    coils = goal_ref.shape[1]
    across = lax.broadcasted_iota(jnp.int32, (part, width), 1)
    down = lax.broadcasted_iota(jnp.int32, (part, width), 0) + coil * part
    first = pl.multiple_of(coil * part, 16)
    second = pl.multiple_of(width + coil * part, 16)
    for slots in groups:
        for slot in slots:
            for copy in copies[slot]:
                copy.wait()
        lefts = []
        for slot in slots:
            turned_ref[slot] = held_ref[slot].T
            lefts.append(
                jnp.concatenate(
                    [
                        turned_ref[slot, pl.ds(first, part)],
                        turned_ref[slot, pl.ds(second, part)],
                        goal_ref[slot, :, 0, :],
                        goal_ref[slot, :, 1, :],
                    ],
                    axis=0,
                )
            )
        products = [
            jnp.dot(left, held_ref[slot], preferred_element_type=F32)
            for left, slot in zip(lefts, slots)
        ]
        for slot, sums in zip(slots, products):
            out = out_ref.at[slot]
            top, bottom = sums[:part], sums[part : 2 * part]
            gram_real = top[:, :width] + bottom[:, width:]
            gram_imag = top[:, width:] - bottom[:, :width]
            packed = jnp.where(across <= down, gram_real, gram_imag)
            proj_real = sums[2 * part : 2 * part + coils]
            proj_imag = sums[2 * part + coils :]
            rhs_real = proj_real[:, :width] + proj_imag[:, width:]
            rhs_imag = proj_imag[:, :width] - proj_real[:, width:]
            out[:part] = packed[:, :LANES]
            out[part:base] = jnp.concatenate(
                [packed[:half, LANES:], packed[half:, LANES:]], axis=1
            )
            out[base : base + coils] = rhs_real[:, :LANES]
            out[base + coils : base + 2 * coils] = rhs_imag[:, :LANES]
            out[base + 2 * coils : base + 3 * coils] = jnp.concatenate(
                [rhs_real[:, LANES:], rhs_imag[:, LANES:]], axis=1
            )


def tell(frames, read_ref, out_ref):
    core = lax.rem(lax.axis_index("frame"), 2)
    row = lax.broadcasted_iota(jnp.int32, (8, LANES), 0)
    lane = lax.broadcasted_iota(jnp.int32, (8, LANES), 1)
    told = jnp.zeros((8, LANES), jnp.int32)
    for place in range(read_ref.shape[1]):
        told = jnp.where((row == core) & (lane == place), lax.div(read_ref[0, place], frames), told)
    for slot in range(out_ref.shape[0]):
        out_ref[slot, out_ref.shape[1] - 8 :] = told.astype(F32)


def other_gram_kernel(
    part,
    frames,
    reads_ref,
    source_ref,
    target_ref,
    out_ref,
    own_held_ref,
    own_goal_ref,
    held_ref,
    goal_ref,
    turned_ref,
    read_ref,
    sem,
    read_sem,
):
    core = lax.rem(lax.axis_index("frame"), 2)
    each = out_ref.shape[0]
    copies = []
    for slot in range(2 * each):
        own, place = slot // each, slot % each
        segment = 2 * place + (core if own else 1 - core)
        held = (own_held_ref if own else held_ref).at[place]
        goal = (own_goal_ref if own else goal_ref).at[place]
        copies.append(
            (
                pltpu.make_async_copy(source_ref.at[segment], held, sem.at[0, slot]),
                pltpu.make_async_copy(target_ref.at[segment], goal, sem.at[1, slot]),
            )
        )
    for pair in copies:
        for copy in pair:
            copy.start()
    listing = pltpu.make_async_copy(reads_ref, read_ref, read_sem)
    listing.start()
    gram_sums(part, ((0,), (1, 2, 3)), held_ref, goal_ref, turned_ref, out_ref, copies)
    listing.wait()
    tell(frames, read_ref, out_ref)
    for pair in copies[each:]:
        for copy in pair:
            copy.wait()


def own_gram_kernel(part, frames, reads_ref, held_ref, goal_ref, out_ref, turned_ref, read_ref, read_sem):
    listing = pltpu.make_async_copy(reads_ref, read_ref, read_sem)
    listing.start()
    slots = tuple(range(out_ref.shape[0]))
    gram_sums(part, (slots,), held_ref, goal_ref, turned_ref, out_ref, [() for _ in slots])
    listing.wait()
    tell(frames, read_ref, out_ref)


def sum_kernel(gram_rows, partial_ref, spread_ref, rhs_ref, told_ref):
    rows = gram_rows + rhs_ref.shape[0]
    total = partial_ref[0, :rows]
    for chip in range(1, partial_ref.shape[0]):
        total = total + partial_ref[chip, :rows]
    for copy in range(spread_ref.shape[0]):
        spread_ref[copy] = total[:gram_rows]
    rhs_ref[...] = total[gram_rows:]
    for chip in range(partial_ref.shape[0]):
        told_ref[2 * chip : 2 * chip + 2] = partial_ref[chip, rows : rows + 2].astype(jnp.int32)


def solve_kernel(part, gram_ref, rhs_ref, out_ref, real_ref, imag_ref, sol_ref):
    width = 4 * part
    half = part // 2
    coils = rhs_ref.shape[0] // 3
    pieces = []
    for coil in range(4):
        block = gram_ref[coil]
        tail = block[part:]
        pieces.append(
            jnp.concatenate(
                [block[:part], jnp.concatenate([tail[:, :64], tail[:, 64:]], axis=0)], axis=1
            )
        )
    packed = jnp.concatenate(pieces, axis=0)
    flipped = packed.T
    down = lax.broadcasted_iota(jnp.int32, (width, width), 0)
    across = lax.broadcasted_iota(jnp.int32, (width, width), 1)
    diagonal = jnp.where(across == down, packed, 0.0)
    shift = regular / width * jnp.sum(diagonal)
    high = jnp.sqrt(jnp.sum(2.0 * (packed * packed) - diagonal * diagonal)) + shift
    scale = 2.0 / (high + shift)
    real = jnp.where(across <= down, packed, flipped)
    imag = jnp.where(across < down, -flipped, packed)
    real_ref[...] = (real + jnp.where(across == down, shift, 0.0)) * scale
    imag_ref[...] = jnp.where(across == down, 0.0, imag) * scale
    rhs_real = jnp.concatenate([rhs_ref[:coils], rhs_ref[2 * coils :, :64]], axis=1)
    rhs_imag = jnp.concatenate([rhs_ref[coils : 2 * coils], rhs_ref[2 * coils :, 64:]], axis=1)
    sol_ref[...] = jnp.concatenate([rhs_real, rhs_imag], axis=0) * scale

    def step(product, spread):
        square = spread * spread
        factor = 2.0 / (2.0 - square)
        real, imag, sol = real_ref[...], imag_ref[...], sol_ref[...]
        first = product(jnp.concatenate([real, sol], axis=0), imag)
        second = product(jnp.concatenate([real - imag, sol], axis=0), real + imag)
        cross, thin = first[:width], first[width:]
        turned = cross.T
        by_real = second[width:] - thin
        change = jnp.concatenate(
            [by_real[:coils] + thin[coils:], by_real[coils:] - thin[:coils]], axis=0
        )
        sol_ref[...] = factor * (2.0 * sol - change)
        real_ref[...] = factor * (2.0 * real - (second[:width] - cross - turned))
        imag_ref[...] = factor * (2.0 * imag - (cross - turned))
        return square / (2.0 - square)

    spread = (high - shift) / (high + shift)
    spread = lax.while_loop(
        lambda spread: spread > 0.99, functools.partial(step, fine_product), spread
    )
    spread = lax.while_loop(
        lambda spread: spread > settled, functools.partial(step, product), spread
    )
    sol = sol_ref[...]
    total = sol
    for _ in range(2):
        by_real = product(total, real_ref[...])
        by_imag = product(total, imag_ref[...])
        change = jnp.concatenate(
            [by_real[:coils] + by_imag[coils:], by_real[coils:] - by_imag[:coils]], axis=0
        )
        total = sol + (total - change)
    sol = total
    weights = jnp.concatenate([sol[:coils], sol[coils:]], axis=1).astype(BF16)
    for copy in range(out_ref.shape[0]):
        out_ref[copy] = weights


def select_kernel(told_ref, piece_ref, out_ref):
    pieces = [piece_ref[place].astype(F32) for place in range(piece_ref.shape[0])]
    for frame in range(out_ref.shape[0]):
        for slot in range(out_ref.shape[1]):
            wanted = jnp.broadcast_to(told_ref[frame : frame + 1, slot : slot + 1], pieces[0].shape)
            chosen = pieces[0]
            for place in range(1, len(pieces)):
                chosen = jnp.where(wanted == place, pieces[place], chosen)
            out_ref[frame, slot] = chosen.astype(BF16)


def fill_kernel(reads_ref, places_ref, weights_ref, source_ref, interp_ref, out_ref):
    frames, slots, coils, depth = weights_ref.shape
    width = depth // 2
    terms = []
    for slot in range(slots):
        holder = jnp.broadcast_to(reads_ref[:, slot : slot + 1] & (frames - 1), (coils, depth))
        chosen = weights_ref[0, slot].astype(F32)
        for frame in range(1, frames):
            chosen = jnp.where(holder == frame, weights_ref[frame, slot].astype(F32), chosen)
        real, imag = chosen[:, :width], chosen[:, width:]
        matrix = jnp.concatenate(
            [jnp.concatenate([real, -imag], axis=1), jnp.concatenate([imag, real], axis=1)], axis=0
        ).astype(BF16)
        filled = across_rows(matrix, source_ref[0, slot]).astype(BF16)
        terms.append(across_rows(filled, interp_ref[0, slot]))
    shape = terms[0].shape
    places = [jnp.broadcast_to(places_ref[:, slot : slot + 1], shape) for slot in range(slots)]
    for block in range(out_ref.shape[0]):
        total = jnp.zeros(shape, F32)
        for place, term in zip(places, terms):
            total = total + jnp.where(place == block, term, 0.0)
        out_ref[block] = total.astype(BF16)


def on_device(cal_source, cal_target, app_source, readers, blocks, interp):
    frames = lax.axis_size("frame")
    segs = lax.axis_size("seg")
    coil_count = lax.axis_size("coil")
    held, samples, depth = cal_source.shape
    coils = cal_target.shape[1]
    width = depth // 2
    part = width // coil_count
    gram_rows = part + part // 2
    rows = gram_rows + 3 * coils + 8
    slots = readers.shape[1]
    cells = interp.shape[2]

    each = held // 2
    block = jax.ShapeDtypeStruct((each, rows, LANES), F32)
    listed = pltpu.with_memory_space_constraint(readers, pltpu.HBM)
    hbm = pl.BlockSpec(memory_space=pltpu.HBM)
    vmem = pl.BlockSpec(memory_space=pltpu.VMEM)
    reading = [pltpu.SMEM(readers.shape, jnp.int32)]
    turned = pltpu.VMEM((each, depth, samples), BF16)
    cost = pl.CostEstimate(
        flops=2 * each * samples * depth * 2 * (part + coils),
        bytes_accessed=2 * each * samples * (depth + 2 * coils),
        transcendentals=0,
    )
    send, own_held, own_goal = pl.pallas_call(
        functools.partial(other_gram_kernel, part, frames),
        in_specs=[hbm, hbm, hbm],
        out_shape=[
            block,
            jax.ShapeDtypeStruct((each, samples, depth), BF16),
            jax.ShapeDtypeStruct((each, coils, 2, samples), BF16),
        ],
        scratch_shapes=[
            pltpu.VMEM((each, samples, depth), BF16),
            pltpu.VMEM((each, coils, 2, samples), BF16),
            turned,
            *reading,
            pltpu.SemaphoreType.DMA((2, held)),
            pltpu.SemaphoreType.DMA,
        ],
        compiler_params=SMALL,
        cost_estimate=cost,
    )(
        listed,
        pltpu.with_memory_space_constraint(cal_source, pltpu.HBM),
        pltpu.with_memory_space_constraint(cal_target, pltpu.HBM),
    )
    keep = pl.pallas_call(
        functools.partial(own_gram_kernel, part, frames),
        in_specs=[hbm, vmem, vmem],
        out_shape=block,
        scratch_shapes=[turned, *reading, pltpu.SemaphoreType.DMA],
        compiler_params=SMALL,
        cost_estimate=cost,
    )(listed, own_held, own_goal)
    other = lax.ppermute(send, "frame", [(frame, frame ^ 1) for frame in range(frames)])
    chips = [[2 * chip + core for chip in range(frames // 2)] for core in range(2)]
    received = lax.all_to_all(
        keep + other, "frame", 0, 0, tiled=True, axis_index_groups=chips
    )
    spread, rhs, told = pl.pallas_call(
        functools.partial(sum_kernel, gram_rows),
        out_shape=[
            jax.ShapeDtypeStruct((coil_count, gram_rows, LANES), F32),
            jax.ShapeDtypeStruct((3 * coils, LANES), F32),
            jax.ShapeDtypeStruct((frames, LANES), jnp.int32),
        ],
        compiler_params=SMALL,
    )(received)
    gram = lax.all_to_all(spread, "coil", 0, 0, tiled=True)
    weights = pl.pallas_call(
        functools.partial(solve_kernel, part),
        out_shape=jax.ShapeDtypeStruct((segs, coils, depth), BF16),
        scratch_shapes=[
            pltpu.VMEM((width, width), F32),
            pltpu.VMEM((width, width), F32),
            pltpu.VMEM((2 * coils, width), F32),
        ],
        compiler_params=SMALL,
    )(gram, rhs)
    pieces = lax.all_to_all(weights, "seg", 0, 0, tiled=True)
    sent = pl.pallas_call(
        select_kernel,
        out_shape=jax.ShapeDtypeStruct((frames, slots, coils, depth), BF16),
        compiler_params=SMALL,
    )(told, pieces)
    chosen = lax.all_to_all(sent, "frame", 0, 0, tiled=True)
    grid = pl.pallas_call(
        fill_kernel,
        out_shape=jax.ShapeDtypeStruct((segs, 2 * coils, cells), BF16),
        compiler_params=SMALL,
    )(readers, blocks, chosen, app_source, interp)
    terms = lax.all_to_all(grid, "seg", 0, 0, tiled=True)
    total = jnp.sum(terms.astype(F32), axis=0)
    power = lax.all_gather(jnp.sum(total * total, axis=0, keepdims=True), "coil", tiled=True)
    return jnp.sqrt(jnp.sum(power, axis=0, keepdims=True) + epsilon)


def solution(mesh):
    placed = (
        P("seg", "frame", None),
        P("seg", "coil", None, "frame"),
        P("frame", "seg", None, None),
        P("frame", "seg"),
        P("frame", "seg"),
        P("frame", "seg", None, None),
    )
    return jax.shard_map(
        on_device, mesh=mesh, in_specs=placed, out_specs=P("frame", "seg"), check_vma=False
    )
```

```python
import functools

import jax
import jax.numpy as jnp
from jax import lax
from jax.experimental import pallas as pl
from jax.experimental.pallas import tpu as pltpu
from jax.sharding import PartitionSpec as P

regular = 0.02
epsilon = 1e-06
settled = 0.0125
F32 = jnp.float32
BF16 = jnp.bfloat16
LANES = 128
CHIPS = (0, 3, 1, 2)
FRAMES = (0, 2, 4, 6, 1, 3, 5, 7)
SMALL = pltpu.CompilerParams(vmem_limit_bytes=16 * 1024 * 1024)


def across_rows(left, right):
    return lax.dot_general(left, right, (((1,), (1,)), ((), ())), preferred_element_type=F32)


def pieces_of(value, count):
    out = []
    for _ in range(count):
        piece = value.astype(BF16)
        value = value - piece.astype(F32)
        out.append(piece)
    return out


def product(left, right):
    rows = left.shape[0]
    a, b = pieces_of(left, 2), pieces_of(right, 2)
    dot = functools.partial(jnp.dot, preferred_element_type=F32)
    first = dot(jnp.concatenate(a, axis=0), b[0])
    return first[:rows] + (first[rows:] + dot(a[0], b[1]))


def fine_product(left, right):
    rows = left.shape[0]
    a, b = pieces_of(left, 3), pieces_of(right, 3)
    dot = functools.partial(jnp.dot, preferred_element_type=F32)
    first = dot(jnp.concatenate(a, axis=0), b[0])
    second = dot(jnp.concatenate(a[:2], axis=0), b[1])
    return first[:rows] + (
        (first[rows : 2 * rows] + second[:rows])
        + (first[2 * rows :] + (second[rows:] + dot(a[0], b[2])))
    )


def gram_sums(part, groups, held_ref, goal_ref, turned_ref, out_ref, copies):
    coil = lax.axis_index("coil")
    depth = held_ref.shape[2]
    width = depth // 2
    half = part // 2
    base = part + half
    coils = goal_ref.shape[1]
    across = lax.broadcasted_iota(jnp.int32, (part, width), 1)
    down = lax.broadcasted_iota(jnp.int32, (part, width), 0) + coil * part
    first = pl.multiple_of(coil * part, 16)
    second = pl.multiple_of(width + coil * part, 16)
    for slots in groups:
        for slot in slots:
            for copy in copies[slot]:
                copy.wait()
        lefts = []
        for slot in slots:
            turned_ref[slot] = held_ref[slot].T
            lefts.append(
                jnp.concatenate(
                    [
                        turned_ref[slot, pl.ds(first, part)],
                        turned_ref[slot, pl.ds(second, part)],
                        goal_ref[slot, :, 0, :],
                        goal_ref[slot, :, 1, :],
                    ],
                    axis=0,
                )
            )
        products = [
            jnp.dot(left, held_ref[slot], preferred_element_type=F32)
            for left, slot in zip(lefts, slots)
        ]
        for slot, sums in zip(slots, products):
            out = out_ref.at[slot]
            top, bottom = sums[:part], sums[part : 2 * part]
            gram_real = top[:, :width] + bottom[:, width:]
            gram_imag = top[:, width:] - bottom[:, :width]
            packed = jnp.where(across <= down, gram_real, gram_imag)
            proj_real = sums[2 * part : 2 * part + coils]
            proj_imag = sums[2 * part + coils :]
            rhs_real = proj_real[:, :width] + proj_imag[:, width:]
            rhs_imag = proj_imag[:, :width] - proj_real[:, width:]
            out[:part] = packed[:, :LANES]
            out[part:base] = jnp.concatenate(
                [packed[:half, LANES:], packed[half:, LANES:]], axis=1
            )
            out[base : base + coils] = rhs_real[:, :LANES]
            out[base + coils : base + 2 * coils] = rhs_imag[:, :LANES]
            out[base + 2 * coils : base + 3 * coils] = jnp.concatenate(
                [rhs_real[:, LANES:], rhs_imag[:, LANES:]], axis=1
            )


def tell(frames, read_ref, out_ref):
    core = lax.rem(lax.axis_index("frame"), 2)
    row = lax.broadcasted_iota(jnp.int32, (8, LANES), 0)
    lane = lax.broadcasted_iota(jnp.int32, (8, LANES), 1)
    told = jnp.zeros((8, LANES), jnp.int32)
    for place in range(read_ref.shape[1]):
        told = jnp.where((row == core) & (lane == place), lax.div(read_ref[0, place], frames), told)
    for slot in range(out_ref.shape[0]):
        out_ref[slot, out_ref.shape[1] - 8 :] = told.astype(F32)


def other_gram_kernel(
    part,
    frames,
    reads_ref,
    source_ref,
    target_ref,
    out_ref,
    own_held_ref,
    own_goal_ref,
    held_ref,
    goal_ref,
    turned_ref,
    read_ref,
    sem,
    read_sem,
):
    core = lax.rem(lax.axis_index("frame"), 2)
    each = out_ref.shape[0]
    copies = []
    for slot in range(2 * each):
        own, place = slot // each, slot % each
        segment = 2 * CHIPS[place] + (core if own else 1 - core)
        held = (own_held_ref if own else held_ref).at[place]
        goal = (own_goal_ref if own else goal_ref).at[place]
        copies.append(
            (
                pltpu.make_async_copy(source_ref.at[segment], held, sem.at[0, slot]),
                pltpu.make_async_copy(target_ref.at[segment], goal, sem.at[1, slot]),
            )
        )
    for pair in copies:
        for copy in pair:
            copy.start()
    listing = pltpu.make_async_copy(reads_ref, read_ref, read_sem)
    listing.start()
    gram_sums(part, ((0,), (1, 2, 3)), held_ref, goal_ref, turned_ref, out_ref, copies)
    listing.wait()
    tell(frames, read_ref, out_ref)
    for pair in copies[each:]:
        for copy in pair:
            copy.wait()


def own_gram_kernel(part, frames, reads_ref, held_ref, goal_ref, out_ref, turned_ref, read_ref, read_sem):
    listing = pltpu.make_async_copy(reads_ref, read_ref, read_sem)
    listing.start()
    slots = tuple(range(out_ref.shape[0]))
    gram_sums(part, (slots,), held_ref, goal_ref, turned_ref, out_ref, [() for _ in slots])
    listing.wait()
    tell(frames, read_ref, out_ref)


def sum_kernel(gram_rows, partial_ref, spread_ref, rhs_ref, told_ref):
    rows = gram_rows + rhs_ref.shape[0]
    total = partial_ref[0, :rows]
    for chip in range(1, partial_ref.shape[0]):
        total = total + partial_ref[chip, :rows]
    for copy in range(spread_ref.shape[0]):
        spread_ref[copy] = total[:gram_rows]
    rhs_ref[...] = total[gram_rows:]
    for place, chip in enumerate(CHIPS):
        told_ref[2 * chip : 2 * chip + 2] = partial_ref[place, rows : rows + 2].astype(jnp.int32)


def solve_kernel(part, gram_ref, rhs_ref, out_ref, real_ref, imag_ref, sol_ref):
    width = 4 * part
    half = part // 2
    coils = rhs_ref.shape[0] // 3
    pieces = []
    for coil in range(4):
        block = gram_ref[coil]
        tail = block[part:]
        pieces.append(
            jnp.concatenate(
                [block[:part], jnp.concatenate([tail[:, :64], tail[:, 64:]], axis=0)], axis=1
            )
        )
    packed = jnp.concatenate(pieces, axis=0)
    flipped = packed.T
    down = lax.broadcasted_iota(jnp.int32, (width, width), 0)
    across = lax.broadcasted_iota(jnp.int32, (width, width), 1)
    diagonal = jnp.where(across == down, packed, 0.0)
    shift = regular / width * jnp.sum(diagonal)
    high = jnp.sqrt(jnp.sum(2.0 * (packed * packed) - diagonal * diagonal)) + shift
    scale = 2.0 / (high + shift)
    real = jnp.where(across <= down, packed, flipped)
    imag = jnp.where(across < down, -flipped, packed)
    real_ref[...] = (real + jnp.where(across == down, shift, 0.0)) * scale
    imag_ref[...] = jnp.where(across == down, 0.0, imag) * scale
    rhs_real = jnp.concatenate([rhs_ref[:coils], rhs_ref[2 * coils :, :64]], axis=1)
    rhs_imag = jnp.concatenate([rhs_ref[coils : 2 * coils], rhs_ref[2 * coils :, 64:]], axis=1)
    sol_ref[...] = jnp.concatenate([rhs_real, rhs_imag], axis=0) * scale

    def step(product, spread):
        square = spread * spread
        factor = 2.0 / (2.0 - square)
        real, imag, sol = real_ref[...], imag_ref[...], sol_ref[...]
        first = product(jnp.concatenate([real, sol], axis=0), imag)
        second = product(jnp.concatenate([real - imag, sol], axis=0), real + imag)
        cross, thin = first[:width], first[width:]
        turned = cross.T
        by_real = second[width:] - thin
        change = jnp.concatenate(
            [by_real[:coils] + thin[coils:], by_real[coils:] - thin[:coils]], axis=0
        )
        sol_ref[...] = factor * (2.0 * sol - change)
        real_ref[...] = factor * (2.0 * real - (second[:width] - cross - turned))
        imag_ref[...] = factor * (2.0 * imag - (cross - turned))
        return square / (2.0 - square)

    spread = (high - shift) / (high + shift)
    spread = lax.while_loop(
        lambda spread: spread > 0.99, functools.partial(step, fine_product), spread
    )
    spread = lax.while_loop(
        lambda spread: spread > settled, functools.partial(step, product), spread
    )
    sol = sol_ref[...]
    total = sol
    for _ in range(2):
        by_real = product(total, real_ref[...])
        by_imag = product(total, imag_ref[...])
        change = jnp.concatenate(
            [by_real[:coils] + by_imag[coils:], by_real[coils:] - by_imag[:coils]], axis=0
        )
        total = sol + (total - change)
    sol = total
    weights = jnp.concatenate([sol[:coils], sol[coils:]], axis=1).astype(BF16)
    for copy in range(out_ref.shape[0]):
        out_ref[copy] = weights


def select_kernel(told_ref, piece_ref, out_ref):
    pieces = [piece_ref[place].astype(F32) for place in range(piece_ref.shape[0])]
    for position, frame in enumerate(FRAMES):
        for slot in range(out_ref.shape[1]):
            wanted = jnp.broadcast_to(told_ref[frame : frame + 1, slot : slot + 1], pieces[0].shape)
            chosen = pieces[0]
            for place in range(1, len(pieces)):
                chosen = jnp.where(wanted == place, pieces[place], chosen)
            out_ref[position, slot] = chosen.astype(BF16)


def fill_kernel(reads_ref, places_ref, weights_ref, source_ref, interp_ref, out_ref):
    frames, slots, coils, depth = weights_ref.shape
    width = depth // 2
    terms = []
    for slot in range(slots):
        holder = jnp.broadcast_to(reads_ref[:, slot : slot + 1] & (frames - 1), (coils, depth))
        chosen = weights_ref[0, slot].astype(F32)
        for position, frame in enumerate(FRAMES):
            if position:
                chosen = jnp.where(holder == frame, weights_ref[position, slot].astype(F32), chosen)
        real, imag = chosen[:, :width], chosen[:, width:]
        matrix = jnp.concatenate(
            [jnp.concatenate([real, -imag], axis=1), jnp.concatenate([imag, real], axis=1)], axis=0
        ).astype(BF16)
        filled = across_rows(matrix, source_ref[0, slot]).astype(BF16)
        terms.append(across_rows(filled, interp_ref[0, slot]))
    shape = terms[0].shape
    places = [jnp.broadcast_to(places_ref[:, slot : slot + 1], shape) for slot in range(slots)]
    for block in range(out_ref.shape[0]):
        total = jnp.zeros(shape, F32)
        for place, term in zip(places, terms):
            total = total + jnp.where(place == block, term, 0.0)
        out_ref[block] = total.astype(BF16)


def on_device(cal_source, cal_target, app_source, readers, blocks, interp):
    frames = lax.axis_size("frame")
    segs = lax.axis_size("seg")
    coil_count = lax.axis_size("coil")
    held, samples, depth = cal_source.shape
    coils = cal_target.shape[1]
    width = depth // 2
    part = width // coil_count
    gram_rows = part + part // 2
    rows = gram_rows + 3 * coils + 8
    slots = readers.shape[1]
    cells = interp.shape[2]

    each = held // 2
    block = jax.ShapeDtypeStruct((each, rows, LANES), F32)
    listed = pltpu.with_memory_space_constraint(readers, pltpu.HBM)
    hbm = pl.BlockSpec(memory_space=pltpu.HBM)
    vmem = pl.BlockSpec(memory_space=pltpu.VMEM)
    reading = [pltpu.SMEM(readers.shape, jnp.int32)]
    turned = pltpu.VMEM((each, depth, samples), BF16)
    cost = pl.CostEstimate(
        flops=2 * each * samples * depth * 2 * (part + coils),
        bytes_accessed=2 * each * samples * (depth + 2 * coils),
        transcendentals=0,
    )
    send, own_held, own_goal = pl.pallas_call(
        functools.partial(other_gram_kernel, part, frames),
        in_specs=[hbm, hbm, hbm],
        out_shape=[
            block,
            jax.ShapeDtypeStruct((each, samples, depth), BF16),
            jax.ShapeDtypeStruct((each, coils, 2, samples), BF16),
        ],
        scratch_shapes=[
            pltpu.VMEM((each, samples, depth), BF16),
            pltpu.VMEM((each, coils, 2, samples), BF16),
            turned,
            *reading,
            pltpu.SemaphoreType.DMA((2, held)),
            pltpu.SemaphoreType.DMA,
        ],
        compiler_params=SMALL,
        cost_estimate=cost,
    )(
        listed,
        pltpu.with_memory_space_constraint(cal_source, pltpu.HBM),
        pltpu.with_memory_space_constraint(cal_target, pltpu.HBM),
    )
    keep = pl.pallas_call(
        functools.partial(own_gram_kernel, part, frames),
        in_specs=[hbm, vmem, vmem],
        out_shape=block,
        scratch_shapes=[turned, *reading, pltpu.SemaphoreType.DMA],
        compiler_params=SMALL,
        cost_estimate=cost,
    )(listed, own_held, own_goal)
    other = lax.ppermute(send, "frame", [(frame, frame ^ 1) for frame in range(frames)])
    chips = [[2 * chip + core for chip in CHIPS] for core in range(2)]
    received = lax.all_to_all(
        keep + other, "frame", 0, 0, tiled=True, axis_index_groups=chips
    )
    spread, rhs, told = pl.pallas_call(
        functools.partial(sum_kernel, gram_rows),
        out_shape=[
            jax.ShapeDtypeStruct((coil_count, gram_rows, LANES), F32),
            jax.ShapeDtypeStruct((3 * coils, LANES), F32),
            jax.ShapeDtypeStruct((frames, LANES), jnp.int32),
        ],
        compiler_params=SMALL,
    )(received)
    gram = lax.all_to_all(spread, "coil", 0, 0, tiled=True)
    weights = pl.pallas_call(
        functools.partial(solve_kernel, part),
        out_shape=jax.ShapeDtypeStruct((segs, coils, depth), BF16),
        scratch_shapes=[
            pltpu.VMEM((width, width), F32),
            pltpu.VMEM((width, width), F32),
            pltpu.VMEM((2 * coils, width), F32),
        ],
        compiler_params=SMALL,
    )(gram, rhs)
    pieces = lax.all_to_all(weights, "seg", 0, 0, tiled=True)
    sent = pl.pallas_call(
        select_kernel,
        out_shape=jax.ShapeDtypeStruct((frames, slots, coils, depth), BF16),
        compiler_params=SMALL,
    )(told, pieces)
    chosen = lax.all_to_all(
        sent, "frame", 0, 0, tiled=True, axis_index_groups=[list(FRAMES)]
    )
    grid = pl.pallas_call(
        fill_kernel,
        out_shape=jax.ShapeDtypeStruct((segs, 2 * coils, cells), BF16),
        compiler_params=SMALL,
    )(readers, blocks, chosen, app_source, interp)
    terms = lax.all_to_all(grid, "seg", 0, 0, tiled=True)
    total = jnp.sum(terms.astype(F32), axis=0)
    power = lax.all_gather(jnp.sum(total * total, axis=0, keepdims=True), "coil", tiled=True)
    return jnp.sqrt(jnp.sum(power, axis=0, keepdims=True) + epsilon)


def solution(mesh):
    placed = (
        P("seg", "frame", None),
        P("seg", "coil", None, "frame"),
        P("frame", "seg", None, None),
        P("frame", "seg"),
        P("frame", "seg"),
        P("frame", "seg", None, None),
    )
    return jax.shard_map(
        on_device, mesh=mesh, in_specs=placed, out_specs=P("frame", "seg"), check_vma=False
    )
```

```python
import functools

import jax
import jax.numpy as jnp
from jax import lax
from jax.experimental import pallas as pl
from jax.experimental.pallas import tpu as pltpu
from jax.sharding import PartitionSpec as P

regular = 0.02
epsilon = 1e-06
settled = 0.0125
F32 = jnp.float32
BF16 = jnp.bfloat16
LANES = 128
SMALL = pltpu.CompilerParams(vmem_limit_bytes=16 * 1024 * 1024)


def across_rows(left, right):
    return lax.dot_general(left, right, (((1,), (1,)), ((), ())), preferred_element_type=F32)


def pieces_of(value, count):
    out = []
    for _ in range(count):
        piece = value.astype(BF16)
        value = value - piece.astype(F32)
        out.append(piece)
    return out


def product(left, right):
    rows = left.shape[0]
    a, b = pieces_of(left, 2), pieces_of(right, 2)
    dot = functools.partial(jnp.dot, preferred_element_type=F32)
    first = dot(jnp.concatenate(a, axis=0), b[0])
    return first[:rows] + (first[rows:] + dot(a[0], b[1]))


def fine_product(left, right):
    rows = left.shape[0]
    a, b = pieces_of(left, 3), pieces_of(right, 3)
    dot = functools.partial(jnp.dot, preferred_element_type=F32)
    first = dot(jnp.concatenate(a, axis=0), b[0])
    second = dot(jnp.concatenate(a[:2], axis=0), b[1])
    return first[:rows] + (
        (first[rows : 2 * rows] + second[:rows])
        + (first[2 * rows :] + (second[rows:] + dot(a[0], b[2])))
    )


def gram_sums(groups, held_ref, goal_ref, out_ref, copies):
    depth = held_ref.shape[2]
    width = depth // 2
    half = width // 2
    base = width + half
    coils = goal_ref.shape[1]
    across = lax.broadcasted_iota(jnp.int32, (width, width), 1)
    down = lax.broadcasted_iota(jnp.int32, (width, width), 0)
    for slots in groups:
        for slot in slots:
            for copy in copies[slot]:
                copy.wait()
        turned = [held_ref[slot].T for slot in slots]
        for slot, flipped in zip(slots, turned):
            out = out_ref.at[slot]
            source = held_ref[slot]
            left = jnp.concatenate(
                [flipped[:width], goal_ref[slot, :, 0, :], goal_ref[slot, :, 1, :]], axis=0
            )
            top = jnp.dot(left, source, preferred_element_type=F32)
            bottom = jnp.dot(flipped[width:], source, preferred_element_type=F32)
            gram_real = top[:width, :width] + bottom[:, width:]
            gram_imag = top[:width, width:] - bottom[:, :width]
            packed = jnp.where(across <= down, gram_real, gram_imag)
            proj_real = top[width : width + coils]
            proj_imag = top[width + coils :]
            rhs_real = proj_real[:, :width] + proj_imag[:, width:]
            rhs_imag = proj_imag[:, :width] - proj_real[:, width:]
            out[:width] = packed[:, :LANES]
            out[width:base] = jnp.concatenate(
                [packed[:half, LANES:], packed[half:, LANES:]], axis=1
            )
            out[base : base + coils] = rhs_real[:, :LANES]
            out[base + coils : base + 2 * coils] = rhs_imag[:, :LANES]
            out[base + 2 * coils : base + 3 * coils] = jnp.concatenate(
                [rhs_real[:, LANES:], rhs_imag[:, LANES:]], axis=1
            )


def tell(frames, read_ref, out_ref):
    core = lax.rem(lax.axis_index("frame"), 2)
    row = lax.broadcasted_iota(jnp.int32, (8, LANES), 0)
    lane = lax.broadcasted_iota(jnp.int32, (8, LANES), 1)
    told = jnp.zeros((8, LANES), jnp.int32)
    for place in range(read_ref.shape[1]):
        told = jnp.where((row == core) & (lane == place), lax.div(read_ref[0, place], frames), told)
    for slot in range(out_ref.shape[0]):
        out_ref[slot, out_ref.shape[1] - 8 :] = told.astype(F32)


def other_gram_kernel(
    frames,
    reads_ref,
    source_ref,
    target_ref,
    out_ref,
    own_held_ref,
    own_goal_ref,
    held_ref,
    goal_ref,
    read_ref,
    sem,
    read_sem,
):
    core = lax.rem(lax.axis_index("frame"), 2)
    each = out_ref.shape[0]
    copies = []
    for slot in range(2 * each):
        own, place = slot // each, slot % each
        segment = 2 * place + (core if own else 1 - core)
        held = (own_held_ref if own else held_ref).at[place]
        goal = (own_goal_ref if own else goal_ref).at[place]
        copies.append(
            (
                pltpu.make_async_copy(source_ref.at[segment], held, sem.at[0, slot]),
                pltpu.make_async_copy(target_ref.at[segment], goal, sem.at[1, slot]),
            )
        )
    for pair in copies:
        for copy in pair:
            copy.start()
    listing = pltpu.make_async_copy(reads_ref, read_ref, read_sem)
    listing.start()
    gram_sums(((0,), (1, 2, 3)), held_ref, goal_ref, out_ref, copies)
    listing.wait()
    tell(frames, read_ref, out_ref)
    for pair in copies[each:]:
        for copy in pair:
            copy.wait()


def own_gram_kernel(frames, reads_ref, held_ref, goal_ref, out_ref, read_ref, read_sem):
    listing = pltpu.make_async_copy(reads_ref, read_ref, read_sem)
    listing.start()
    slots = tuple(range(out_ref.shape[0]))
    gram_sums((slots,), held_ref, goal_ref, out_ref, [() for _ in slots])
    listing.wait()
    tell(frames, read_ref, out_ref)


def solve_kernel(partial_ref, out_ref, told_ref, real_ref, imag_ref, sol_ref):
    width = real_ref.shape[0]
    half = width // 2
    coils = out_ref.shape[1]
    base = width + half
    rows = base + 3 * coils
    for chip in range(partial_ref.shape[0]):
        told_ref[2 * chip : 2 * chip + 2] = partial_ref[chip, rows : rows + 2].astype(jnp.int32)
    total = partial_ref[0, :rows]
    for chip in range(1, partial_ref.shape[0]):
        total = total + partial_ref[chip, :rows]
    tail = total[width:base]
    rhs = total[base:]
    packed = jnp.concatenate(
        [total[:width], jnp.concatenate([tail[:, :64], tail[:, 64:]], axis=0)], axis=1
    )
    flipped = packed.T
    down = lax.broadcasted_iota(jnp.int32, (width, width), 0)
    across = lax.broadcasted_iota(jnp.int32, (width, width), 1)
    diagonal = jnp.where(across == down, packed, 0.0)
    shift = regular / width * jnp.sum(diagonal)
    high = jnp.sqrt(jnp.sum(2.0 * (packed * packed) - diagonal * diagonal)) + shift
    scale = 2.0 / (high + shift)
    real = jnp.where(across <= down, packed, flipped)
    imag = jnp.where(across < down, -flipped, packed)
    real_ref[...] = (real + jnp.where(across == down, shift, 0.0)) * scale
    imag_ref[...] = jnp.where(across == down, 0.0, imag) * scale
    rhs_real = jnp.concatenate([rhs[:coils], rhs[2 * coils :, :64]], axis=1)
    rhs_imag = jnp.concatenate([rhs[coils : 2 * coils], rhs[2 * coils :, 64:]], axis=1)
    sol_ref[...] = jnp.concatenate([rhs_real, rhs_imag], axis=0) * scale

    def step(product, spread):
        square = spread * spread
        factor = 2.0 / (2.0 - square)
        real, imag, sol = real_ref[...], imag_ref[...], sol_ref[...]
        first = product(jnp.concatenate([real, sol], axis=0), imag)
        second = product(jnp.concatenate([real - imag, sol], axis=0), real + imag)
        cross, thin = first[:width], first[width:]
        turned = cross.T
        by_real = second[width:] - thin
        change = jnp.concatenate(
            [by_real[:coils] + thin[coils:], by_real[coils:] - thin[:coils]], axis=0
        )
        sol_ref[...] = factor * (2.0 * sol - change)
        real_ref[...] = factor * (2.0 * real - (second[:width] - cross - turned))
        imag_ref[...] = factor * (2.0 * imag - (cross - turned))
        return square / (2.0 - square)

    spread = (high - shift) / (high + shift)
    spread = lax.while_loop(
        lambda spread: spread > 0.99, functools.partial(step, fine_product), spread
    )
    spread = lax.while_loop(
        lambda spread: spread > settled, functools.partial(step, product), spread
    )
    sol = sol_ref[...]
    total = sol
    for _ in range(2):
        by_real = product(total, real_ref[...])
        by_imag = product(total, imag_ref[...])
        change = jnp.concatenate(
            [by_real[:coils] + by_imag[coils:], by_real[coils:] - by_imag[:coils]], axis=0
        )
        total = sol + (total - change)
    sol = total
    weights = jnp.concatenate([sol[:coils], sol[coils:]], axis=1).astype(BF16)
    for copy in range(out_ref.shape[0]):
        out_ref[copy] = weights


def select_kernel(told_ref, piece_ref, out_ref):
    pieces = [piece_ref[place].astype(F32) for place in range(piece_ref.shape[0])]
    for frame in range(out_ref.shape[0]):
        for slot in range(out_ref.shape[1]):
            wanted = jnp.broadcast_to(told_ref[frame : frame + 1, slot : slot + 1], pieces[0].shape)
            chosen = pieces[0]
            for place in range(1, len(pieces)):
                chosen = jnp.where(wanted == place, pieces[place], chosen)
            out_ref[frame, slot] = chosen.astype(BF16)


def fill_kernel(reads_ref, places_ref, weights_ref, source_ref, interp_ref, out_ref):
    frames, slots, coils, depth = weights_ref.shape
    width = depth // 2
    terms = []
    for slot in range(slots):
        holder = jnp.broadcast_to(reads_ref[:, slot : slot + 1] & (frames - 1), (coils, depth))
        chosen = weights_ref[0, slot].astype(F32)
        for frame in range(1, frames):
            chosen = jnp.where(holder == frame, weights_ref[frame, slot].astype(F32), chosen)
        real, imag = chosen[:, :width], chosen[:, width:]
        matrix = jnp.concatenate(
            [jnp.concatenate([real, -imag], axis=1), jnp.concatenate([imag, real], axis=1)], axis=0
        ).astype(BF16)
        filled = across_rows(matrix, source_ref[0, slot]).astype(BF16)
        terms.append(across_rows(filled, interp_ref[0, slot]))
    shape = terms[0].shape
    places = [jnp.broadcast_to(places_ref[:, slot : slot + 1], shape) for slot in range(slots)]
    for block in range(out_ref.shape[0]):
        total = jnp.zeros(shape, F32)
        for place, term in zip(places, terms):
            total = total + jnp.where(place == block, term, 0.0)
        out_ref[block] = total.astype(BF16)


def on_device(cal_source, cal_target, app_source, readers, blocks, interp):
    frames = lax.axis_size("frame")
    segs = lax.axis_size("seg")
    held, samples, depth = cal_source.shape
    coils = cal_target.shape[1]
    width = depth // 2
    rows = width + width // 2 + 3 * coils + 8
    slots = readers.shape[1]
    cells = interp.shape[2]

    each = held // 2
    block = jax.ShapeDtypeStruct((each, rows, LANES), F32)
    listed = pltpu.with_memory_space_constraint(readers, pltpu.HBM)
    hbm = pl.BlockSpec(memory_space=pltpu.HBM)
    vmem = pl.BlockSpec(memory_space=pltpu.VMEM)
    reading = [pltpu.SMEM(readers.shape, jnp.int32)]
    cost = pl.CostEstimate(
        flops=2 * each * samples * depth * (depth + 2 * coils),
        bytes_accessed=2 * each * samples * (depth + 2 * coils),
        transcendentals=0,
    )
    send, own_held, own_goal = pl.pallas_call(
        functools.partial(other_gram_kernel, frames),
        in_specs=[hbm, hbm, hbm],
        out_shape=[
            block,
            jax.ShapeDtypeStruct((each, samples, depth), BF16),
            jax.ShapeDtypeStruct((each, coils, 2, samples), BF16),
        ],
        scratch_shapes=[
            pltpu.VMEM((each, samples, depth), BF16),
            pltpu.VMEM((each, coils, 2, samples), BF16),
            *reading,
            pltpu.SemaphoreType.DMA((2, held)),
            pltpu.SemaphoreType.DMA,
        ],
        compiler_params=SMALL,
        cost_estimate=cost,
    )(
        listed,
        pltpu.with_memory_space_constraint(cal_source, pltpu.HBM),
        pltpu.with_memory_space_constraint(cal_target, pltpu.HBM),
    )
    keep = pl.pallas_call(
        functools.partial(own_gram_kernel, frames),
        in_specs=[hbm, vmem, vmem],
        out_shape=block,
        scratch_shapes=[*reading, pltpu.SemaphoreType.DMA],
        compiler_params=SMALL,
        cost_estimate=cost,
    )(listed, own_held, own_goal)
    other = lax.ppermute(send, "frame", [(frame, frame ^ 1) for frame in range(frames)])
    chips = [[2 * chip + core for chip in range(frames // 2)] for core in range(2)]
    received = lax.all_to_all(
        keep + other, "frame", 0, 0, tiled=True, axis_index_groups=chips
    )
    weights, told = pl.pallas_call(
        solve_kernel,
        out_shape=[
            jax.ShapeDtypeStruct((segs, coils, depth), BF16),
            jax.ShapeDtypeStruct((frames, LANES), jnp.int32),
        ],
        scratch_shapes=[
            pltpu.VMEM((width, width), F32),
            pltpu.VMEM((width, width), F32),
            pltpu.VMEM((2 * coils, width), F32),
        ],
        compiler_params=SMALL,
    )(received)
    pieces = lax.all_to_all(weights, "seg", 0, 0, tiled=True)
    sent = pl.pallas_call(
        select_kernel,
        out_shape=jax.ShapeDtypeStruct((frames, slots, coils, depth), BF16),
        compiler_params=SMALL,
    )(told, pieces)
    chosen = lax.all_to_all(sent, "frame", 0, 0, tiled=True)
    grid = pl.pallas_call(
        fill_kernel,
        out_shape=jax.ShapeDtypeStruct((segs, 2 * coils, cells), BF16),
        compiler_params=SMALL,
    )(readers, blocks, chosen, app_source, interp)
    terms = lax.all_to_all(grid, "seg", 0, 0, tiled=True)
    total = jnp.sum(terms.astype(F32), axis=0)
    power = lax.all_gather(jnp.sum(total * total, axis=0, keepdims=True), "coil", tiled=True)
    return jnp.sqrt(jnp.sum(power, axis=0, keepdims=True) + epsilon)


def solution(mesh):
    placed = (
        P("seg", "frame", None),
        P("seg", "coil", None, "frame"),
        P("frame", "seg", None, None),
        P("frame", "seg"),
        P("frame", "seg"),
        P("frame", "seg", None, None),
    )
    return jax.shard_map(
        on_device, mesh=mesh, in_specs=placed, out_specs=P("frame", "seg"), check_vma=False
    )
```

```python
import functools

import jax
import jax.numpy as jnp
from jax import lax
from jax.experimental import pallas as pl
from jax.experimental.pallas import tpu as pltpu
from jax.sharding import PartitionSpec as P

regular = 0.02
epsilon = 1e-06
settled = 0.0125
F32 = jnp.float32
BF16 = jnp.bfloat16
LANES = 128
SMALL = pltpu.CompilerParams(vmem_limit_bytes=16 * 1024 * 1024)


def across_rows(left, right):
    return lax.dot_general(left, right, (((1,), (1,)), ((), ())), preferred_element_type=F32)


def pieces_of(value, count):
    out = []
    for _ in range(count):
        piece = value.astype(BF16)
        value = value - piece.astype(F32)
        out.append(piece)
    return out


def product(left, right):
    rows = left.shape[0]
    a, b = pieces_of(left, 2), pieces_of(right, 2)
    dot = functools.partial(jnp.dot, preferred_element_type=F32)
    first = dot(jnp.concatenate(a, axis=0), b[0])
    return first[:rows] + (first[rows:] + dot(a[0], b[1]))


def fine_product(left, right):
    rows = left.shape[0]
    a, b = pieces_of(left, 3), pieces_of(right, 3)
    dot = functools.partial(jnp.dot, preferred_element_type=F32)
    first = dot(jnp.concatenate(a, axis=0), b[0])
    second = dot(jnp.concatenate(a[:2], axis=0), b[1])
    return first[:rows] + (
        (first[rows : 2 * rows] + second[:rows])
        + (first[2 * rows :] + (second[rows:] + dot(a[0], b[2])))
    )


def gram_sums(part, groups, picked, held_ref, goal_ref, turned_ref, out_ref, copies):
    coil = lax.axis_index("coil")
    depth = held_ref.shape[2]
    width = depth // 2
    half = part // 2
    base = part + half
    coils = goal_ref.shape[1]
    across = lax.broadcasted_iota(jnp.int32, (part, width), 1)
    down = lax.broadcasted_iota(jnp.int32, (part, width), 0) + coil * part
    first = pl.multiple_of(coil * part, 16)
    second = pl.multiple_of(width + coil * part, 16)
    row = lax.broadcasted_iota(jnp.int32, (2 * part, depth), 0)
    column = lax.broadcasted_iota(jnp.int32, (2 * part, depth), 1)
    wanted = coil * part + jnp.where(row < part, row, row - part + width)
    pick = jnp.where(column == wanted, 1.0, 0.0).astype(BF16)
    for slots in groups:
        for slot in slots:
            for copy in copies[slot]:
                copy.wait()
        lefts = []
        for slot in slots:
            if slot in picked:
                mine = [across_rows(pick, held_ref[slot]).astype(BF16)]
            else:
                turned_ref[slot] = held_ref[slot].T
                mine = [
                    turned_ref[slot, pl.ds(first, part)],
                    turned_ref[slot, pl.ds(second, part)],
                ]
            lefts.append(
                jnp.concatenate([*mine, goal_ref[slot, :, 0, :], goal_ref[slot, :, 1, :]], axis=0)
            )
        products = [
            jnp.dot(left, held_ref[slot], preferred_element_type=F32)
            for left, slot in zip(lefts, slots)
        ]
        for slot, sums in zip(slots, products):
            out = out_ref.at[slot]
            top, bottom = sums[:part], sums[part : 2 * part]
            gram_real = top[:, :width] + bottom[:, width:]
            gram_imag = top[:, width:] - bottom[:, :width]
            packed = jnp.where(across <= down, gram_real, gram_imag)
            proj_real = sums[2 * part : 2 * part + coils]
            proj_imag = sums[2 * part + coils :]
            rhs_real = proj_real[:, :width] + proj_imag[:, width:]
            rhs_imag = proj_imag[:, :width] - proj_real[:, width:]
            out[:part] = packed[:, :LANES]
            out[part:base] = jnp.concatenate(
                [packed[:half, LANES:], packed[half:, LANES:]], axis=1
            )
            out[base : base + coils] = rhs_real[:, :LANES]
            out[base + coils : base + 2 * coils] = rhs_imag[:, :LANES]
            out[base + 2 * coils : base + 3 * coils] = jnp.concatenate(
                [rhs_real[:, LANES:], rhs_imag[:, LANES:]], axis=1
            )


def tell(frames, read_ref, out_ref):
    core = lax.rem(lax.axis_index("frame"), 2)
    row = lax.broadcasted_iota(jnp.int32, (8, LANES), 0)
    lane = lax.broadcasted_iota(jnp.int32, (8, LANES), 1)
    told = jnp.zeros((8, LANES), jnp.int32)
    for place in range(read_ref.shape[1]):
        told = jnp.where((row == core) & (lane == place), lax.div(read_ref[0, place], frames), told)
    for slot in range(out_ref.shape[0]):
        out_ref[slot, out_ref.shape[1] - 8 :] = told.astype(F32)


def other_gram_kernel(
    part,
    frames,
    reads_ref,
    source_ref,
    target_ref,
    out_ref,
    own_held_ref,
    own_goal_ref,
    held_ref,
    goal_ref,
    turned_ref,
    read_ref,
    sem,
    read_sem,
):
    core = lax.rem(lax.axis_index("frame"), 2)
    each = out_ref.shape[0]
    copies = []
    for slot in range(2 * each):
        own, place = slot // each, slot % each
        segment = 2 * place + (core if own else 1 - core)
        held = (own_held_ref if own else held_ref).at[place]
        goal = (own_goal_ref if own else goal_ref).at[place]
        copies.append(
            (
                pltpu.make_async_copy(source_ref.at[segment], held, sem.at[0, slot]),
                pltpu.make_async_copy(target_ref.at[segment], goal, sem.at[1, slot]),
            )
        )
    for pair in copies:
        for copy in pair:
            copy.start()
    listing = pltpu.make_async_copy(reads_ref, read_ref, read_sem)
    listing.start()
    gram_sums(part, ((0,), (1, 2, 3)), (), held_ref, goal_ref, turned_ref, out_ref, copies)
    listing.wait()
    tell(frames, read_ref, out_ref)
    for pair in copies[each:]:
        for copy in pair:
            copy.wait()


def own_gram_kernel(part, frames, reads_ref, held_ref, goal_ref, out_ref, turned_ref, read_ref, read_sem):
    listing = pltpu.make_async_copy(reads_ref, read_ref, read_sem)
    listing.start()
    slots = tuple(range(out_ref.shape[0]))
    gram_sums(part, (slots,), (2,), held_ref, goal_ref, turned_ref, out_ref, [() for _ in slots])
    listing.wait()
    tell(frames, read_ref, out_ref)


def sum_kernel(gram_rows, partial_ref, spread_ref, rhs_ref, told_ref):
    rows = gram_rows + rhs_ref.shape[0]
    total = partial_ref[0, :rows]
    for chip in range(1, partial_ref.shape[0]):
        total = total + partial_ref[chip, :rows]
    for copy in range(spread_ref.shape[0]):
        spread_ref[copy] = total[:gram_rows]
    rhs_ref[...] = total[gram_rows:]
    for chip in range(partial_ref.shape[0]):
        told_ref[2 * chip : 2 * chip + 2] = partial_ref[chip, rows : rows + 2].astype(jnp.int32)


def solve_kernel(part, gram_ref, rhs_ref, out_ref, real_ref, imag_ref, sol_ref):
    width = 4 * part
    half = part // 2
    coils = rhs_ref.shape[0] // 3
    pieces = []
    for coil in range(4):
        block = gram_ref[coil]
        tail = block[part:]
        pieces.append(
            jnp.concatenate(
                [block[:part], jnp.concatenate([tail[:, :64], tail[:, 64:]], axis=0)], axis=1
            )
        )
    packed = jnp.concatenate(pieces, axis=0)
    flipped = packed.T
    down = lax.broadcasted_iota(jnp.int32, (width, width), 0)
    across = lax.broadcasted_iota(jnp.int32, (width, width), 1)
    diagonal = jnp.where(across == down, packed, 0.0)
    shift = regular / width * jnp.sum(diagonal)
    high = jnp.sqrt(jnp.sum(2.0 * (packed * packed) - diagonal * diagonal)) + shift
    scale = 2.0 / (high + shift)
    real = jnp.where(across <= down, packed, flipped)
    imag = jnp.where(across < down, -flipped, packed)
    real_ref[...] = (real + jnp.where(across == down, shift, 0.0)) * scale
    imag_ref[...] = jnp.where(across == down, 0.0, imag) * scale
    rhs_real = jnp.concatenate([rhs_ref[:coils], rhs_ref[2 * coils :, :64]], axis=1)
    rhs_imag = jnp.concatenate([rhs_ref[coils : 2 * coils], rhs_ref[2 * coils :, 64:]], axis=1)
    sol_ref[...] = jnp.concatenate([rhs_real, rhs_imag], axis=0) * scale

    def step(product, spread):
        square = spread * spread
        factor = 2.0 / (2.0 - square)
        real, imag, sol = real_ref[...], imag_ref[...], sol_ref[...]
        first = product(jnp.concatenate([real, sol], axis=0), imag)
        second = product(jnp.concatenate([real - imag, sol], axis=0), real + imag)
        cross, thin = first[:width], first[width:]
        turned = cross.T
        by_real = second[width:] - thin
        change = jnp.concatenate(
            [by_real[:coils] + thin[coils:], by_real[coils:] - thin[:coils]], axis=0
        )
        sol_ref[...] = factor * (2.0 * sol - change)
        real_ref[...] = factor * (2.0 * real - (second[:width] - cross - turned))
        imag_ref[...] = factor * (2.0 * imag - (cross - turned))
        return square / (2.0 - square)

    spread = (high - shift) / (high + shift)
    spread = lax.while_loop(
        lambda spread: spread > 0.99, functools.partial(step, fine_product), spread
    )
    spread = lax.while_loop(
        lambda spread: spread > settled, functools.partial(step, product), spread
    )
    sol = sol_ref[...]
    total = sol
    for _ in range(2):
        by_real = product(total, real_ref[...])
        by_imag = product(total, imag_ref[...])
        change = jnp.concatenate(
            [by_real[:coils] + by_imag[coils:], by_real[coils:] - by_imag[:coils]], axis=0
        )
        total = sol + (total - change)
    sol = total
    weights = jnp.concatenate([sol[:coils], sol[coils:]], axis=1).astype(BF16)
    for copy in range(out_ref.shape[0]):
        out_ref[copy] = weights


def select_kernel(told_ref, piece_ref, out_ref):
    pieces = [piece_ref[place].astype(F32) for place in range(piece_ref.shape[0])]
    for frame in range(out_ref.shape[0]):
        for slot in range(out_ref.shape[1]):
            wanted = jnp.broadcast_to(told_ref[frame : frame + 1, slot : slot + 1], pieces[0].shape)
            chosen = pieces[0]
            for place in range(1, len(pieces)):
                chosen = jnp.where(wanted == place, pieces[place], chosen)
            out_ref[frame, slot] = chosen.astype(BF16)


def fill_kernel(reads_ref, places_ref, weights_ref, source_ref, interp_ref, out_ref):
    frames, slots, coils, depth = weights_ref.shape
    width = depth // 2
    terms = []
    for slot in range(slots):
        holder = jnp.broadcast_to(reads_ref[:, slot : slot + 1] & (frames - 1), (coils, depth))
        chosen = weights_ref[0, slot].astype(F32)
        for frame in range(1, frames):
            chosen = jnp.where(holder == frame, weights_ref[frame, slot].astype(F32), chosen)
        real, imag = chosen[:, :width], chosen[:, width:]
        matrix = jnp.concatenate(
            [jnp.concatenate([real, -imag], axis=1), jnp.concatenate([imag, real], axis=1)], axis=0
        ).astype(BF16)
        filled = across_rows(matrix, source_ref[0, slot]).astype(BF16)
        terms.append(across_rows(filled, interp_ref[0, slot]))
    shape = terms[0].shape
    places = [jnp.broadcast_to(places_ref[:, slot : slot + 1], shape) for slot in range(slots)]
    for block in range(out_ref.shape[0]):
        total = jnp.zeros(shape, F32)
        for place, term in zip(places, terms):
            total = total + jnp.where(place == block, term, 0.0)
        out_ref[block] = total.astype(BF16)


def on_device(cal_source, cal_target, app_source, readers, blocks, interp):
    frames = lax.axis_size("frame")
    segs = lax.axis_size("seg")
    coil_count = lax.axis_size("coil")
    held, samples, depth = cal_source.shape
    coils = cal_target.shape[1]
    width = depth // 2
    part = width // coil_count
    gram_rows = part + part // 2
    rows = gram_rows + 3 * coils + 8
    slots = readers.shape[1]
    cells = interp.shape[2]

    each = held // 2
    block = jax.ShapeDtypeStruct((each, rows, LANES), F32)
    listed = pltpu.with_memory_space_constraint(readers, pltpu.HBM)
    hbm = pl.BlockSpec(memory_space=pltpu.HBM)
    vmem = pl.BlockSpec(memory_space=pltpu.VMEM)
    reading = [pltpu.SMEM(readers.shape, jnp.int32)]
    turned = pltpu.VMEM((each, depth, samples), BF16)
    cost = pl.CostEstimate(
        flops=2 * each * samples * depth * 2 * (part + coils),
        bytes_accessed=2 * each * samples * (depth + 2 * coils),
        transcendentals=0,
    )
    send, own_held, own_goal = pl.pallas_call(
        functools.partial(other_gram_kernel, part, frames),
        in_specs=[hbm, hbm, hbm],
        out_shape=[
            block,
            jax.ShapeDtypeStruct((each, samples, depth), BF16),
            jax.ShapeDtypeStruct((each, coils, 2, samples), BF16),
        ],
        scratch_shapes=[
            pltpu.VMEM((each, samples, depth), BF16),
            pltpu.VMEM((each, coils, 2, samples), BF16),
            turned,
            *reading,
            pltpu.SemaphoreType.DMA((2, held)),
            pltpu.SemaphoreType.DMA,
        ],
        compiler_params=SMALL,
        cost_estimate=cost,
    )(
        listed,
        pltpu.with_memory_space_constraint(cal_source, pltpu.HBM),
        pltpu.with_memory_space_constraint(cal_target, pltpu.HBM),
    )
    keep = pl.pallas_call(
        functools.partial(own_gram_kernel, part, frames),
        in_specs=[hbm, vmem, vmem],
        out_shape=block,
        scratch_shapes=[turned, *reading, pltpu.SemaphoreType.DMA],
        compiler_params=SMALL,
        cost_estimate=cost,
    )(listed, own_held, own_goal)
    other = lax.ppermute(send, "frame", [(frame, frame ^ 1) for frame in range(frames)])
    chips = [[2 * chip + core for chip in range(frames // 2)] for core in range(2)]
    received = lax.all_to_all(
        keep + other, "frame", 0, 0, tiled=True, axis_index_groups=chips
    )
    spread, rhs, told = pl.pallas_call(
        functools.partial(sum_kernel, gram_rows),
        out_shape=[
            jax.ShapeDtypeStruct((coil_count, gram_rows, LANES), F32),
            jax.ShapeDtypeStruct((3 * coils, LANES), F32),
            jax.ShapeDtypeStruct((frames, LANES), jnp.int32),
        ],
        compiler_params=SMALL,
    )(received)
    gram = lax.all_to_all(spread, "coil", 0, 0, tiled=True)
    weights = pl.pallas_call(
        functools.partial(solve_kernel, part),
        out_shape=jax.ShapeDtypeStruct((segs, coils, depth), BF16),
        scratch_shapes=[
            pltpu.VMEM((width, width), F32),
            pltpu.VMEM((width, width), F32),
            pltpu.VMEM((2 * coils, width), F32),
        ],
        compiler_params=SMALL,
    )(gram, rhs)
    pieces = lax.all_to_all(weights, "seg", 0, 0, tiled=True)
    sent = pl.pallas_call(
        select_kernel,
        out_shape=jax.ShapeDtypeStruct((frames, slots, coils, depth), BF16),
        compiler_params=SMALL,
    )(told, pieces)
    chosen = lax.all_to_all(sent, "frame", 0, 0, tiled=True)
    grid = pl.pallas_call(
        fill_kernel,
        out_shape=jax.ShapeDtypeStruct((segs, 2 * coils, cells), BF16),
        compiler_params=SMALL,
    )(readers, blocks, chosen, app_source, interp)
    terms = lax.all_to_all(grid, "seg", 0, 0, tiled=True)
    total = jnp.sum(terms.astype(F32), axis=0)
    power = lax.all_gather(jnp.sum(total * total, axis=0, keepdims=True), "coil", tiled=True)
    return jnp.sqrt(jnp.sum(power, axis=0, keepdims=True) + epsilon)


def solution(mesh):
    placed = (
        P("seg", "frame", None),
        P("seg", "coil", None, "frame"),
        P("frame", "seg", None, None),
        P("frame", "seg"),
        P("frame", "seg"),
        P("frame", "seg", None, None),
    )
    return jax.shard_map(
        on_device, mesh=mesh, in_specs=placed, out_specs=P("frame", "seg"), check_vma=False
    )
```

```python
import functools

import jax
import jax.numpy as jnp
from jax import lax
from jax.experimental import pallas as pl
from jax.experimental.pallas import tpu as pltpu
from jax.sharding import PartitionSpec as P

regular = 0.02
epsilon = 1e-06
settled = 0.0125
F32 = jnp.float32
BF16 = jnp.bfloat16
LANES = 128
SMALL = pltpu.CompilerParams(vmem_limit_bytes=16 * 1024 * 1024)


def across_rows(left, right):
    return lax.dot_general(left, right, (((1,), (1,)), ((), ())), preferred_element_type=F32)


def pieces_of(value, count):
    out = []
    for _ in range(count):
        piece = value.astype(BF16)
        value = value - piece.astype(F32)
        out.append(piece)
    return out


def product(left, right):
    rows = left.shape[0]
    a, b = pieces_of(left, 2), pieces_of(right, 2)
    dot = functools.partial(jnp.dot, preferred_element_type=F32)
    first = dot(jnp.concatenate(a, axis=0), b[0])
    return first[:rows] + (first[rows:] + dot(a[0], b[1]))


def fine_product(left, right):
    rows = left.shape[0]
    a, b = pieces_of(left, 3), pieces_of(right, 3)
    dot = functools.partial(jnp.dot, preferred_element_type=F32)
    first = dot(jnp.concatenate(a, axis=0), b[0])
    second = dot(jnp.concatenate(a[:2], axis=0), b[1])
    return first[:rows] + (
        (first[rows : 2 * rows] + second[:rows])
        + (first[2 * rows :] + (second[rows:] + dot(a[0], b[2])))
    )


def gram_sums(part, groups, picked, held_ref, goal_ref, turned_ref, out_ref, copies):
    coil = lax.axis_index("coil")
    depth = held_ref.shape[2]
    width = depth // 2
    half = part // 2
    base = part + half
    coils = goal_ref.shape[1]
    across = lax.broadcasted_iota(jnp.int32, (part, width), 1)
    down = lax.broadcasted_iota(jnp.int32, (part, width), 0) + coil * part
    first = pl.multiple_of(coil * part, 16)
    second = pl.multiple_of(width + coil * part, 16)
    row = lax.broadcasted_iota(jnp.int32, (2 * part, depth), 0)
    column = lax.broadcasted_iota(jnp.int32, (2 * part, depth), 1)
    wanted = coil * part + jnp.where(row < part, row, row - part + width)
    pick = jnp.where(column == wanted, 1.0, 0.0).astype(BF16)
    for slots in groups:
        for slot in slots:
            for copy in copies[slot]:
                copy.wait()
        lefts = []
        for slot in slots:
            if slot in picked:
                mine = [across_rows(pick, held_ref[slot]).astype(BF16)]
            else:
                turned_ref[slot] = held_ref[slot].T
                mine = [
                    turned_ref[slot, pl.ds(first, part)],
                    turned_ref[slot, pl.ds(second, part)],
                ]
            lefts.append(
                jnp.concatenate([*mine, goal_ref[slot, :, 0, :], goal_ref[slot, :, 1, :]], axis=0)
            )
        products = [
            jnp.dot(left, held_ref[slot], preferred_element_type=F32)
            for left, slot in zip(lefts, slots)
        ]
        for slot, sums in zip(slots, products):
            out = out_ref.at[slot]
            top, bottom = sums[:part], sums[part : 2 * part]
            gram_real = top[:, :width] + bottom[:, width:]
            gram_imag = top[:, width:] - bottom[:, :width]
            packed = jnp.where(across <= down, gram_real, gram_imag)
            proj_real = sums[2 * part : 2 * part + coils]
            proj_imag = sums[2 * part + coils :]
            rhs_real = proj_real[:, :width] + proj_imag[:, width:]
            rhs_imag = proj_imag[:, :width] - proj_real[:, width:]
            out[:part] = packed[:, :LANES]
            out[part:base] = jnp.concatenate(
                [packed[:half, LANES:], packed[half:, LANES:]], axis=1
            )
            out[base : base + coils] = rhs_real[:, :LANES]
            out[base + coils : base + 2 * coils] = rhs_imag[:, :LANES]
            out[base + 2 * coils : base + 3 * coils] = jnp.concatenate(
                [rhs_real[:, LANES:], rhs_imag[:, LANES:]], axis=1
            )


def tell(frames, read_ref, out_ref):
    core = lax.rem(lax.axis_index("frame"), 2)
    row = lax.broadcasted_iota(jnp.int32, (8, LANES), 0)
    lane = lax.broadcasted_iota(jnp.int32, (8, LANES), 1)
    told = jnp.zeros((8, LANES), jnp.int32)
    for place in range(read_ref.shape[1]):
        told = jnp.where((row == core) & (lane == place), lax.div(read_ref[0, place], frames), told)
    for slot in range(out_ref.shape[0]):
        out_ref[slot, out_ref.shape[1] - 8 :] = told.astype(F32)


def other_gram_kernel(
    part,
    frames,
    reads_ref,
    source_ref,
    target_ref,
    app_ref,
    interp_ref,
    out_ref,
    own_held_ref,
    own_goal_ref,
    own_app_ref,
    own_interp_ref,
    held_ref,
    goal_ref,
    turned_ref,
    read_ref,
    sem,
    late_sem,
):
    core = lax.rem(lax.axis_index("frame"), 2)
    each = out_ref.shape[0]
    copies = []
    for slot in range(2 * each):
        own, place = slot // each, slot % each
        segment = 2 * place + (core if own else 1 - core)
        held = (own_held_ref if own else held_ref).at[place]
        goal = (own_goal_ref if own else goal_ref).at[place]
        copies.append(
            (
                pltpu.make_async_copy(source_ref.at[segment], held, sem.at[0, slot]),
                pltpu.make_async_copy(target_ref.at[segment], goal, sem.at[1, slot]),
            )
        )
    for pair in copies:
        for copy in pair:
            copy.start()
    late = [
        pltpu.make_async_copy(reads_ref, read_ref, late_sem.at[0]),
        pltpu.make_async_copy(app_ref, own_app_ref, late_sem.at[1]),
        pltpu.make_async_copy(interp_ref, own_interp_ref, late_sem.at[2]),
    ]
    for copy in late:
        copy.start()
    gram_sums(part, ((0,), (1, 2, 3)), (), held_ref, goal_ref, turned_ref, out_ref, copies)
    late[0].wait()
    tell(frames, read_ref, out_ref)
    for copy in late[1:]:
        copy.wait()
    for pair in copies[each:]:
        for copy in pair:
            copy.wait()


def own_gram_kernel(part, frames, reads_ref, held_ref, goal_ref, out_ref, turned_ref, read_ref, read_sem):
    listing = pltpu.make_async_copy(reads_ref, read_ref, read_sem)
    listing.start()
    slots = tuple(range(out_ref.shape[0]))
    gram_sums(part, (slots,), (2,), held_ref, goal_ref, turned_ref, out_ref, [() for _ in slots])
    listing.wait()
    tell(frames, read_ref, out_ref)


def sum_kernel(gram_rows, partial_ref, spread_ref, rhs_ref, told_ref):
    rows = gram_rows + rhs_ref.shape[0]
    total = partial_ref[0, :rows]
    for chip in range(1, partial_ref.shape[0]):
        total = total + partial_ref[chip, :rows]
    for copy in range(spread_ref.shape[0]):
        spread_ref[copy] = total[:gram_rows]
    rhs_ref[...] = total[gram_rows:]
    for chip in range(partial_ref.shape[0]):
        told_ref[2 * chip : 2 * chip + 2] = partial_ref[chip, rows : rows + 2].astype(jnp.int32)


def solve_kernel(part, gram_ref, rhs_ref, out_ref, real_ref, imag_ref, sol_ref):
    width = 4 * part
    half = part // 2
    coils = rhs_ref.shape[0] // 3
    pieces = []
    for coil in range(4):
        block = gram_ref[coil]
        tail = block[part:]
        pieces.append(
            jnp.concatenate(
                [block[:part], jnp.concatenate([tail[:, :64], tail[:, 64:]], axis=0)], axis=1
            )
        )
    packed = jnp.concatenate(pieces, axis=0)
    flipped = packed.T
    down = lax.broadcasted_iota(jnp.int32, (width, width), 0)
    across = lax.broadcasted_iota(jnp.int32, (width, width), 1)
    diagonal = jnp.where(across == down, packed, 0.0)
    shift = regular / width * jnp.sum(diagonal, keepdims=True)
    norm = jnp.sum(2.0 * (packed * packed) - diagonal * diagonal, keepdims=True)
    high = jnp.sqrt(norm) + shift
    scale = 2.0 / (high + shift)
    real = jnp.where(across <= down, packed, flipped)
    imag = jnp.where(across < down, -flipped, packed)
    real_ref[...] = (real + jnp.where(across == down, shift, 0.0)) * scale
    imag_ref[...] = jnp.where(across == down, 0.0, imag) * scale
    rhs_real = jnp.concatenate([rhs_ref[:coils], rhs_ref[2 * coils :, :64]], axis=1)
    rhs_imag = jnp.concatenate([rhs_ref[coils : 2 * coils], rhs_ref[2 * coils :, 64:]], axis=1)
    sol_ref[...] = jnp.concatenate([rhs_real, rhs_imag], axis=0) * scale

    def step(product, spread):
        square = spread * spread
        factor = 2.0 / (2.0 - square)
        real, imag, sol = real_ref[...], imag_ref[...], sol_ref[...]
        first = product(jnp.concatenate([real, sol], axis=0), imag)
        second = product(jnp.concatenate([real - imag, sol], axis=0), real + imag)
        cross, thin = first[:width], first[width:]
        turned = cross.T
        by_real = second[width:] - thin
        change = jnp.concatenate(
            [by_real[:coils] + thin[coils:], by_real[coils:] - thin[:coils]], axis=0
        )
        sol_ref[...] = factor * (2.0 * sol - change)
        real_ref[...] = factor * (2.0 * real - (second[:width] - cross - turned))
        imag_ref[...] = factor * (2.0 * imag - (cross - turned))
        return square / (2.0 - square)

    spread = jnp.sum((high - shift) / (high + shift))
    spread = lax.while_loop(
        lambda spread: spread > 0.99, functools.partial(step, fine_product), spread
    )
    spread = lax.while_loop(
        lambda spread: spread > settled, functools.partial(step, product), spread
    )
    sol = sol_ref[...]
    total = sol
    for _ in range(2):
        by_real = product(total, real_ref[...])
        by_imag = product(total, imag_ref[...])
        change = jnp.concatenate(
            [by_real[:coils] + by_imag[coils:], by_real[coils:] - by_imag[:coils]], axis=0
        )
        total = sol + (total - change)
    sol = total
    weights = jnp.concatenate([sol[:coils], sol[coils:]], axis=1).astype(BF16)
    for copy in range(out_ref.shape[0]):
        out_ref[copy] = weights


def select_kernel(told_ref, piece_ref, out_ref):
    pieces = [piece_ref[place].astype(F32) for place in range(piece_ref.shape[0])]
    for frame in range(out_ref.shape[0]):
        for slot in range(out_ref.shape[1]):
            wanted = jnp.broadcast_to(told_ref[frame : frame + 1, slot : slot + 1], pieces[0].shape)
            chosen = pieces[0]
            for place in range(1, len(pieces)):
                chosen = jnp.where(wanted == place, pieces[place], chosen)
            out_ref[frame, slot] = chosen.astype(BF16)


def fill_kernel(reads_ref, places_ref, weights_ref, source_ref, interp_ref, out_ref):
    frames, slots, coils, depth = weights_ref.shape
    width = depth // 2
    terms = []
    for slot in range(slots):
        holder = jnp.broadcast_to(reads_ref[:, slot : slot + 1] & (frames - 1), (coils, depth))
        chosen = weights_ref[0, slot].astype(F32)
        for frame in range(1, frames):
            chosen = jnp.where(holder == frame, weights_ref[frame, slot].astype(F32), chosen)
        real, imag = chosen[:, :width], chosen[:, width:]
        matrix = jnp.concatenate(
            [jnp.concatenate([real, -imag], axis=1), jnp.concatenate([imag, real], axis=1)], axis=0
        ).astype(BF16)
        filled = across_rows(matrix, source_ref[0, slot]).astype(BF16)
        terms.append(across_rows(filled, interp_ref[0, slot]))
    shape = terms[0].shape
    places = [jnp.broadcast_to(places_ref[:, slot : slot + 1], shape) for slot in range(slots)]
    for block in range(out_ref.shape[0]):
        total = jnp.zeros(shape, F32)
        for place, term in zip(places, terms):
            total = total + jnp.where(place == block, term, 0.0)
        out_ref[block] = total.astype(BF16)


def on_device(cal_source, cal_target, app_source, readers, blocks, interp):
    frames = lax.axis_size("frame")
    segs = lax.axis_size("seg")
    coil_count = lax.axis_size("coil")
    held, samples, depth = cal_source.shape
    coils = cal_target.shape[1]
    width = depth // 2
    part = width // coil_count
    gram_rows = part + part // 2
    rows = gram_rows + 3 * coils + 8
    slots = readers.shape[1]
    cells = interp.shape[2]

    each = held // 2
    block = jax.ShapeDtypeStruct((each, rows, LANES), F32)
    listed = pltpu.with_memory_space_constraint(readers, pltpu.HBM)
    hbm = pl.BlockSpec(memory_space=pltpu.HBM)
    vmem = pl.BlockSpec(memory_space=pltpu.VMEM)
    reading = [pltpu.SMEM(readers.shape, jnp.int32)]
    turned = pltpu.VMEM((each, depth, samples), BF16)
    cost = pl.CostEstimate(
        flops=2 * each * samples * depth * 2 * (part + coils),
        bytes_accessed=2 * each * samples * (depth + 2 * coils),
        transcendentals=0,
    )
    send, own_held, own_goal, own_app, own_interp = pl.pallas_call(
        functools.partial(other_gram_kernel, part, frames),
        in_specs=[hbm] * 5,
        out_shape=[
            block,
            jax.ShapeDtypeStruct((each, samples, depth), BF16),
            jax.ShapeDtypeStruct((each, coils, 2, samples), BF16),
            jax.ShapeDtypeStruct(app_source.shape, BF16),
            jax.ShapeDtypeStruct(interp.shape, BF16),
        ],
        scratch_shapes=[
            pltpu.VMEM((each, samples, depth), BF16),
            pltpu.VMEM((each, coils, 2, samples), BF16),
            turned,
            *reading,
            pltpu.SemaphoreType.DMA((2, held)),
            pltpu.SemaphoreType.DMA((3,)),
        ],
        compiler_params=SMALL,
        cost_estimate=cost,
    )(
        listed,
        pltpu.with_memory_space_constraint(cal_source, pltpu.HBM),
        pltpu.with_memory_space_constraint(cal_target, pltpu.HBM),
        pltpu.with_memory_space_constraint(app_source, pltpu.HBM),
        pltpu.with_memory_space_constraint(interp, pltpu.HBM),
    )
    keep = pl.pallas_call(
        functools.partial(own_gram_kernel, part, frames),
        in_specs=[hbm, vmem, vmem],
        out_shape=block,
        scratch_shapes=[turned, *reading, pltpu.SemaphoreType.DMA],
        compiler_params=SMALL,
        cost_estimate=cost,
    )(listed, own_held, own_goal)
    other = lax.ppermute(send, "frame", [(frame, frame ^ 1) for frame in range(frames)])
    chips = [[2 * chip + core for chip in range(frames // 2)] for core in range(2)]
    received = lax.all_to_all(
        keep + other, "frame", 0, 0, tiled=True, axis_index_groups=chips
    )
    spread, rhs, told = pl.pallas_call(
        functools.partial(sum_kernel, gram_rows),
        out_shape=[
            jax.ShapeDtypeStruct((coil_count, gram_rows, LANES), F32),
            jax.ShapeDtypeStruct((3 * coils, LANES), F32),
            jax.ShapeDtypeStruct((frames, LANES), jnp.int32),
        ],
        compiler_params=SMALL,
    )(received)
    gram = lax.all_to_all(spread, "coil", 0, 0, tiled=True)
    weights = pl.pallas_call(
        functools.partial(solve_kernel, part),
        out_shape=jax.ShapeDtypeStruct((segs, coils, depth), BF16),
        scratch_shapes=[
            pltpu.VMEM((width, width), F32),
            pltpu.VMEM((width, width), F32),
            pltpu.VMEM((2 * coils, width), F32),
        ],
        compiler_params=SMALL,
    )(gram, rhs)
    pieces = lax.all_to_all(weights, "seg", 0, 0, tiled=True)
    sent = pl.pallas_call(
        select_kernel,
        out_shape=jax.ShapeDtypeStruct((frames, slots, coils, depth), BF16),
        compiler_params=SMALL,
    )(told, pieces)
    chosen = lax.all_to_all(sent, "frame", 0, 0, tiled=True)
    grid = pl.pallas_call(
        fill_kernel,
        out_shape=jax.ShapeDtypeStruct((segs, 2 * coils, cells), BF16),
        compiler_params=SMALL,
    )(readers, blocks, chosen, own_app, own_interp)
    terms = lax.all_to_all(grid, "seg", 0, 0, tiled=True)
    total = jnp.sum(terms.astype(F32), axis=0)
    power = lax.all_gather(jnp.sum(total * total, axis=0, keepdims=True), "coil", tiled=True)
    return jnp.sqrt(jnp.sum(power, axis=0, keepdims=True) + epsilon)


def solution(mesh):
    placed = (
        P("seg", "frame", None),
        P("seg", "coil", None, "frame"),
        P("frame", "seg", None, None),
        P("frame", "seg"),
        P("frame", "seg"),
        P("frame", "seg", None, None),
    )
    return jax.shard_map(
        on_device, mesh=mesh, in_specs=placed, out_specs=P("frame", "seg"), check_vma=False
    )
```

```python
import functools

import jax
import jax.numpy as jnp
from jax import lax
from jax.experimental import pallas as pl
from jax.experimental.pallas import tpu as pltpu
from jax.sharding import PartitionSpec as P

regular = 0.02
epsilon = 1e-06
settled = 0.0125
F32 = jnp.float32
BF16 = jnp.bfloat16
LANES = 128
SMALL = pltpu.CompilerParams(vmem_limit_bytes=16 * 1024 * 1024)


def across_rows(left, right):
    return lax.dot_general(left, right, (((1,), (1,)), ((), ())), preferred_element_type=F32)


def pieces_of(value, count):
    out = []
    for _ in range(count):
        piece = value.astype(BF16)
        value = value - piece.astype(F32)
        out.append(piece)
    return out


def product(left, right):
    rows = left.shape[0]
    a, b = pieces_of(left, 2), pieces_of(right, 2)
    dot = functools.partial(jnp.dot, preferred_element_type=F32)
    first = dot(jnp.concatenate(a, axis=0), b[0])
    return first[:rows] + (first[rows:] + dot(a[0], b[1]))


def fine_product(left, right):
    rows = left.shape[0]
    a, b = pieces_of(left, 3), pieces_of(right, 3)
    dot = functools.partial(jnp.dot, preferred_element_type=F32)
    first = dot(jnp.concatenate(a, axis=0), b[0])
    second = dot(jnp.concatenate(a[:2], axis=0), b[1])
    return first[:rows] + (
        (first[rows : 2 * rows] + second[:rows])
        + (first[2 * rows :] + (second[rows:] + dot(a[0], b[2])))
    )


def gram_sums(part, groups, picked, held_ref, goal_ref, turned_ref, out_ref, copies):
    coil = lax.axis_index("coil")
    depth = held_ref.shape[2]
    width = depth // 2
    half = part // 2
    base = part + half
    coils = goal_ref.shape[1]
    across = lax.broadcasted_iota(jnp.int32, (part, width), 1)
    down = lax.broadcasted_iota(jnp.int32, (part, width), 0) + coil * part
    first = pl.multiple_of(coil * part, 16)
    second = pl.multiple_of(width + coil * part, 16)
    row = lax.broadcasted_iota(jnp.int32, (2 * part, depth), 0)
    column = lax.broadcasted_iota(jnp.int32, (2 * part, depth), 1)
    wanted = coil * part + jnp.where(row < part, row, row - part + width)
    pick = jnp.where(column == wanted, 1.0, 0.0).astype(BF16)
    for slots in groups:
        for slot in slots:
            for copy in copies[slot]:
                copy.wait()
        lefts = []
        for slot in slots:
            if slot in picked:
                mine = [across_rows(pick, held_ref[slot]).astype(BF16)]
            else:
                turned_ref[slot] = held_ref[slot].T
                mine = [
                    turned_ref[slot, pl.ds(first, part)],
                    turned_ref[slot, pl.ds(second, part)],
                ]
            lefts.append(
                jnp.concatenate([*mine, goal_ref[slot, :, 0, :], goal_ref[slot, :, 1, :]], axis=0)
            )
        products = [
            jnp.dot(left, held_ref[slot], preferred_element_type=F32)
            for left, slot in zip(lefts, slots)
        ]
        for slot, sums in zip(slots, products):
            out = out_ref.at[slot]
            top, bottom = sums[:part], sums[part : 2 * part]
            gram_real = top[:, :width] + bottom[:, width:]
            gram_imag = top[:, width:] - bottom[:, :width]
            packed = jnp.where(across <= down, gram_real, gram_imag)
            proj_real = sums[2 * part : 2 * part + coils]
            proj_imag = sums[2 * part + coils :]
            rhs_real = proj_real[:, :width] + proj_imag[:, width:]
            rhs_imag = proj_imag[:, :width] - proj_real[:, width:]
            out[:part] = packed[:, :LANES]
            out[part:base] = jnp.concatenate(
                [packed[:half, LANES:], packed[half:, LANES:]], axis=1
            )
            out[base : base + coils] = rhs_real[:, :LANES]
            out[base + coils : base + 2 * coils] = rhs_imag[:, :LANES]
            out[base + 2 * coils : base + 3 * coils] = jnp.concatenate(
                [rhs_real[:, LANES:], rhs_imag[:, LANES:]], axis=1
            )


def tell(frames, read_ref, out_ref):
    core = lax.rem(lax.axis_index("frame"), 2)
    row = lax.broadcasted_iota(jnp.int32, (8, LANES), 0)
    lane = lax.broadcasted_iota(jnp.int32, (8, LANES), 1)
    told = jnp.zeros((8, LANES), jnp.int32)
    for place in range(read_ref.shape[1]):
        told = jnp.where((row == core) & (lane == place), lax.div(read_ref[0, place], frames), told)
    for slot in range(out_ref.shape[0]):
        out_ref[slot, out_ref.shape[1] - 8 :] = told.astype(F32)


def other_gram_kernel(
    part,
    frames,
    reads_ref,
    source_ref,
    target_ref,
    app_ref,
    interp_ref,
    out_ref,
    own_held_ref,
    own_goal_ref,
    own_app_ref,
    own_interp_ref,
    held_ref,
    goal_ref,
    turned_ref,
    read_ref,
    sem,
    late_sem,
):
    core = lax.rem(lax.axis_index("frame"), 2)
    each = out_ref.shape[0]
    copies = []
    for slot in range(2 * each):
        own, place = slot // each, slot % each
        segment = 2 * place + (core if own else 1 - core)
        held = (own_held_ref if own else held_ref).at[place]
        goal = (own_goal_ref if own else goal_ref).at[place]
        copies.append(
            (
                pltpu.make_async_copy(source_ref.at[segment], held, sem.at[0, slot]),
                pltpu.make_async_copy(target_ref.at[segment], goal, sem.at[1, slot]),
            )
        )
    for pair in copies:
        for copy in pair:
            copy.start()
    late = [
        pltpu.make_async_copy(reads_ref, read_ref, late_sem.at[0]),
        pltpu.make_async_copy(app_ref, own_app_ref, late_sem.at[1]),
        pltpu.make_async_copy(interp_ref, own_interp_ref, late_sem.at[2]),
    ]
    for copy in late:
        copy.start()
    gram_sums(part, ((0,), (1, 2, 3)), (), held_ref, goal_ref, turned_ref, out_ref, copies)
    late[0].wait()
    tell(frames, read_ref, out_ref)
    for copy in late[1:]:
        copy.wait()
    for pair in copies[each:]:
        for copy in pair:
            copy.wait()


def own_gram_kernel(
    part, frames, reads_ref, held_ref, goal_ref, app_ref, out_ref, flipped_ref, turned_ref, read_ref, read_sem
):
    listing = pltpu.make_async_copy(reads_ref, read_ref, read_sem)
    listing.start()
    slots = tuple(range(out_ref.shape[0]))
    for slot in range(app_ref.shape[1]):
        flipped_ref[0, slot] = app_ref[0, slot].T
    gram_sums(part, (slots,), (2,), held_ref, goal_ref, turned_ref, out_ref, [() for _ in slots])
    listing.wait()
    tell(frames, read_ref, out_ref)


def sum_kernel(gram_rows, partial_ref, spread_ref, rhs_ref, told_ref):
    rows = gram_rows + rhs_ref.shape[0]
    total = partial_ref[0, :rows]
    for chip in range(1, partial_ref.shape[0]):
        total = total + partial_ref[chip, :rows]
    for copy in range(spread_ref.shape[0]):
        spread_ref[copy] = total[:gram_rows]
    rhs_ref[...] = total[gram_rows:]
    for chip in range(partial_ref.shape[0]):
        told_ref[2 * chip : 2 * chip + 2] = partial_ref[chip, rows : rows + 2].astype(jnp.int32)


def solve_kernel(part, gram_ref, rhs_ref, out_ref, real_ref, imag_ref, sol_ref):
    width = 4 * part
    half = part // 2
    coils = rhs_ref.shape[0] // 3
    pieces = []
    for coil in range(4):
        block = gram_ref[coil]
        tail = block[part:]
        pieces.append(
            jnp.concatenate(
                [block[:part], jnp.concatenate([tail[:, :64], tail[:, 64:]], axis=0)], axis=1
            )
        )
    packed = jnp.concatenate(pieces, axis=0)
    flipped = packed.T
    down = lax.broadcasted_iota(jnp.int32, (width, width), 0)
    across = lax.broadcasted_iota(jnp.int32, (width, width), 1)
    diagonal = jnp.where(across == down, packed, 0.0)
    shift = regular / width * jnp.sum(diagonal, keepdims=True)
    norm = jnp.sum(2.0 * (packed * packed) - diagonal * diagonal, keepdims=True)
    high = jnp.sqrt(norm) + shift
    scale = 2.0 / (high + shift)
    real = jnp.where(across <= down, packed, flipped)
    imag = jnp.where(across < down, -flipped, packed)
    real_ref[...] = (real + jnp.where(across == down, shift, 0.0)) * scale
    imag_ref[...] = jnp.where(across == down, 0.0, imag) * scale
    rhs_real = jnp.concatenate([rhs_ref[:coils], rhs_ref[2 * coils :, :64]], axis=1)
    rhs_imag = jnp.concatenate([rhs_ref[coils : 2 * coils], rhs_ref[2 * coils :, 64:]], axis=1)
    sol_ref[...] = jnp.concatenate([rhs_real, rhs_imag], axis=0) * scale

    def step(product, spread):
        square = spread * spread
        factor = 2.0 / (2.0 - square)
        real, imag, sol = real_ref[...], imag_ref[...], sol_ref[...]
        first = product(jnp.concatenate([real, sol], axis=0), imag)
        second = product(jnp.concatenate([real - imag, sol], axis=0), real + imag)
        cross, thin = first[:width], first[width:]
        turned = cross.T
        by_real = second[width:] - thin
        change = jnp.concatenate(
            [by_real[:coils] + thin[coils:], by_real[coils:] - thin[:coils]], axis=0
        )
        sol_ref[...] = factor * (2.0 * sol - change)
        real_ref[...] = factor * (2.0 * real - (second[:width] - cross - turned))
        imag_ref[...] = factor * (2.0 * imag - (cross - turned))
        return square / (2.0 - square)

    spread = jnp.sum((high - shift) / (high + shift))
    spread = lax.while_loop(
        lambda spread: spread > 0.99, functools.partial(step, fine_product), spread
    )
    spread = lax.while_loop(
        lambda spread: spread > settled, functools.partial(step, product), spread
    )
    sol = sol_ref[...]
    total = sol
    for _ in range(2):
        by_real = product(total, real_ref[...])
        by_imag = product(total, imag_ref[...])
        change = jnp.concatenate(
            [by_real[:coils] + by_imag[coils:], by_real[coils:] - by_imag[:coils]], axis=0
        )
        total = sol + (total - change)
    sol = total
    weights = jnp.concatenate([sol[:coils], sol[coils:]], axis=1).astype(BF16)
    for copy in range(out_ref.shape[0]):
        out_ref[copy] = weights


def select_kernel(told_ref, piece_ref, out_ref):
    pieces = [piece_ref[place].astype(F32) for place in range(piece_ref.shape[0])]
    for frame in range(out_ref.shape[0]):
        for slot in range(out_ref.shape[1]):
            wanted = jnp.broadcast_to(told_ref[frame : frame + 1, slot : slot + 1], pieces[0].shape)
            chosen = pieces[0]
            for place in range(1, len(pieces)):
                chosen = jnp.where(wanted == place, pieces[place], chosen)
            out_ref[frame, slot] = chosen.astype(BF16)


def fill_kernel(reads_ref, places_ref, weights_ref, source_ref, interp_ref, out_ref):
    frames, slots, coils, depth = weights_ref.shape
    width = depth // 2
    terms = []
    for slot in range(slots):
        holder = jnp.broadcast_to(reads_ref[:, slot : slot + 1] & (frames - 1), (coils, depth))
        chosen = weights_ref[0, slot].astype(F32)
        for frame in range(1, frames):
            chosen = jnp.where(holder == frame, weights_ref[frame, slot].astype(F32), chosen)
        real, imag = chosen[:, :width], chosen[:, width:]
        matrix = jnp.concatenate(
            [jnp.concatenate([real, -imag], axis=1), jnp.concatenate([imag, real], axis=1)], axis=0
        ).astype(BF16)
        filled = jnp.dot(matrix, source_ref[0, slot], preferred_element_type=F32).astype(BF16)
        terms.append(across_rows(filled, interp_ref[0, slot]))
    shape = terms[0].shape
    places = [jnp.broadcast_to(places_ref[:, slot : slot + 1], shape) for slot in range(slots)]
    for block in range(out_ref.shape[0]):
        total = jnp.zeros(shape, F32)
        for place, term in zip(places, terms):
            total = total + jnp.where(place == block, term, 0.0)
        out_ref[block] = total.astype(BF16)


def on_device(cal_source, cal_target, app_source, readers, blocks, interp):
    frames = lax.axis_size("frame")
    segs = lax.axis_size("seg")
    coil_count = lax.axis_size("coil")
    held, samples, depth = cal_source.shape
    coils = cal_target.shape[1]
    width = depth // 2
    part = width // coil_count
    gram_rows = part + part // 2
    rows = gram_rows + 3 * coils + 8
    slots = readers.shape[1]
    cells = interp.shape[2]

    each = held // 2
    block = jax.ShapeDtypeStruct((each, rows, LANES), F32)
    listed = pltpu.with_memory_space_constraint(readers, pltpu.HBM)
    hbm = pl.BlockSpec(memory_space=pltpu.HBM)
    vmem = pl.BlockSpec(memory_space=pltpu.VMEM)
    reading = [pltpu.SMEM(readers.shape, jnp.int32)]
    turned = pltpu.VMEM((each, depth, samples), BF16)
    cost = pl.CostEstimate(
        flops=2 * each * samples * depth * 2 * (part + coils),
        bytes_accessed=2 * each * samples * (depth + 2 * coils),
        transcendentals=0,
    )
    send, own_held, own_goal, own_app, own_interp = pl.pallas_call(
        functools.partial(other_gram_kernel, part, frames),
        in_specs=[hbm] * 5,
        out_shape=[
            block,
            jax.ShapeDtypeStruct((each, samples, depth), BF16),
            jax.ShapeDtypeStruct((each, coils, 2, samples), BF16),
            jax.ShapeDtypeStruct(app_source.shape, BF16),
            jax.ShapeDtypeStruct(interp.shape, BF16),
        ],
        scratch_shapes=[
            pltpu.VMEM((each, samples, depth), BF16),
            pltpu.VMEM((each, coils, 2, samples), BF16),
            turned,
            *reading,
            pltpu.SemaphoreType.DMA((2, held)),
            pltpu.SemaphoreType.DMA((3,)),
        ],
        compiler_params=SMALL,
        cost_estimate=cost,
    )(
        listed,
        pltpu.with_memory_space_constraint(cal_source, pltpu.HBM),
        pltpu.with_memory_space_constraint(cal_target, pltpu.HBM),
        pltpu.with_memory_space_constraint(app_source, pltpu.HBM),
        pltpu.with_memory_space_constraint(interp, pltpu.HBM),
    )
    keep, flipped = pl.pallas_call(
        functools.partial(own_gram_kernel, part, frames),
        in_specs=[hbm, vmem, vmem, vmem],
        out_shape=[
            block,
            jax.ShapeDtypeStruct((1, slots, depth, app_source.shape[2]), BF16),
        ],
        scratch_shapes=[turned, *reading, pltpu.SemaphoreType.DMA],
        compiler_params=SMALL,
        cost_estimate=cost,
    )(listed, own_held, own_goal, own_app)
    other = lax.ppermute(send, "frame", [(frame, frame ^ 1) for frame in range(frames)])
    chips = [[2 * chip + core for chip in range(frames // 2)] for core in range(2)]
    received = lax.all_to_all(
        keep + other, "frame", 0, 0, tiled=True, axis_index_groups=chips
    )
    spread, rhs, told = pl.pallas_call(
        functools.partial(sum_kernel, gram_rows),
        out_shape=[
            jax.ShapeDtypeStruct((coil_count, gram_rows, LANES), F32),
            jax.ShapeDtypeStruct((3 * coils, LANES), F32),
            jax.ShapeDtypeStruct((frames, LANES), jnp.int32),
        ],
        compiler_params=SMALL,
    )(received)
    gram = lax.all_to_all(spread, "coil", 0, 0, tiled=True)
    weights = pl.pallas_call(
        functools.partial(solve_kernel, part),
        out_shape=jax.ShapeDtypeStruct((segs, coils, depth), BF16),
        scratch_shapes=[
            pltpu.VMEM((width, width), F32),
            pltpu.VMEM((width, width), F32),
            pltpu.VMEM((2 * coils, width), F32),
        ],
        compiler_params=SMALL,
    )(gram, rhs)
    pieces = lax.all_to_all(weights, "seg", 0, 0, tiled=True)
    sent = pl.pallas_call(
        select_kernel,
        out_shape=jax.ShapeDtypeStruct((frames, slots, coils, depth), BF16),
        compiler_params=SMALL,
    )(told, pieces)
    chosen = lax.all_to_all(sent, "frame", 0, 0, tiled=True)
    grid = pl.pallas_call(
        fill_kernel,
        out_shape=jax.ShapeDtypeStruct((segs, 2 * coils, cells), BF16),
        compiler_params=SMALL,
    )(readers, blocks, chosen, flipped, own_interp)
    terms = lax.all_to_all(grid, "seg", 0, 0, tiled=True)
    total = jnp.sum(terms.astype(F32), axis=0)
    power = lax.all_gather(jnp.sum(total * total, axis=0, keepdims=True), "coil", tiled=True)
    return jnp.sqrt(jnp.sum(power, axis=0, keepdims=True) + epsilon)


def solution(mesh):
    placed = (
        P("seg", "frame", None),
        P("seg", "coil", None, "frame"),
        P("frame", "seg", None, None),
        P("frame", "seg"),
        P("frame", "seg"),
        P("frame", "seg", None, None),
    )
    return jax.shard_map(
        on_device, mesh=mesh, in_specs=placed, out_specs=P("frame", "seg"), check_vma=False
    )
```

```python
import functools

import jax
import jax.numpy as jnp
from jax import lax
from jax.experimental import pallas as pl
from jax.experimental.pallas import tpu as pltpu
from jax.sharding import PartitionSpec as P

regular = 0.02
epsilon = 1e-06
settled = 0.0125
F32 = jnp.float32
BF16 = jnp.bfloat16
LANES = 128
SMALL = pltpu.CompilerParams(vmem_limit_bytes=16 * 1024 * 1024)


def across_rows(left, right):
    return lax.dot_general(left, right, (((1,), (1,)), ((), ())), preferred_element_type=F32)


def pieces_of(value, count):
    out = []
    for _ in range(count):
        piece = value.astype(BF16)
        value = value - piece.astype(F32)
        out.append(piece)
    return out


def product(left, right):
    rows = left.shape[0]
    a, b = pieces_of(left, 2), pieces_of(right, 2)
    dot = functools.partial(jnp.dot, preferred_element_type=F32)
    first = dot(jnp.concatenate(a, axis=0), b[0])
    return first[:rows] + (first[rows:] + dot(a[0], b[1]))


def fine_product(left, right):
    rows = left.shape[0]
    a, b = pieces_of(left, 3), pieces_of(right, 3)
    dot = functools.partial(jnp.dot, preferred_element_type=F32)
    first = dot(jnp.concatenate(a, axis=0), b[0])
    second = dot(jnp.concatenate(a[:2], axis=0), b[1])
    return first[:rows] + (
        (first[rows : 2 * rows] + second[:rows])
        + (first[2 * rows :] + (second[rows:] + dot(a[0], b[2])))
    )


def gram_sums(part, groups, picked, held_ref, goal_ref, turned_ref, out_ref, copies, beside=None):
    coil = lax.axis_index("coil")
    depth = held_ref.shape[2]
    width = depth // 2
    half = part // 2
    base = part + half
    coils = goal_ref.shape[1]
    across = lax.broadcasted_iota(jnp.int32, (part, width), 1)
    down = lax.broadcasted_iota(jnp.int32, (part, width), 0) + coil * part
    first = pl.multiple_of(coil * part, 16)
    second = pl.multiple_of(width + coil * part, 16)
    row = lax.broadcasted_iota(jnp.int32, (2 * part, depth), 0)
    column = lax.broadcasted_iota(jnp.int32, (2 * part, depth), 1)
    wanted = coil * part + jnp.where(row < part, row, row - part + width)
    pick = jnp.where(column == wanted, 1.0, 0.0).astype(BF16)
    for slots in groups:
        for slot in slots:
            for copy in copies[slot]:
                copy.wait()
        if beside is not None and slots is groups[0]:
            beside()
        lefts = []
        for slot in slots:
            if slot in picked:
                mine = [across_rows(pick, held_ref[slot]).astype(BF16)]
            else:
                turned_ref[slot] = held_ref[slot].T
                mine = [
                    turned_ref[slot, pl.ds(first, part)],
                    turned_ref[slot, pl.ds(second, part)],
                ]
            lefts.append(
                jnp.concatenate([*mine, goal_ref[slot, :, 0, :], goal_ref[slot, :, 1, :]], axis=0)
            )
        products = [
            jnp.dot(left, held_ref[slot], preferred_element_type=F32)
            for left, slot in zip(lefts, slots)
        ]
        for slot, sums in zip(slots, products):
            out = out_ref.at[slot]
            top, bottom = sums[:part], sums[part : 2 * part]
            gram_real = top[:, :width] + bottom[:, width:]
            gram_imag = top[:, width:] - bottom[:, :width]
            packed = jnp.where(across <= down, gram_real, gram_imag)
            proj_real = sums[2 * part : 2 * part + coils]
            proj_imag = sums[2 * part + coils :]
            rhs_real = proj_real[:, :width] + proj_imag[:, width:]
            rhs_imag = proj_imag[:, :width] - proj_real[:, width:]
            out[:part] = packed[:, :LANES]
            out[part:base] = jnp.concatenate(
                [packed[:half, LANES:], packed[half:, LANES:]], axis=1
            )
            out[base : base + coils] = rhs_real[:, :LANES]
            out[base + coils : base + 2 * coils] = rhs_imag[:, :LANES]
            out[base + 2 * coils : base + 3 * coils] = jnp.concatenate(
                [rhs_real[:, LANES:], rhs_imag[:, LANES:]], axis=1
            )


def tell(frames, read_ref, out_ref):
    core = lax.rem(lax.axis_index("frame"), 2)
    row = lax.broadcasted_iota(jnp.int32, (8, LANES), 0)
    lane = lax.broadcasted_iota(jnp.int32, (8, LANES), 1)
    told = jnp.zeros((8, LANES), jnp.int32)
    for place in range(read_ref.shape[1]):
        told = jnp.where((row == core) & (lane == place), lax.div(read_ref[0, place], frames), told)
    for slot in range(out_ref.shape[0]):
        out_ref[slot, out_ref.shape[1] - 8 :] = told.astype(F32)


def other_gram_kernel(
    part,
    frames,
    reads_ref,
    source_ref,
    target_ref,
    app_ref,
    interp_ref,
    out_ref,
    own_held_ref,
    own_goal_ref,
    flipped_ref,
    own_interp_ref,
    held_ref,
    goal_ref,
    turned_ref,
    own_app_ref,
    read_ref,
    sem,
    late_sem,
):
    core = lax.rem(lax.axis_index("frame"), 2)
    each = out_ref.shape[0]
    copies = []
    for slot in range(2 * each):
        own, place = slot // each, slot % each
        segment = 2 * place + (core if own else 1 - core)
        held = (own_held_ref if own else held_ref).at[place]
        goal = (own_goal_ref if own else goal_ref).at[place]
        copies.append(
            (
                pltpu.make_async_copy(source_ref.at[segment], held, sem.at[0, slot]),
                pltpu.make_async_copy(target_ref.at[segment], goal, sem.at[1, slot]),
            )
        )
    app_copy = pltpu.make_async_copy(app_ref, own_app_ref, late_sem.at[1])
    for slot, pair in enumerate(copies):
        for copy in pair:
            copy.start()
        if slot == 0:
            app_copy.start()
    late = [
        pltpu.make_async_copy(reads_ref, read_ref, late_sem.at[0]),
        pltpu.make_async_copy(interp_ref, own_interp_ref, late_sem.at[2]),
    ]
    for copy in late:
        copy.start()

    def turn():
        app_copy.wait()
        for slot in range(own_app_ref.shape[1]):
            flipped_ref[0, slot] = own_app_ref[0, slot].T

    gram_sums(part, ((0,), (1, 2, 3)), (), held_ref, goal_ref, turned_ref, out_ref, copies, turn)
    late[0].wait()
    tell(frames, read_ref, out_ref)
    late[1].wait()
    for pair in copies[each:]:
        for copy in pair:
            copy.wait()


def own_gram_kernel(part, frames, reads_ref, held_ref, goal_ref, out_ref, turned_ref, read_ref, read_sem):
    listing = pltpu.make_async_copy(reads_ref, read_ref, read_sem)
    listing.start()
    slots = tuple(range(out_ref.shape[0]))
    gram_sums(part, (slots,), (2,), held_ref, goal_ref, turned_ref, out_ref, [() for _ in slots])
    listing.wait()
    tell(frames, read_ref, out_ref)


def sum_kernel(gram_rows, partial_ref, spread_ref, rhs_ref, told_ref):
    rows = gram_rows + rhs_ref.shape[0]
    total = partial_ref[0, :rows]
    for chip in range(1, partial_ref.shape[0]):
        total = total + partial_ref[chip, :rows]
    for copy in range(spread_ref.shape[0]):
        spread_ref[copy] = total[:gram_rows]
    rhs_ref[...] = total[gram_rows:]
    for chip in range(partial_ref.shape[0]):
        told_ref[2 * chip : 2 * chip + 2] = partial_ref[chip, rows : rows + 2].astype(jnp.int32)


def solve_kernel(part, gram_ref, rhs_ref, out_ref, real_ref, imag_ref, sol_ref):
    width = 4 * part
    half = part // 2
    coils = rhs_ref.shape[0] // 3
    pieces = []
    for coil in range(4):
        block = gram_ref[coil]
        tail = block[part:]
        pieces.append(
            jnp.concatenate(
                [block[:part], jnp.concatenate([tail[:, :64], tail[:, 64:]], axis=0)], axis=1
            )
        )
    packed = jnp.concatenate(pieces, axis=0)
    flipped = packed.T
    down = lax.broadcasted_iota(jnp.int32, (width, width), 0)
    across = lax.broadcasted_iota(jnp.int32, (width, width), 1)
    diagonal = jnp.where(across == down, packed, 0.0)
    shift = regular / width * jnp.sum(diagonal, keepdims=True)
    norm = jnp.sum(2.0 * (packed * packed) - diagonal * diagonal, keepdims=True)
    high = jnp.sqrt(norm) + shift
    scale = 2.0 / (high + shift)
    real = jnp.where(across <= down, packed, flipped)
    imag = jnp.where(across < down, -flipped, packed)
    real_ref[...] = (real + jnp.where(across == down, shift, 0.0)) * scale
    imag_ref[...] = jnp.where(across == down, 0.0, imag) * scale
    rhs_real = jnp.concatenate([rhs_ref[:coils], rhs_ref[2 * coils :, :64]], axis=1)
    rhs_imag = jnp.concatenate([rhs_ref[coils : 2 * coils], rhs_ref[2 * coils :, 64:]], axis=1)
    sol_ref[...] = jnp.concatenate([rhs_real, rhs_imag], axis=0) * scale

    def step(product, spread):
        square = spread * spread
        factor = 2.0 / (2.0 - square)
        real, imag, sol = real_ref[...], imag_ref[...], sol_ref[...]
        first = product(jnp.concatenate([real, sol], axis=0), imag)
        second = product(jnp.concatenate([real - imag, sol], axis=0), real + imag)
        cross, thin = first[:width], first[width:]
        turned = cross.T
        by_real = second[width:] - thin
        change = jnp.concatenate(
            [by_real[:coils] + thin[coils:], by_real[coils:] - thin[:coils]], axis=0
        )
        sol_ref[...] = factor * (2.0 * sol - change)
        real_ref[...] = factor * (2.0 * real - (second[:width] - cross - turned))
        imag_ref[...] = factor * (2.0 * imag - (cross - turned))
        return square / (2.0 - square)

    spread = jnp.sum((high - shift) / (high + shift))
    spread = lax.while_loop(
        lambda spread: spread > 0.99, functools.partial(step, fine_product), spread
    )
    spread = lax.while_loop(
        lambda spread: spread > settled, functools.partial(step, product), spread
    )
    sol = sol_ref[...]
    total = sol
    for _ in range(2):
        by_real = product(total, real_ref[...])
        by_imag = product(total, imag_ref[...])
        change = jnp.concatenate(
            [by_real[:coils] + by_imag[coils:], by_real[coils:] - by_imag[:coils]], axis=0
        )
        total = sol + (total - change)
    sol = total
    weights = jnp.concatenate([sol[:coils], sol[coils:]], axis=1).astype(BF16)
    for copy in range(out_ref.shape[0]):
        out_ref[copy] = weights


def select_kernel(told_ref, piece_ref, out_ref):
    pieces = [piece_ref[place].astype(F32) for place in range(piece_ref.shape[0])]
    for frame in range(out_ref.shape[0]):
        for slot in range(out_ref.shape[1]):
            wanted = jnp.broadcast_to(told_ref[frame : frame + 1, slot : slot + 1], pieces[0].shape)
            chosen = pieces[0]
            for place in range(1, len(pieces)):
                chosen = jnp.where(wanted == place, pieces[place], chosen)
            out_ref[frame, slot] = chosen.astype(BF16)


def fill_kernel(reads_ref, places_ref, weights_ref, source_ref, interp_ref, out_ref):
    frames, slots, coils, depth = weights_ref.shape
    width = depth // 2
    terms = []
    for slot in range(slots):
        holder = jnp.broadcast_to(reads_ref[:, slot : slot + 1] & (frames - 1), (coils, depth))
        chosen = weights_ref[0, slot].astype(F32)
        for frame in range(1, frames):
            chosen = jnp.where(holder == frame, weights_ref[frame, slot].astype(F32), chosen)
        real, imag = chosen[:, :width], chosen[:, width:]
        matrix = jnp.concatenate(
            [jnp.concatenate([real, -imag], axis=1), jnp.concatenate([imag, real], axis=1)], axis=0
        ).astype(BF16)
        filled = jnp.dot(matrix, source_ref[0, slot], preferred_element_type=F32).astype(BF16)
        terms.append(across_rows(filled, interp_ref[0, slot]))
    shape = terms[0].shape
    places = [jnp.broadcast_to(places_ref[:, slot : slot + 1], shape) for slot in range(slots)]
    for block in range(out_ref.shape[0]):
        total = jnp.zeros(shape, F32)
        for place, term in zip(places, terms):
            total = total + jnp.where(place == block, term, 0.0)
        out_ref[block] = total.astype(BF16)


def on_device(cal_source, cal_target, app_source, readers, blocks, interp):
    frames = lax.axis_size("frame")
    segs = lax.axis_size("seg")
    coil_count = lax.axis_size("coil")
    held, samples, depth = cal_source.shape
    coils = cal_target.shape[1]
    width = depth // 2
    part = width // coil_count
    gram_rows = part + part // 2
    rows = gram_rows + 3 * coils + 8
    slots = readers.shape[1]
    cells = interp.shape[2]

    each = held // 2
    block = jax.ShapeDtypeStruct((each, rows, LANES), F32)
    listed = pltpu.with_memory_space_constraint(readers, pltpu.HBM)
    hbm = pl.BlockSpec(memory_space=pltpu.HBM)
    vmem = pl.BlockSpec(memory_space=pltpu.VMEM)
    reading = [pltpu.SMEM(readers.shape, jnp.int32)]
    turned = pltpu.VMEM((each, depth, samples), BF16)
    cost = pl.CostEstimate(
        flops=2 * each * samples * depth * 2 * (part + coils),
        bytes_accessed=2 * each * samples * (depth + 2 * coils),
        transcendentals=0,
    )
    send, own_held, own_goal, flipped, own_interp = pl.pallas_call(
        functools.partial(other_gram_kernel, part, frames),
        in_specs=[hbm] * 5,
        out_shape=[
            block,
            jax.ShapeDtypeStruct((each, samples, depth), BF16),
            jax.ShapeDtypeStruct((each, coils, 2, samples), BF16),
            jax.ShapeDtypeStruct((1, slots, depth, app_source.shape[2]), BF16),
            jax.ShapeDtypeStruct(interp.shape, BF16),
        ],
        scratch_shapes=[
            pltpu.VMEM((each, samples, depth), BF16),
            pltpu.VMEM((each, coils, 2, samples), BF16),
            turned,
            pltpu.VMEM(app_source.shape, BF16),
            *reading,
            pltpu.SemaphoreType.DMA((2, held)),
            pltpu.SemaphoreType.DMA((3,)),
        ],
        compiler_params=SMALL,
        cost_estimate=cost,
    )(
        listed,
        pltpu.with_memory_space_constraint(cal_source, pltpu.HBM),
        pltpu.with_memory_space_constraint(cal_target, pltpu.HBM),
        pltpu.with_memory_space_constraint(app_source, pltpu.HBM),
        pltpu.with_memory_space_constraint(interp, pltpu.HBM),
    )
    keep = pl.pallas_call(
        functools.partial(own_gram_kernel, part, frames),
        in_specs=[hbm, vmem, vmem],
        out_shape=block,
        scratch_shapes=[turned, *reading, pltpu.SemaphoreType.DMA],
        compiler_params=SMALL,
        cost_estimate=cost,
    )(listed, own_held, own_goal)
    other = lax.ppermute(send, "frame", [(frame, frame ^ 1) for frame in range(frames)])
    chips = [[2 * chip + core for chip in range(frames // 2)] for core in range(2)]
    received = lax.all_to_all(
        keep + other, "frame", 0, 0, tiled=True, axis_index_groups=chips
    )
    spread, rhs, told = pl.pallas_call(
        functools.partial(sum_kernel, gram_rows),
        out_shape=[
            jax.ShapeDtypeStruct((coil_count, gram_rows, LANES), F32),
            jax.ShapeDtypeStruct((3 * coils, LANES), F32),
            jax.ShapeDtypeStruct((frames, LANES), jnp.int32),
        ],
        compiler_params=SMALL,
    )(received)
    gram = lax.all_to_all(spread, "coil", 0, 0, tiled=True)
    weights = pl.pallas_call(
        functools.partial(solve_kernel, part),
        out_shape=jax.ShapeDtypeStruct((segs, coils, depth), BF16),
        scratch_shapes=[
            pltpu.VMEM((width, width), F32),
            pltpu.VMEM((width, width), F32),
            pltpu.VMEM((2 * coils, width), F32),
        ],
        compiler_params=SMALL,
    )(gram, rhs)
    pieces = lax.all_to_all(weights, "seg", 0, 0, tiled=True)
    sent = pl.pallas_call(
        select_kernel,
        out_shape=jax.ShapeDtypeStruct((frames, slots, coils, depth), BF16),
        compiler_params=SMALL,
    )(told, pieces)
    chosen = lax.all_to_all(sent, "frame", 0, 0, tiled=True)
    grid = pl.pallas_call(
        fill_kernel,
        out_shape=jax.ShapeDtypeStruct((segs, 2 * coils, cells), BF16),
        compiler_params=SMALL,
    )(readers, blocks, chosen, flipped, own_interp)
    terms = lax.all_to_all(grid, "seg", 0, 0, tiled=True)
    total = jnp.sum(terms.astype(F32), axis=0)
    power = lax.all_gather(jnp.sum(total * total, axis=0, keepdims=True), "coil", tiled=True)
    return jnp.sqrt(jnp.sum(power, axis=0, keepdims=True) + epsilon)


def solution(mesh):
    placed = (
        P("seg", "frame", None),
        P("seg", "coil", None, "frame"),
        P("frame", "seg", None, None),
        P("frame", "seg"),
        P("frame", "seg"),
        P("frame", "seg", None, None),
    )
    return jax.shard_map(
        on_device, mesh=mesh, in_specs=placed, out_specs=P("frame", "seg"), check_vma=False
    )
```

```python
import functools

import jax
import jax.numpy as jnp
from jax import lax
from jax.experimental import pallas as pl
from jax.experimental.pallas import tpu as pltpu
from jax.sharding import PartitionSpec as P

regular = 0.02
epsilon = 1e-06
settled = 0.0125
F32 = jnp.float32
BF16 = jnp.bfloat16
LANES = 128
SMALL = pltpu.CompilerParams(vmem_limit_bytes=16 * 1024 * 1024)


def across_rows(left, right):
    return lax.dot_general(left, right, (((1,), (1,)), ((), ())), preferred_element_type=F32)


def pieces_of(value, count):
    out = []
    for _ in range(count):
        piece = value.astype(BF16)
        value = value - piece.astype(F32)
        out.append(piece)
    return out


def product(left, right):
    rows = left.shape[0]
    a, b = pieces_of(left, 2), pieces_of(right, 2)
    dot = functools.partial(jnp.dot, preferred_element_type=F32)
    first = dot(jnp.concatenate(a, axis=0), b[0])
    return first[:rows] + (first[rows:] + dot(a[0], b[1]))


def fine_product(left, right):
    rows = left.shape[0]
    a, b = pieces_of(left, 3), pieces_of(right, 3)
    dot = functools.partial(jnp.dot, preferred_element_type=F32)
    first = dot(jnp.concatenate(a, axis=0), b[0])
    second = dot(jnp.concatenate(a[:2], axis=0), b[1])
    return first[:rows] + (
        (first[rows : 2 * rows] + second[:rows])
        + (first[2 * rows :] + (second[rows:] + dot(a[0], b[2])))
    )


def gram_sums(part, groups, picked, held_ref, goal_ref, turned_ref, out_ref, copies):
    coil = lax.axis_index("coil")
    depth = held_ref.shape[2]
    width = depth // 2
    half = part // 2
    base = part + half
    coils = goal_ref.shape[1]
    across = lax.broadcasted_iota(jnp.int32, (part, width), 1)
    down = lax.broadcasted_iota(jnp.int32, (part, width), 0) + coil * part
    first = pl.multiple_of(coil * part, 16)
    second = pl.multiple_of(width + coil * part, 16)
    row = lax.broadcasted_iota(jnp.int32, (2 * part, depth), 0)
    column = lax.broadcasted_iota(jnp.int32, (2 * part, depth), 1)
    wanted = coil * part + jnp.where(row < part, row, row - part + width)
    pick = jnp.where(column == wanted, 1.0, 0.0).astype(BF16)
    for slots in groups:
        for slot in slots:
            for copy in copies[slot]:
                copy.wait()
        lefts = []
        for slot in slots:
            if slot in picked:
                mine = [across_rows(pick, held_ref[slot]).astype(BF16)]
            else:
                turned_ref[slot] = held_ref[slot].T
                mine = [
                    turned_ref[slot, pl.ds(first, part)],
                    turned_ref[slot, pl.ds(second, part)],
                ]
            lefts.append(
                jnp.concatenate([*mine, goal_ref[slot, :, 0, :], goal_ref[slot, :, 1, :]], axis=0)
            )
        products = [
            jnp.dot(left, held_ref[slot], preferred_element_type=F32)
            for left, slot in zip(lefts, slots)
        ]
        for slot, sums in zip(slots, products):
            out = out_ref.at[slot]
            top, bottom = sums[:part], sums[part : 2 * part]
            gram_real = top[:, :width] + bottom[:, width:]
            gram_imag = top[:, width:] - bottom[:, :width]
            packed = jnp.where(across <= down, gram_real, gram_imag)
            proj_real = sums[2 * part : 2 * part + coils]
            proj_imag = sums[2 * part + coils :]
            rhs_real = proj_real[:, :width] + proj_imag[:, width:]
            rhs_imag = proj_imag[:, :width] - proj_real[:, width:]
            out[:part] = packed[:, :LANES]
            out[part:base] = jnp.concatenate(
                [packed[:half, LANES:], packed[half:, LANES:]], axis=1
            )
            out[base : base + coils] = rhs_real[:, :LANES]
            out[base + coils : base + 2 * coils] = rhs_imag[:, :LANES]
            out[base + 2 * coils : base + 3 * coils] = jnp.concatenate(
                [rhs_real[:, LANES:], rhs_imag[:, LANES:]], axis=1
            )


def tell(frames, read_ref, out_ref):
    core = lax.rem(lax.axis_index("frame"), 2)
    row = lax.broadcasted_iota(jnp.int32, (8, LANES), 0)
    lane = lax.broadcasted_iota(jnp.int32, (8, LANES), 1)
    told = jnp.zeros((8, LANES), jnp.int32)
    for place in range(read_ref.shape[1]):
        told = jnp.where((row == core) & (lane == place), lax.div(read_ref[0, place], frames), told)
    for slot in range(out_ref.shape[0]):
        out_ref[slot, out_ref.shape[1] - 8 :] = told.astype(F32)


def other_gram_kernel(
    part,
    frames,
    reads_ref,
    source_ref,
    target_ref,
    app_ref,
    interp_ref,
    out_ref,
    own_held_ref,
    own_goal_ref,
    own_app_ref,
    own_interp_ref,
    held_ref,
    goal_ref,
    turned_ref,
    read_ref,
    sem,
    late_sem,
):
    core = lax.rem(lax.axis_index("frame"), 2)
    each = out_ref.shape[0]
    copies = []
    for slot in range(2 * each):
        own, place = slot // each, slot % each
        segment = 2 * place + (core if own else 1 - core)
        held = (own_held_ref if own else held_ref).at[place]
        goal = (own_goal_ref if own else goal_ref).at[place]
        copies.append(
            (
                pltpu.make_async_copy(source_ref.at[segment], held, sem.at[0, slot]),
                pltpu.make_async_copy(target_ref.at[segment], goal, sem.at[1, slot]),
            )
        )
    for pair in copies:
        for copy in pair:
            copy.start()
    late = [
        pltpu.make_async_copy(reads_ref, read_ref, late_sem.at[0]),
        pltpu.make_async_copy(app_ref, own_app_ref, late_sem.at[1]),
        pltpu.make_async_copy(interp_ref, own_interp_ref, late_sem.at[2]),
    ]
    for copy in late:
        copy.start()
    gram_sums(part, ((0,), (1, 2, 3)), (), held_ref, goal_ref, turned_ref, out_ref, copies)
    late[0].wait()
    tell(frames, read_ref, out_ref)
    for copy in late[1:]:
        copy.wait()
    for pair in copies[each:]:
        for copy in pair:
            copy.wait()


def own_gram_kernel(part, frames, reads_ref, held_ref, goal_ref, out_ref, turned_ref, read_ref, read_sem):
    listing = pltpu.make_async_copy(reads_ref, read_ref, read_sem)
    listing.start()
    slots = tuple(range(out_ref.shape[0]))
    gram_sums(part, (slots,), (2,), held_ref, goal_ref, turned_ref, out_ref, [() for _ in slots])
    listing.wait()
    tell(frames, read_ref, out_ref)


def sum_kernel(gram_rows, partial_ref, spread_ref, rhs_ref, told_ref):
    rows = gram_rows + rhs_ref.shape[0]
    total = partial_ref[0, :rows]
    for chip in range(1, partial_ref.shape[0]):
        total = total + partial_ref[chip, :rows]
    for copy in range(spread_ref.shape[0]):
        spread_ref[copy] = total[:gram_rows]
    rhs_ref[...] = total[gram_rows:]
    for chip in range(partial_ref.shape[0]):
        told_ref[2 * chip : 2 * chip + 2] = partial_ref[chip, rows : rows + 2].astype(jnp.int32)


def solve_kernel(part, gram_ref, rhs_ref, app_ref, out_ref, flipped_ref, real_ref, imag_ref, sol_ref):
    width = 4 * part
    half = part // 2
    coils = rhs_ref.shape[0] // 3
    pieces = []
    for coil in range(4):
        block = gram_ref[coil]
        tail = block[part:]
        pieces.append(
            jnp.concatenate(
                [block[:part], jnp.concatenate([tail[:, :64], tail[:, 64:]], axis=0)], axis=1
            )
        )
    packed = jnp.concatenate(pieces, axis=0)
    flipped = packed.T
    down = lax.broadcasted_iota(jnp.int32, (width, width), 0)
    across = lax.broadcasted_iota(jnp.int32, (width, width), 1)
    diagonal = jnp.where(across == down, packed, 0.0)
    for slot in range(app_ref.shape[1]):
        flipped_ref[0, slot] = app_ref[0, slot].T
    shift = regular / width * jnp.sum(diagonal, keepdims=True)
    norm = jnp.sum(2.0 * (packed * packed) - diagonal * diagonal, keepdims=True)
    high = jnp.sqrt(norm) + shift
    scale = 2.0 / (high + shift)
    real = jnp.where(across <= down, packed, flipped)
    imag = jnp.where(across < down, -flipped, packed)
    real_ref[...] = (real + jnp.where(across == down, shift, 0.0)) * scale
    imag_ref[...] = jnp.where(across == down, 0.0, imag) * scale
    rhs_real = jnp.concatenate([rhs_ref[:coils], rhs_ref[2 * coils :, :64]], axis=1)
    rhs_imag = jnp.concatenate([rhs_ref[coils : 2 * coils], rhs_ref[2 * coils :, 64:]], axis=1)
    sol_ref[...] = jnp.concatenate([rhs_real, rhs_imag], axis=0) * scale

    def step(product, spread):
        square = spread * spread
        factor = 2.0 / (2.0 - square)
        real, imag, sol = real_ref[...], imag_ref[...], sol_ref[...]
        first = product(jnp.concatenate([real, sol], axis=0), imag)
        second = product(jnp.concatenate([real - imag, sol], axis=0), real + imag)
        cross, thin = first[:width], first[width:]
        turned = cross.T
        by_real = second[width:] - thin
        change = jnp.concatenate(
            [by_real[:coils] + thin[coils:], by_real[coils:] - thin[:coils]], axis=0
        )
        sol_ref[...] = factor * (2.0 * sol - change)
        real_ref[...] = factor * (2.0 * real - (second[:width] - cross - turned))
        imag_ref[...] = factor * (2.0 * imag - (cross - turned))
        return square / (2.0 - square)

    spread = jnp.sum((high - shift) / (high + shift))
    spread = lax.while_loop(
        lambda spread: spread > 0.998, functools.partial(step, fine_product), spread
    )
    spread = lax.while_loop(
        lambda spread: spread > settled, functools.partial(step, product), spread
    )
    sol = sol_ref[...]
    total = sol
    for _ in range(2):
        by_real = product(total, real_ref[...])
        by_imag = product(total, imag_ref[...])
        change = jnp.concatenate(
            [by_real[:coils] + by_imag[coils:], by_real[coils:] - by_imag[:coils]], axis=0
        )
        total = sol + (total - change)
    sol = total
    weights = jnp.concatenate([sol[:coils], sol[coils:]], axis=1).astype(BF16)
    for copy in range(out_ref.shape[0]):
        out_ref[copy] = weights


def select_kernel(told_ref, piece_ref, out_ref):
    pieces = [piece_ref[place].astype(F32) for place in range(piece_ref.shape[0])]
    for frame in range(out_ref.shape[0]):
        for slot in range(out_ref.shape[1]):
            wanted = jnp.broadcast_to(told_ref[frame : frame + 1, slot : slot + 1], pieces[0].shape)
            chosen = pieces[0]
            for place in range(1, len(pieces)):
                chosen = jnp.where(wanted == place, pieces[place], chosen)
            out_ref[frame, slot] = chosen.astype(BF16)


def fill_kernel(reads_ref, places_ref, weights_ref, source_ref, interp_ref, out_ref):
    frames, slots, coils, depth = weights_ref.shape
    width = depth // 2
    terms = []
    for slot in range(slots):
        holder = jnp.broadcast_to(reads_ref[:, slot : slot + 1] & (frames - 1), (coils, depth))
        chosen = weights_ref[0, slot].astype(F32)
        for frame in range(1, frames):
            chosen = jnp.where(holder == frame, weights_ref[frame, slot].astype(F32), chosen)
        real, imag = chosen[:, :width], chosen[:, width:]
        matrix = jnp.concatenate(
            [jnp.concatenate([real, -imag], axis=1), jnp.concatenate([imag, real], axis=1)], axis=0
        ).astype(BF16)
        filled = jnp.dot(matrix, source_ref[0, slot], preferred_element_type=F32).astype(BF16)
        terms.append(across_rows(filled, interp_ref[0, slot]))
    shape = terms[0].shape
    places = [jnp.broadcast_to(places_ref[:, slot : slot + 1], shape) for slot in range(slots)]
    for block in range(out_ref.shape[0]):
        total = jnp.zeros(shape, F32)
        for place, term in zip(places, terms):
            total = total + jnp.where(place == block, term, 0.0)
        out_ref[block] = total.astype(BF16)


def on_device(cal_source, cal_target, app_source, readers, blocks, interp):
    frames = lax.axis_size("frame")
    segs = lax.axis_size("seg")
    coil_count = lax.axis_size("coil")
    held, samples, depth = cal_source.shape
    coils = cal_target.shape[1]
    width = depth // 2
    part = width // coil_count
    gram_rows = part + part // 2
    rows = gram_rows + 3 * coils + 8
    slots = readers.shape[1]
    cells = interp.shape[2]

    each = held // 2
    block = jax.ShapeDtypeStruct((each, rows, LANES), F32)
    listed = pltpu.with_memory_space_constraint(readers, pltpu.HBM)
    hbm = pl.BlockSpec(memory_space=pltpu.HBM)
    vmem = pl.BlockSpec(memory_space=pltpu.VMEM)
    reading = [pltpu.SMEM(readers.shape, jnp.int32)]
    turned = pltpu.VMEM((each, depth, samples), BF16)
    cost = pl.CostEstimate(
        flops=2 * each * samples * depth * 2 * (part + coils),
        bytes_accessed=2 * each * samples * (depth + 2 * coils),
        transcendentals=0,
    )
    send, own_held, own_goal, own_app, own_interp = pl.pallas_call(
        functools.partial(other_gram_kernel, part, frames),
        in_specs=[hbm] * 5,
        out_shape=[
            block,
            jax.ShapeDtypeStruct((each, samples, depth), BF16),
            jax.ShapeDtypeStruct((each, coils, 2, samples), BF16),
            jax.ShapeDtypeStruct(app_source.shape, BF16),
            jax.ShapeDtypeStruct(interp.shape, BF16),
        ],
        scratch_shapes=[
            pltpu.VMEM((each, samples, depth), BF16),
            pltpu.VMEM((each, coils, 2, samples), BF16),
            turned,
            *reading,
            pltpu.SemaphoreType.DMA((2, held)),
            pltpu.SemaphoreType.DMA((3,)),
        ],
        compiler_params=SMALL,
        cost_estimate=cost,
    )(
        listed,
        pltpu.with_memory_space_constraint(cal_source, pltpu.HBM),
        pltpu.with_memory_space_constraint(cal_target, pltpu.HBM),
        pltpu.with_memory_space_constraint(app_source, pltpu.HBM),
        pltpu.with_memory_space_constraint(interp, pltpu.HBM),
    )
    keep = pl.pallas_call(
        functools.partial(own_gram_kernel, part, frames),
        in_specs=[hbm, vmem, vmem],
        out_shape=block,
        scratch_shapes=[turned, *reading, pltpu.SemaphoreType.DMA],
        compiler_params=SMALL,
        cost_estimate=cost,
    )(listed, own_held, own_goal)
    other = lax.ppermute(send, "frame", [(frame, frame ^ 1) for frame in range(frames)])
    chips = [[2 * chip + core for chip in range(frames // 2)] for core in range(2)]
    received = lax.all_to_all(
        keep + other, "frame", 0, 0, tiled=True, axis_index_groups=chips
    )
    spread, rhs, told = pl.pallas_call(
        functools.partial(sum_kernel, gram_rows),
        out_shape=[
            jax.ShapeDtypeStruct((coil_count, gram_rows, LANES), F32),
            jax.ShapeDtypeStruct((3 * coils, LANES), F32),
            jax.ShapeDtypeStruct((frames, LANES), jnp.int32),
        ],
        compiler_params=SMALL,
    )(received)
    gram = lax.all_to_all(spread, "coil", 0, 0, tiled=True)
    weights, flipped = pl.pallas_call(
        functools.partial(solve_kernel, part),
        out_shape=[
            jax.ShapeDtypeStruct((segs, coils, depth), BF16),
            jax.ShapeDtypeStruct((1, slots, depth, app_source.shape[2]), BF16),
        ],
        scratch_shapes=[
            pltpu.VMEM((width, width), F32),
            pltpu.VMEM((width, width), F32),
            pltpu.VMEM((2 * coils, width), F32),
        ],
        compiler_params=SMALL,
    )(gram, rhs, own_app)
    pieces = lax.all_to_all(weights, "seg", 0, 0, tiled=True)
    sent = pl.pallas_call(
        select_kernel,
        out_shape=jax.ShapeDtypeStruct((frames, slots, coils, depth), BF16),
        compiler_params=SMALL,
    )(told, pieces)
    chosen = lax.all_to_all(sent, "frame", 0, 0, tiled=True)
    grid = pl.pallas_call(
        fill_kernel,
        out_shape=jax.ShapeDtypeStruct((segs, 2 * coils, cells), BF16),
        compiler_params=SMALL,
    )(readers, blocks, chosen, flipped, own_interp)
    terms = lax.all_to_all(grid, "seg", 0, 0, tiled=True)
    total = jnp.sum(terms.astype(F32), axis=0)
    power = lax.all_gather(jnp.sum(total * total, axis=0, keepdims=True), "coil", tiled=True)
    return jnp.sqrt(jnp.sum(power, axis=0, keepdims=True) + epsilon)


def solution(mesh):
    placed = (
        P("seg", "frame", None),
        P("seg", "coil", None, "frame"),
        P("frame", "seg", None, None),
        P("frame", "seg"),
        P("frame", "seg"),
        P("frame", "seg", None, None),
    )
    return jax.shard_map(
        on_device, mesh=mesh, in_specs=placed, out_specs=P("frame", "seg"), check_vma=False
    )
```

```python
import functools

import jax
import jax.numpy as jnp
from jax import lax
from jax.experimental import pallas as pl
from jax.experimental.pallas import tpu as pltpu
from jax.sharding import PartitionSpec as P

regular = 0.02
epsilon = 1e-06
settled = 0.0125
F32 = jnp.float32
BF16 = jnp.bfloat16
LANES = 128
CHIPS = (0, 3, 1, 2)
SMALL = pltpu.CompilerParams(vmem_limit_bytes=16 * 1024 * 1024)


def across_rows(left, right):
    return lax.dot_general(left, right, (((1,), (1,)), ((), ())), preferred_element_type=F32)


def pieces_of(value, count):
    out = []
    for _ in range(count):
        piece = value.astype(BF16)
        value = value - piece.astype(F32)
        out.append(piece)
    return out


def product(left, right):
    rows = left.shape[0]
    a, b = pieces_of(left, 2), pieces_of(right, 2)
    dot = functools.partial(jnp.dot, preferred_element_type=F32)
    first = dot(jnp.concatenate(a, axis=0), b[0])
    return first[:rows] + (first[rows:] + dot(a[0], b[1]))


def fine_product(left, right):
    rows = left.shape[0]
    a, b = pieces_of(left, 3), pieces_of(right, 3)
    dot = functools.partial(jnp.dot, preferred_element_type=F32)
    first = dot(jnp.concatenate(a, axis=0), b[0])
    second = dot(jnp.concatenate(a[:2], axis=0), b[1])
    return first[:rows] + (
        (first[rows : 2 * rows] + second[:rows])
        + (first[2 * rows :] + (second[rows:] + dot(a[0], b[2])))
    )


def gram_sums(part, groups, picked, held_ref, goal_ref, turned_ref, out_ref, copies):
    coil = lax.axis_index("coil")
    depth = held_ref.shape[2]
    width = depth // 2
    half = part // 2
    base = part + half
    coils = goal_ref.shape[1]
    across = lax.broadcasted_iota(jnp.int32, (part, width), 1)
    down = lax.broadcasted_iota(jnp.int32, (part, width), 0) + coil * part
    first = pl.multiple_of(coil * part, 16)
    second = pl.multiple_of(width + coil * part, 16)
    row = lax.broadcasted_iota(jnp.int32, (2 * part, depth), 0)
    column = lax.broadcasted_iota(jnp.int32, (2 * part, depth), 1)
    wanted = coil * part + jnp.where(row < part, row, row - part + width)
    pick = jnp.where(column == wanted, 1.0, 0.0).astype(BF16)
    for slots in groups:
        for slot in slots:
            for copy in copies[slot]:
                copy.wait()
        lefts = []
        for slot in slots:
            if slot in picked:
                mine = [across_rows(pick, held_ref[slot]).astype(BF16)]
            else:
                turned_ref[slot] = held_ref[slot].T
                mine = [
                    turned_ref[slot, pl.ds(first, part)],
                    turned_ref[slot, pl.ds(second, part)],
                ]
            lefts.append(
                jnp.concatenate([*mine, goal_ref[slot, :, 0, :], goal_ref[slot, :, 1, :]], axis=0)
            )
        products = [
            jnp.dot(left, held_ref[slot], preferred_element_type=F32)
            for left, slot in zip(lefts, slots)
        ]
        for slot, sums in zip(slots, products):
            out = out_ref.at[slot]
            top, bottom = sums[:part], sums[part : 2 * part]
            gram_real = top[:, :width] + bottom[:, width:]
            gram_imag = top[:, width:] - bottom[:, :width]
            packed = jnp.where(across <= down, gram_real, gram_imag)
            proj_real = sums[2 * part : 2 * part + coils]
            proj_imag = sums[2 * part + coils :]
            rhs_real = proj_real[:, :width] + proj_imag[:, width:]
            rhs_imag = proj_imag[:, :width] - proj_real[:, width:]
            out[:part] = packed[:, :LANES]
            out[part:base] = jnp.concatenate(
                [packed[:half, LANES:], packed[half:, LANES:]], axis=1
            )
            out[base : base + coils] = rhs_real[:, :LANES]
            out[base + coils : base + 2 * coils] = rhs_imag[:, :LANES]
            out[base + 2 * coils : base + 3 * coils] = jnp.concatenate(
                [rhs_real[:, LANES:], rhs_imag[:, LANES:]], axis=1
            )


def tell(frames, read_ref, out_ref):
    core = lax.rem(lax.axis_index("frame"), 2)
    row = lax.broadcasted_iota(jnp.int32, (8, LANES), 0)
    lane = lax.broadcasted_iota(jnp.int32, (8, LANES), 1)
    told = jnp.zeros((8, LANES), jnp.int32)
    for place in range(read_ref.shape[1]):
        told = jnp.where((row == core) & (lane == place), lax.div(read_ref[0, place], frames), told)
    for slot in range(out_ref.shape[0]):
        out_ref[slot, out_ref.shape[1] - 8 :] = told.astype(F32)


def other_gram_kernel(
    part,
    frames,
    reads_ref,
    source_ref,
    target_ref,
    app_ref,
    interp_ref,
    out_ref,
    own_held_ref,
    own_goal_ref,
    own_app_ref,
    own_interp_ref,
    held_ref,
    goal_ref,
    turned_ref,
    read_ref,
    sem,
    late_sem,
):
    core = lax.rem(lax.axis_index("frame"), 2)
    each = out_ref.shape[0]
    copies = []
    for slot in range(2 * each):
        own, place = slot // each, slot % each
        segment = 2 * CHIPS[place] + (core if own else 1 - core)
        held = (own_held_ref if own else held_ref).at[place]
        goal = (own_goal_ref if own else goal_ref).at[place]
        copies.append(
            (
                pltpu.make_async_copy(source_ref.at[segment], held, sem.at[0, slot]),
                pltpu.make_async_copy(target_ref.at[segment], goal, sem.at[1, slot]),
            )
        )
    for pair in copies:
        for copy in pair:
            copy.start()
    late = [
        pltpu.make_async_copy(reads_ref, read_ref, late_sem.at[0]),
        pltpu.make_async_copy(app_ref, own_app_ref, late_sem.at[1]),
        pltpu.make_async_copy(interp_ref, own_interp_ref, late_sem.at[2]),
    ]
    for copy in late:
        copy.start()
    gram_sums(part, ((0,), (1, 2, 3)), (), held_ref, goal_ref, turned_ref, out_ref, copies)
    late[0].wait()
    tell(frames, read_ref, out_ref)
    for copy in late[1:]:
        copy.wait()
    for pair in copies[each:]:
        for copy in pair:
            copy.wait()


def own_gram_kernel(part, frames, reads_ref, held_ref, goal_ref, out_ref, turned_ref, read_ref, read_sem):
    listing = pltpu.make_async_copy(reads_ref, read_ref, read_sem)
    listing.start()
    slots = tuple(range(out_ref.shape[0]))
    gram_sums(part, (slots,), (2,), held_ref, goal_ref, turned_ref, out_ref, [() for _ in slots])
    listing.wait()
    tell(frames, read_ref, out_ref)


def sum_kernel(gram_rows, partial_ref, spread_ref, rhs_ref, told_ref):
    rows = gram_rows + rhs_ref.shape[0]
    total = partial_ref[0, :rows]
    for chip in range(1, partial_ref.shape[0]):
        total = total + partial_ref[chip, :rows]
    for copy in range(spread_ref.shape[0]):
        spread_ref[copy] = total[:gram_rows]
    rhs_ref[...] = total[gram_rows:]
    for place, chip in enumerate(CHIPS):
        told_ref[2 * chip : 2 * chip + 2] = partial_ref[place, rows : rows + 2].astype(jnp.int32)


def solve_kernel(part, gram_ref, rhs_ref, app_ref, out_ref, flipped_ref, real_ref, imag_ref, sol_ref):
    width = 4 * part
    half = part // 2
    coils = rhs_ref.shape[0] // 3
    pieces = []
    for coil in range(4):
        block = gram_ref[coil]
        tail = block[part:]
        pieces.append(
            jnp.concatenate(
                [block[:part], jnp.concatenate([tail[:, :64], tail[:, 64:]], axis=0)], axis=1
            )
        )
    packed = jnp.concatenate(pieces, axis=0)
    flipped = packed.T
    down = lax.broadcasted_iota(jnp.int32, (width, width), 0)
    across = lax.broadcasted_iota(jnp.int32, (width, width), 1)
    diagonal = jnp.where(across == down, packed, 0.0)
    for slot in range(app_ref.shape[1]):
        flipped_ref[0, slot] = app_ref[0, slot].T
    shift = regular / width * jnp.sum(diagonal, keepdims=True)
    norm = jnp.sum(2.0 * (packed * packed) - diagonal * diagonal, keepdims=True)
    high = jnp.sqrt(norm) + shift
    scale = 2.0 / (high + shift)
    real = jnp.where(across <= down, packed, flipped)
    imag = jnp.where(across < down, -flipped, packed)
    real_ref[...] = (real + jnp.where(across == down, shift, 0.0)) * scale
    imag_ref[...] = jnp.where(across == down, 0.0, imag) * scale
    rhs_real = jnp.concatenate([rhs_ref[:coils], rhs_ref[2 * coils :, :64]], axis=1)
    rhs_imag = jnp.concatenate([rhs_ref[coils : 2 * coils], rhs_ref[2 * coils :, 64:]], axis=1)
    sol_ref[...] = jnp.concatenate([rhs_real, rhs_imag], axis=0) * scale

    def step(product, spread):
        square = spread * spread
        factor = 2.0 / (2.0 - square)
        real, imag, sol = real_ref[...], imag_ref[...], sol_ref[...]
        first = product(jnp.concatenate([real, sol], axis=0), imag)
        second = product(jnp.concatenate([real - imag, sol], axis=0), real + imag)
        cross, thin = first[:width], first[width:]
        turned = cross.T
        by_real = second[width:] - thin
        change = jnp.concatenate(
            [by_real[:coils] + thin[coils:], by_real[coils:] - thin[:coils]], axis=0
        )
        sol_ref[...] = factor * (2.0 * sol - change)
        real_ref[...] = factor * (2.0 * real - (second[:width] - cross - turned))
        imag_ref[...] = factor * (2.0 * imag - (cross - turned))
        return square / (2.0 - square)

    spread = jnp.sum((high - shift) / (high + shift))
    spread = lax.while_loop(
        lambda spread: spread > 0.998, functools.partial(step, fine_product), spread
    )
    spread = lax.while_loop(
        lambda spread: spread > settled, functools.partial(step, product), spread
    )
    sol = sol_ref[...]
    total = sol
    for _ in range(2):
        by_real = product(total, real_ref[...])
        by_imag = product(total, imag_ref[...])
        change = jnp.concatenate(
            [by_real[:coils] + by_imag[coils:], by_real[coils:] - by_imag[:coils]], axis=0
        )
        total = sol + (total - change)
    sol = total
    weights = jnp.concatenate([sol[:coils], sol[coils:]], axis=1).astype(BF16)
    for copy in range(out_ref.shape[0]):
        out_ref[copy] = weights


def select_kernel(told_ref, piece_ref, out_ref):
    pieces = [piece_ref[place].astype(F32) for place in range(piece_ref.shape[0])]
    for frame in range(out_ref.shape[0]):
        for slot in range(out_ref.shape[1]):
            wanted = jnp.broadcast_to(told_ref[frame : frame + 1, slot : slot + 1], pieces[0].shape)
            chosen = pieces[0]
            for place in range(1, len(pieces)):
                chosen = jnp.where(wanted == place, pieces[place], chosen)
            out_ref[frame, slot] = chosen.astype(BF16)


def fill_kernel(reads_ref, places_ref, weights_ref, source_ref, interp_ref, out_ref):
    frames, slots, coils, depth = weights_ref.shape
    width = depth // 2
    terms = []
    for slot in range(slots):
        holder = jnp.broadcast_to(reads_ref[:, slot : slot + 1] & (frames - 1), (coils, depth))
        chosen = weights_ref[0, slot].astype(F32)
        for frame in range(1, frames):
            chosen = jnp.where(holder == frame, weights_ref[frame, slot].astype(F32), chosen)
        real, imag = chosen[:, :width], chosen[:, width:]
        matrix = jnp.concatenate(
            [jnp.concatenate([real, -imag], axis=1), jnp.concatenate([imag, real], axis=1)], axis=0
        ).astype(BF16)
        filled = jnp.dot(matrix, source_ref[0, slot], preferred_element_type=F32).astype(BF16)
        terms.append(across_rows(filled, interp_ref[0, slot]))
    shape = terms[0].shape
    places = [jnp.broadcast_to(places_ref[:, slot : slot + 1], shape) for slot in range(slots)]
    for block in range(out_ref.shape[0]):
        total = jnp.zeros(shape, F32)
        for place, term in zip(places, terms):
            total = total + jnp.where(place == block, term, 0.0)
        out_ref[block] = total.astype(BF16)


def on_device(cal_source, cal_target, app_source, readers, blocks, interp):
    frames = lax.axis_size("frame")
    segs = lax.axis_size("seg")
    coil_count = lax.axis_size("coil")
    held, samples, depth = cal_source.shape
    coils = cal_target.shape[1]
    width = depth // 2
    part = width // coil_count
    gram_rows = part + part // 2
    rows = gram_rows + 3 * coils + 8
    slots = readers.shape[1]
    cells = interp.shape[2]

    each = held // 2
    block = jax.ShapeDtypeStruct((each, rows, LANES), F32)
    listed = pltpu.with_memory_space_constraint(readers, pltpu.HBM)
    hbm = pl.BlockSpec(memory_space=pltpu.HBM)
    vmem = pl.BlockSpec(memory_space=pltpu.VMEM)
    reading = [pltpu.SMEM(readers.shape, jnp.int32)]
    turned = pltpu.VMEM((each, depth, samples), BF16)
    cost = pl.CostEstimate(
        flops=2 * each * samples * depth * 2 * (part + coils),
        bytes_accessed=2 * each * samples * (depth + 2 * coils),
        transcendentals=0,
    )
    send, own_held, own_goal, own_app, own_interp = pl.pallas_call(
        functools.partial(other_gram_kernel, part, frames),
        in_specs=[hbm] * 5,
        out_shape=[
            block,
            jax.ShapeDtypeStruct((each, samples, depth), BF16),
            jax.ShapeDtypeStruct((each, coils, 2, samples), BF16),
            jax.ShapeDtypeStruct(app_source.shape, BF16),
            jax.ShapeDtypeStruct(interp.shape, BF16),
        ],
        scratch_shapes=[
            pltpu.VMEM((each, samples, depth), BF16),
            pltpu.VMEM((each, coils, 2, samples), BF16),
            turned,
            *reading,
            pltpu.SemaphoreType.DMA((2, held)),
            pltpu.SemaphoreType.DMA((3,)),
        ],
        compiler_params=SMALL,
        cost_estimate=cost,
    )(
        listed,
        pltpu.with_memory_space_constraint(cal_source, pltpu.HBM),
        pltpu.with_memory_space_constraint(cal_target, pltpu.HBM),
        pltpu.with_memory_space_constraint(app_source, pltpu.HBM),
        pltpu.with_memory_space_constraint(interp, pltpu.HBM),
    )
    keep = pl.pallas_call(
        functools.partial(own_gram_kernel, part, frames),
        in_specs=[hbm, vmem, vmem],
        out_shape=block,
        scratch_shapes=[turned, *reading, pltpu.SemaphoreType.DMA],
        compiler_params=SMALL,
        cost_estimate=cost,
    )(listed, own_held, own_goal)
    other = lax.ppermute(send, "frame", [(frame, frame ^ 1) for frame in range(frames)])
    chips = [[2 * chip + core for chip in CHIPS] for core in range(2)]
    received = lax.all_to_all(
        keep + other, "frame", 0, 0, tiled=True, axis_index_groups=chips
    )
    spread, rhs, told = pl.pallas_call(
        functools.partial(sum_kernel, gram_rows),
        out_shape=[
            jax.ShapeDtypeStruct((coil_count, gram_rows, LANES), F32),
            jax.ShapeDtypeStruct((3 * coils, LANES), F32),
            jax.ShapeDtypeStruct((frames, LANES), jnp.int32),
        ],
        compiler_params=SMALL,
    )(received)
    gram = lax.all_to_all(spread, "coil", 0, 0, tiled=True)
    weights, flipped = pl.pallas_call(
        functools.partial(solve_kernel, part),
        out_shape=[
            jax.ShapeDtypeStruct((segs, coils, depth), BF16),
            jax.ShapeDtypeStruct((1, slots, depth, app_source.shape[2]), BF16),
        ],
        scratch_shapes=[
            pltpu.VMEM((width, width), F32),
            pltpu.VMEM((width, width), F32),
            pltpu.VMEM((2 * coils, width), F32),
        ],
        compiler_params=SMALL,
    )(gram, rhs, own_app)
    pieces = lax.all_to_all(weights, "seg", 0, 0, tiled=True)
    sent = pl.pallas_call(
        select_kernel,
        out_shape=jax.ShapeDtypeStruct((frames, slots, coils, depth), BF16),
        compiler_params=SMALL,
    )(told, pieces)
    chosen = lax.all_to_all(sent, "frame", 0, 0, tiled=True)
    grid = pl.pallas_call(
        fill_kernel,
        out_shape=jax.ShapeDtypeStruct((segs, 2 * coils, cells), BF16),
        compiler_params=SMALL,
    )(readers, blocks, chosen, flipped, own_interp)
    terms = lax.all_to_all(grid, "seg", 0, 0, tiled=True)
    total = jnp.sum(terms.astype(F32), axis=0)
    power = lax.all_gather(jnp.sum(total * total, axis=0, keepdims=True), "coil", tiled=True)
    return jnp.sqrt(jnp.sum(power, axis=0, keepdims=True) + epsilon)


def solution(mesh):
    placed = (
        P("seg", "frame", None),
        P("seg", "coil", None, "frame"),
        P("frame", "seg", None, None),
        P("frame", "seg"),
        P("frame", "seg"),
        P("frame", "seg", None, None),
    )
    return jax.shard_map(
        on_device, mesh=mesh, in_specs=placed, out_specs=P("frame", "seg"), check_vma=False
    )
```

```python
import functools

import jax
import jax.numpy as jnp
from jax import lax
from jax.experimental import pallas as pl
from jax.experimental.pallas import tpu as pltpu
from jax.sharding import PartitionSpec as P

regular = 0.02
epsilon = 1e-06
settled = 0.0125
F32 = jnp.float32
BF16 = jnp.bfloat16
LANES = 128
SMALL = pltpu.CompilerParams(vmem_limit_bytes=16 * 1024 * 1024)


def across_rows(left, right):
    return lax.dot_general(left, right, (((1,), (1,)), ((), ())), preferred_element_type=F32)


def pieces_of(value, count):
    out = []
    for _ in range(count):
        piece = value.astype(BF16)
        value = value - piece.astype(F32)
        out.append(piece)
    return out


def product(left, right):
    rows = left.shape[0]
    a, b = pieces_of(left, 2), pieces_of(right, 2)
    dot = functools.partial(jnp.dot, preferred_element_type=F32)
    first = dot(jnp.concatenate(a, axis=0), b[0])
    return first[:rows] + (first[rows:] + dot(a[0], b[1]))


def fine_product(left, right):
    rows = left.shape[0]
    a, b = pieces_of(left, 3), pieces_of(right, 3)
    dot = functools.partial(jnp.dot, preferred_element_type=F32)
    first = dot(jnp.concatenate(a, axis=0), b[0])
    second = dot(jnp.concatenate(a[:2], axis=0), b[1])
    return first[:rows] + (
        (first[rows : 2 * rows] + second[:rows])
        + (first[2 * rows :] + (second[rows:] + dot(a[0], b[2])))
    )


def gram_sums(part, groups, picked, held_ref, goal_ref, turned_ref, out_ref, copies):
    coil = lax.axis_index("coil")
    depth = held_ref.shape[2]
    width = depth // 2
    half = part // 2
    base = part + half
    coils = goal_ref.shape[1]
    across = lax.broadcasted_iota(jnp.int32, (part, width), 1)
    down = lax.broadcasted_iota(jnp.int32, (part, width), 0) + coil * part
    first = pl.multiple_of(coil * part, 16)
    second = pl.multiple_of(width + coil * part, 16)
    row = lax.broadcasted_iota(jnp.int32, (2 * part, depth), 0)
    column = lax.broadcasted_iota(jnp.int32, (2 * part, depth), 1)
    wanted = coil * part + jnp.where(row < part, row, row - part + width)
    pick = jnp.where(column == wanted, 1.0, 0.0).astype(BF16)
    for slots in groups:
        for slot in slots:
            for copy in copies[slot]:
                copy.wait()
        lefts = []
        for slot in slots:
            if slot in picked:
                mine = [across_rows(pick, held_ref[slot]).astype(BF16)]
            else:
                turned_ref[slot] = held_ref[slot].T
                mine = [
                    turned_ref[slot, pl.ds(first, part)],
                    turned_ref[slot, pl.ds(second, part)],
                ]
            lefts.append(
                jnp.concatenate([*mine, goal_ref[slot, :, 0, :], goal_ref[slot, :, 1, :]], axis=0)
            )
        products = [
            jnp.dot(left, held_ref[slot], preferred_element_type=F32)
            for left, slot in zip(lefts, slots)
        ]
        for slot, sums in zip(slots, products):
            out = out_ref.at[slot]
            top, bottom = sums[:part], sums[part : 2 * part]
            gram_real = top[:, :width] + bottom[:, width:]
            gram_imag = top[:, width:] - bottom[:, :width]
            packed = jnp.where(across <= down, gram_real, gram_imag)
            proj_real = sums[2 * part : 2 * part + coils]
            proj_imag = sums[2 * part + coils :]
            rhs_real = proj_real[:, :width] + proj_imag[:, width:]
            rhs_imag = proj_imag[:, :width] - proj_real[:, width:]
            out[:part] = packed[:, :LANES]
            out[part:base] = jnp.concatenate(
                [packed[:half, LANES:], packed[half:, LANES:]], axis=1
            )
            out[base : base + coils] = rhs_real[:, :LANES]
            out[base + coils : base + 2 * coils] = rhs_imag[:, :LANES]
            out[base + 2 * coils : base + 3 * coils] = jnp.concatenate(
                [rhs_real[:, LANES:], rhs_imag[:, LANES:]], axis=1
            )


def tell(frames, read_ref):
    core = lax.rem(lax.axis_index("frame"), 2)
    row = lax.broadcasted_iota(jnp.int32, (8, LANES), 0)
    lane = lax.broadcasted_iota(jnp.int32, (8, LANES), 1)
    told = jnp.zeros((8, LANES), jnp.int32)
    for place in range(read_ref.shape[1]):
        told = jnp.where((row == core) & (lane == place), lax.div(read_ref[0, place], frames), told)
    return told.astype(F32)


def other_gram_kernel(
    part,
    frames,
    reads_ref,
    source_ref,
    target_ref,
    app_ref,
    interp_ref,
    out_ref,
    row_ref,
    own_held_ref,
    own_goal_ref,
    own_app_ref,
    own_interp_ref,
    held_ref,
    goal_ref,
    turned_ref,
    read_ref,
    sem,
    late_sem,
):
    core = lax.rem(lax.axis_index("frame"), 2)
    each = out_ref.shape[0]
    copies = []
    for slot in range(2 * each):
        own, place = slot // each, slot % each
        segment = 2 * place + (core if own else 1 - core)
        held = (own_held_ref if own else held_ref).at[place]
        goal = (own_goal_ref if own else goal_ref).at[place]
        copies.append(
            (
                pltpu.make_async_copy(source_ref.at[segment], held, sem.at[0, slot]),
                pltpu.make_async_copy(target_ref.at[segment], goal, sem.at[1, slot]),
            )
        )
    for pair in copies:
        for copy in pair:
            copy.start()
    late = [
        pltpu.make_async_copy(reads_ref, read_ref, late_sem.at[0]),
        pltpu.make_async_copy(app_ref, own_app_ref, late_sem.at[1]),
        pltpu.make_async_copy(interp_ref, own_interp_ref, late_sem.at[2]),
    ]
    for copy in late:
        copy.start()
    gram_sums(part, ((0,), (1, 2, 3)), (), held_ref, goal_ref, turned_ref, out_ref, copies)
    late[0].wait()
    told = tell(frames, read_ref)
    row_ref[...] = told
    for slot in range(each):
        out_ref[slot, out_ref.shape[1] - 8 :] = told
    for copy in late[1:]:
        copy.wait()
    for pair in copies[each:]:
        for copy in pair:
            copy.wait()


def own_gram_kernel(part, row_ref, held_ref, goal_ref, out_ref, turned_ref):
    slots = tuple(range(out_ref.shape[0]))
    gram_sums(part, (slots,), (2,), held_ref, goal_ref, turned_ref, out_ref, [() for _ in slots])
    for slot in slots:
        out_ref[slot, out_ref.shape[1] - 8 :] = row_ref[...]


def sum_kernel(gram_rows, partial_ref, spread_ref, rhs_ref, told_ref):
    rows = gram_rows + rhs_ref.shape[0]
    total = partial_ref[0, :rows]
    for chip in range(1, partial_ref.shape[0]):
        total = total + partial_ref[chip, :rows]
    for copy in range(spread_ref.shape[0]):
        spread_ref[copy] = total[:gram_rows]
    rhs_ref[...] = total[gram_rows:]
    for chip in range(partial_ref.shape[0]):
        told_ref[2 * chip : 2 * chip + 2] = partial_ref[chip, rows : rows + 2].astype(jnp.int32)


def solve_kernel(part, gram_ref, rhs_ref, app_ref, out_ref, flipped_ref, real_ref, imag_ref, sol_ref):
    width = 4 * part
    half = part // 2
    coils = rhs_ref.shape[0] // 3
    pieces = []
    for coil in range(4):
        block = gram_ref[coil]
        tail = block[part:]
        pieces.append(
            jnp.concatenate(
                [block[:part], jnp.concatenate([tail[:, :64], tail[:, 64:]], axis=0)], axis=1
            )
        )
    packed = jnp.concatenate(pieces, axis=0)
    flipped = packed.T
    down = lax.broadcasted_iota(jnp.int32, (width, width), 0)
    across = lax.broadcasted_iota(jnp.int32, (width, width), 1)
    diagonal = jnp.where(across == down, packed, 0.0)
    for slot in range(app_ref.shape[1]):
        flipped_ref[0, slot] = app_ref[0, slot].T
    shift = regular / width * jnp.sum(diagonal, keepdims=True)
    norm = jnp.sum(2.0 * (packed * packed) - diagonal * diagonal, keepdims=True)
    high = jnp.sqrt(norm) + shift
    scale = 2.0 / (high + shift)
    real = jnp.where(across <= down, packed, flipped)
    imag = jnp.where(across < down, -flipped, packed)
    real_ref[...] = (real + jnp.where(across == down, shift, 0.0)) * scale
    imag_ref[...] = jnp.where(across == down, 0.0, imag) * scale
    rhs_real = jnp.concatenate([rhs_ref[:coils], rhs_ref[2 * coils :, :64]], axis=1)
    rhs_imag = jnp.concatenate([rhs_ref[coils : 2 * coils], rhs_ref[2 * coils :, 64:]], axis=1)
    sol_ref[...] = jnp.concatenate([rhs_real, rhs_imag], axis=0) * scale

    def step(product, spread):
        square = spread * spread
        factor = 2.0 / (2.0 - square)
        real, imag, sol = real_ref[...], imag_ref[...], sol_ref[...]
        first = product(jnp.concatenate([real, sol], axis=0), imag)
        second = product(jnp.concatenate([real - imag, sol], axis=0), real + imag)
        cross, thin = first[:width], first[width:]
        turned = cross.T
        by_real = second[width:] - thin
        change = jnp.concatenate(
            [by_real[:coils] + thin[coils:], by_real[coils:] - thin[:coils]], axis=0
        )
        sol_ref[...] = factor * (2.0 * sol - change)
        real_ref[...] = factor * (2.0 * real - (second[:width] - cross - turned))
        imag_ref[...] = factor * (2.0 * imag - (cross - turned))
        return square / (2.0 - square)

    spread = jnp.sum((high - shift) / (high + shift))
    spread = lax.while_loop(
        lambda spread: spread > 0.998, functools.partial(step, fine_product), spread
    )
    spread = lax.while_loop(
        lambda spread: spread > settled, functools.partial(step, product), spread
    )
    sol = sol_ref[...]
    total = sol
    for _ in range(2):
        by_real = product(total, real_ref[...])
        by_imag = product(total, imag_ref[...])
        change = jnp.concatenate(
            [by_real[:coils] + by_imag[coils:], by_real[coils:] - by_imag[:coils]], axis=0
        )
        total = sol + (total - change)
    sol = total
    weights = jnp.concatenate([sol[:coils], sol[coils:]], axis=1).astype(BF16)
    for copy in range(out_ref.shape[0]):
        out_ref[copy] = weights


def select_kernel(told_ref, piece_ref, out_ref):
    pieces = [piece_ref[place].astype(F32) for place in range(piece_ref.shape[0])]
    for frame in range(out_ref.shape[0]):
        for slot in range(out_ref.shape[1]):
            wanted = jnp.broadcast_to(told_ref[frame : frame + 1, slot : slot + 1], pieces[0].shape)
            chosen = pieces[0]
            for place in range(1, len(pieces)):
                chosen = jnp.where(wanted == place, pieces[place], chosen)
            out_ref[frame, slot] = chosen.astype(BF16)


def fill_kernel(reads_ref, places_ref, weights_ref, source_ref, interp_ref, out_ref):
    frames, slots, coils, depth = weights_ref.shape
    width = depth // 2
    terms = []
    for slot in range(slots):
        holder = jnp.broadcast_to(reads_ref[:, slot : slot + 1] & (frames - 1), (coils, depth))
        chosen = weights_ref[0, slot].astype(F32)
        for frame in range(1, frames):
            chosen = jnp.where(holder == frame, weights_ref[frame, slot].astype(F32), chosen)
        real, imag = chosen[:, :width], chosen[:, width:]
        matrix = jnp.concatenate(
            [jnp.concatenate([real, -imag], axis=1), jnp.concatenate([imag, real], axis=1)], axis=0
        ).astype(BF16)
        filled = jnp.dot(matrix, source_ref[0, slot], preferred_element_type=F32).astype(BF16)
        terms.append(across_rows(filled, interp_ref[0, slot]))
    shape = terms[0].shape
    places = [jnp.broadcast_to(places_ref[:, slot : slot + 1], shape) for slot in range(slots)]
    for block in range(out_ref.shape[0]):
        total = jnp.zeros(shape, F32)
        for place, term in zip(places, terms):
            total = total + jnp.where(place == block, term, 0.0)
        out_ref[block] = total.astype(BF16)


def on_device(cal_source, cal_target, app_source, readers, blocks, interp):
    frames = lax.axis_size("frame")
    segs = lax.axis_size("seg")
    coil_count = lax.axis_size("coil")
    held, samples, depth = cal_source.shape
    coils = cal_target.shape[1]
    width = depth // 2
    part = width // coil_count
    gram_rows = part + part // 2
    rows = gram_rows + 3 * coils + 8
    slots = readers.shape[1]
    cells = interp.shape[2]

    each = held // 2
    block = jax.ShapeDtypeStruct((each, rows, LANES), F32)
    listed = pltpu.with_memory_space_constraint(readers, pltpu.HBM)
    hbm = pl.BlockSpec(memory_space=pltpu.HBM)
    vmem = pl.BlockSpec(memory_space=pltpu.VMEM)
    reading = [pltpu.SMEM(readers.shape, jnp.int32)]
    turned = pltpu.VMEM((each, depth, samples), BF16)
    cost = pl.CostEstimate(
        flops=2 * each * samples * depth * 2 * (part + coils),
        bytes_accessed=2 * each * samples * (depth + 2 * coils),
        transcendentals=0,
    )
    send, row, own_held, own_goal, own_app, own_interp = pl.pallas_call(
        functools.partial(other_gram_kernel, part, frames),
        in_specs=[hbm] * 5,
        out_shape=[
            block,
            jax.ShapeDtypeStruct((8, LANES), F32),
            jax.ShapeDtypeStruct((each, samples, depth), BF16),
            jax.ShapeDtypeStruct((each, coils, 2, samples), BF16),
            jax.ShapeDtypeStruct(app_source.shape, BF16),
            jax.ShapeDtypeStruct(interp.shape, BF16),
        ],
        scratch_shapes=[
            pltpu.VMEM((each, samples, depth), BF16),
            pltpu.VMEM((each, coils, 2, samples), BF16),
            turned,
            *reading,
            pltpu.SemaphoreType.DMA((2, held)),
            pltpu.SemaphoreType.DMA((3,)),
        ],
        compiler_params=SMALL,
        cost_estimate=cost,
    )(
        listed,
        pltpu.with_memory_space_constraint(cal_source, pltpu.HBM),
        pltpu.with_memory_space_constraint(cal_target, pltpu.HBM),
        pltpu.with_memory_space_constraint(app_source, pltpu.HBM),
        pltpu.with_memory_space_constraint(interp, pltpu.HBM),
    )
    keep = pl.pallas_call(
        functools.partial(own_gram_kernel, part),
        in_specs=[vmem, vmem, vmem],
        out_shape=block,
        scratch_shapes=[turned],
        compiler_params=SMALL,
        cost_estimate=cost,
    )(row, own_held, own_goal)
    other = lax.ppermute(send, "frame", [(frame, frame ^ 1) for frame in range(frames)])
    chips = [[2 * chip + core for chip in range(frames // 2)] for core in range(2)]
    received = lax.all_to_all(
        keep + other, "frame", 0, 0, tiled=True, axis_index_groups=chips
    )
    spread, rhs, told = pl.pallas_call(
        functools.partial(sum_kernel, gram_rows),
        out_shape=[
            jax.ShapeDtypeStruct((coil_count, gram_rows, LANES), F32),
            jax.ShapeDtypeStruct((3 * coils, LANES), F32),
            jax.ShapeDtypeStruct((frames, LANES), jnp.int32),
        ],
        compiler_params=SMALL,
    )(received)
    gram = lax.all_to_all(spread, "coil", 0, 0, tiled=True)
    weights, flipped = pl.pallas_call(
        functools.partial(solve_kernel, part),
        out_shape=[
            jax.ShapeDtypeStruct((segs, coils, depth), BF16),
            jax.ShapeDtypeStruct((1, slots, depth, app_source.shape[2]), BF16),
        ],
        scratch_shapes=[
            pltpu.VMEM((width, width), F32),
            pltpu.VMEM((width, width), F32),
            pltpu.VMEM((2 * coils, width), F32),
        ],
        compiler_params=SMALL,
    )(gram, rhs, own_app)
    pieces = lax.all_to_all(weights, "seg", 0, 0, tiled=True)
    sent = pl.pallas_call(
        select_kernel,
        out_shape=jax.ShapeDtypeStruct((frames, slots, coils, depth), BF16),
        compiler_params=SMALL,
    )(told, pieces)
    chosen = lax.all_to_all(sent, "frame", 0, 0, tiled=True)
    grid = pl.pallas_call(
        fill_kernel,
        out_shape=jax.ShapeDtypeStruct((segs, 2 * coils, cells), BF16),
        compiler_params=SMALL,
    )(readers, blocks, chosen, flipped, own_interp)
    terms = lax.all_to_all(grid, "seg", 0, 0, tiled=True)
    total = jnp.sum(terms.astype(F32), axis=0)
    power = lax.all_gather(jnp.sum(total * total, axis=0, keepdims=True), "coil", tiled=True)
    return jnp.sqrt(jnp.sum(power, axis=0, keepdims=True) + epsilon)


def solution(mesh):
    placed = (
        P("seg", "frame", None),
        P("seg", "coil", None, "frame"),
        P("frame", "seg", None, None),
        P("frame", "seg"),
        P("frame", "seg"),
        P("frame", "seg", None, None),
    )
    return jax.shard_map(
        on_device, mesh=mesh, in_specs=placed, out_specs=P("frame", "seg"), check_vma=False
    )
```

```python
import functools

import jax
import jax.numpy as jnp
from jax import lax
from jax.experimental import pallas as pl
from jax.experimental.pallas import tpu as pltpu
from jax.sharding import PartitionSpec as P

regular = 0.02
epsilon = 1e-06
settled = 0.0125
F32 = jnp.float32
BF16 = jnp.bfloat16
LANES = 128
SMALL = pltpu.CompilerParams(vmem_limit_bytes=16 * 1024 * 1024)


def across_rows(left, right):
    return lax.dot_general(left, right, (((1,), (1,)), ((), ())), preferred_element_type=F32)


def pieces_of(value, count):
    out = []
    for _ in range(count):
        piece = value.astype(BF16)
        value = value - piece.astype(F32)
        out.append(piece)
    return out


def product(left, right):
    return product_with(left, pieces_of(right, 2))


def product_with(left, b):
    rows = left.shape[0]
    a = pieces_of(left, 2)
    dot = functools.partial(jnp.dot, preferred_element_type=F32)
    first = dot(jnp.concatenate(a, axis=0), b[0])
    return first[:rows] + (first[rows:] + dot(a[0], b[1]))


def fine_product(left, right):
    rows = left.shape[0]
    a, b = pieces_of(left, 3), pieces_of(right, 3)
    dot = functools.partial(jnp.dot, preferred_element_type=F32)
    first = dot(jnp.concatenate(a, axis=0), b[0])
    second = dot(jnp.concatenate(a[:2], axis=0), b[1])
    return first[:rows] + (
        (first[rows : 2 * rows] + second[:rows])
        + (first[2 * rows :] + (second[rows:] + dot(a[0], b[2])))
    )


def gram_sums(part, groups, picked, held_ref, goal_ref, turned_ref, out_ref, copies):
    coil = lax.axis_index("coil")
    depth = held_ref.shape[2]
    width = depth // 2
    half = part // 2
    base = part + half
    coils = goal_ref.shape[1]
    across = lax.broadcasted_iota(jnp.int32, (part, width), 1)
    down = lax.broadcasted_iota(jnp.int32, (part, width), 0) + coil * part
    first = pl.multiple_of(coil * part, 16)
    second = pl.multiple_of(width + coil * part, 16)
    row = lax.broadcasted_iota(jnp.int32, (2 * part, depth), 0)
    column = lax.broadcasted_iota(jnp.int32, (2 * part, depth), 1)
    wanted = coil * part + jnp.where(row < part, row, row - part + width)
    pick = jnp.where(column == wanted, 1.0, 0.0).astype(BF16)
    for slots in groups:
        for slot in slots:
            for copy in copies[slot]:
                copy.wait()
        lefts = []
        for slot in slots:
            if slot in picked:
                mine = [across_rows(pick, held_ref[slot]).astype(BF16)]
            else:
                turned_ref[slot] = held_ref[slot].T
                mine = [
                    turned_ref[slot, pl.ds(first, part)],
                    turned_ref[slot, pl.ds(second, part)],
                ]
            lefts.append(
                jnp.concatenate([*mine, goal_ref[slot, :, 0, :], goal_ref[slot, :, 1, :]], axis=0)
            )
        products = [
            jnp.dot(left, held_ref[slot], preferred_element_type=F32)
            for left, slot in zip(lefts, slots)
        ]
        for slot, sums in zip(slots, products):
            out = out_ref.at[slot]
            top, bottom = sums[:part], sums[part : 2 * part]
            gram_real = top[:, :width] + bottom[:, width:]
            gram_imag = top[:, width:] - bottom[:, :width]
            packed = jnp.where(across <= down, gram_real, gram_imag)
            proj_real = sums[2 * part : 2 * part + coils]
            proj_imag = sums[2 * part + coils :]
            rhs_real = proj_real[:, :width] + proj_imag[:, width:]
            rhs_imag = proj_imag[:, :width] - proj_real[:, width:]
            out[:part] = packed[:, :LANES]
            out[part:base] = jnp.concatenate(
                [packed[:half, LANES:], packed[half:, LANES:]], axis=1
            )
            out[base : base + coils] = rhs_real[:, :LANES]
            out[base + coils : base + 2 * coils] = rhs_imag[:, :LANES]
            out[base + 2 * coils : base + 3 * coils] = jnp.concatenate(
                [rhs_real[:, LANES:], rhs_imag[:, LANES:]], axis=1
            )


def tell(frames, read_ref):
    core = lax.rem(lax.axis_index("frame"), 2)
    row = lax.broadcasted_iota(jnp.int32, (8, LANES), 0)
    lane = lax.broadcasted_iota(jnp.int32, (8, LANES), 1)
    told = jnp.zeros((8, LANES), jnp.int32)
    for place in range(read_ref.shape[1]):
        told = jnp.where((row == core) & (lane == place), lax.div(read_ref[0, place], frames), told)
    return told.astype(F32)


def other_gram_kernel(
    part,
    frames,
    reads_ref,
    source_ref,
    target_ref,
    app_ref,
    interp_ref,
    out_ref,
    row_ref,
    own_held_ref,
    own_goal_ref,
    own_app_ref,
    own_interp_ref,
    held_ref,
    goal_ref,
    turned_ref,
    read_ref,
    sem,
    late_sem,
):
    core = lax.rem(lax.axis_index("frame"), 2)
    each = out_ref.shape[0]
    copies = []
    for slot in range(2 * each):
        own, place = slot // each, slot % each
        segment = 2 * place + (core if own else 1 - core)
        held = (own_held_ref if own else held_ref).at[place]
        goal = (own_goal_ref if own else goal_ref).at[place]
        copies.append(
            (
                pltpu.make_async_copy(source_ref.at[segment], held, sem.at[0, slot]),
                pltpu.make_async_copy(target_ref.at[segment], goal, sem.at[1, slot]),
            )
        )
    for pair in copies:
        for copy in pair:
            copy.start()
    late = [
        pltpu.make_async_copy(reads_ref, read_ref, late_sem.at[0]),
        pltpu.make_async_copy(app_ref, own_app_ref, late_sem.at[1]),
        pltpu.make_async_copy(interp_ref, own_interp_ref, late_sem.at[2]),
    ]
    for copy in late:
        copy.start()
    gram_sums(part, ((0,), (1, 2, 3)), (), held_ref, goal_ref, turned_ref, out_ref, copies)
    late[0].wait()
    told = tell(frames, read_ref)
    row_ref[...] = told
    for slot in range(each):
        out_ref[slot, out_ref.shape[1] - 8 :] = told
    for copy in late[1:]:
        copy.wait()
    for pair in copies[each:]:
        for copy in pair:
            copy.wait()


def own_gram_kernel(part, row_ref, held_ref, goal_ref, out_ref, turned_ref):
    slots = tuple(range(out_ref.shape[0]))
    gram_sums(part, (slots,), (2,), held_ref, goal_ref, turned_ref, out_ref, [() for _ in slots])
    for slot in slots:
        out_ref[slot, out_ref.shape[1] - 8 :] = row_ref[...]


def sum_kernel(gram_rows, partial_ref, spread_ref, rhs_ref, told_ref):
    rows = gram_rows + rhs_ref.shape[0]
    total = partial_ref[0, :rows]
    for chip in range(1, partial_ref.shape[0]):
        total = total + partial_ref[chip, :rows]
    for copy in range(spread_ref.shape[0]):
        spread_ref[copy] = total[:gram_rows]
    rhs_ref[...] = total[gram_rows:]
    for chip in range(partial_ref.shape[0]):
        told_ref[2 * chip : 2 * chip + 2] = partial_ref[chip, rows : rows + 2].astype(jnp.int32)


def solve_kernel(part, gram_ref, rhs_ref, app_ref, out_ref, flipped_ref, real_ref, imag_ref, sol_ref):
    width = 4 * part
    half = part // 2
    coils = rhs_ref.shape[0] // 3
    pieces = []
    for coil in range(4):
        block = gram_ref[coil]
        tail = block[part:]
        pieces.append(
            jnp.concatenate(
                [block[:part], jnp.concatenate([tail[:, :64], tail[:, 64:]], axis=0)], axis=1
            )
        )
    packed = jnp.concatenate(pieces, axis=0)
    flipped = packed.T
    down = lax.broadcasted_iota(jnp.int32, (width, width), 0)
    across = lax.broadcasted_iota(jnp.int32, (width, width), 1)
    diagonal = jnp.where(across == down, packed, 0.0)
    for slot in range(app_ref.shape[1]):
        flipped_ref[0, slot] = app_ref[0, slot].T
    shift = regular / width * jnp.sum(diagonal, keepdims=True)
    norm = jnp.sum(2.0 * (packed * packed) - diagonal * diagonal, keepdims=True)
    high = jnp.sqrt(norm) + shift
    scale = 2.0 / (high + shift)
    real = jnp.where(across <= down, packed, flipped)
    imag = jnp.where(across < down, -flipped, packed)
    real_ref[...] = (real + jnp.where(across == down, shift, 0.0)) * scale
    imag_ref[...] = jnp.where(across == down, 0.0, imag) * scale
    rhs_real = jnp.concatenate([rhs_ref[:coils], rhs_ref[2 * coils :, :64]], axis=1)
    rhs_imag = jnp.concatenate([rhs_ref[coils : 2 * coils], rhs_ref[2 * coils :, 64:]], axis=1)
    sol_ref[...] = jnp.concatenate([rhs_real, rhs_imag], axis=0) * scale

    def step(product, spread):
        square = spread * spread
        factor = 2.0 / (2.0 - square)
        real, imag, sol = real_ref[...], imag_ref[...], sol_ref[...]
        first = product(jnp.concatenate([real, sol], axis=0), imag)
        second = product(jnp.concatenate([real - imag, sol], axis=0), real + imag)
        cross, thin = first[:width], first[width:]
        turned = cross.T
        by_real = second[width:] - thin
        change = jnp.concatenate(
            [by_real[:coils] + thin[coils:], by_real[coils:] - thin[:coils]], axis=0
        )
        sol_ref[...] = factor * (2.0 * sol - change)
        real_ref[...] = factor * (2.0 * real - (second[:width] - cross - turned))
        imag_ref[...] = factor * (2.0 * imag - (cross - turned))
        return square / (2.0 - square)

    spread = jnp.sum((high - shift) / (high + shift))
    spread = lax.while_loop(
        lambda spread: spread > 0.998, functools.partial(step, fine_product), spread
    )
    spread = lax.while_loop(
        lambda spread: spread > settled, functools.partial(step, product), spread
    )
    sol = sol_ref[...]
    total = sol
    real_pieces, imag_pieces = pieces_of(real_ref[...], 2), pieces_of(imag_ref[...], 2)
    for _ in range(2):
        by_real = product_with(total, real_pieces)
        by_imag = product_with(total, imag_pieces)
        change = jnp.concatenate(
            [by_real[:coils] + by_imag[coils:], by_real[coils:] - by_imag[:coils]], axis=0
        )
        total = sol + (total - change)
    sol = total
    weights = jnp.concatenate([sol[:coils], sol[coils:]], axis=1).astype(BF16)
    for copy in range(out_ref.shape[0]):
        out_ref[copy] = weights


def select_kernel(told_ref, piece_ref, out_ref):
    pieces = [piece_ref[place].astype(F32) for place in range(piece_ref.shape[0])]
    for frame in range(out_ref.shape[0]):
        for slot in range(out_ref.shape[1]):
            wanted = jnp.broadcast_to(told_ref[frame : frame + 1, slot : slot + 1], pieces[0].shape)
            chosen = pieces[0]
            for place in range(1, len(pieces)):
                chosen = jnp.where(wanted == place, pieces[place], chosen)
            out_ref[frame, slot] = chosen.astype(BF16)


def fill_kernel(reads_ref, places_ref, weights_ref, source_ref, interp_ref, out_ref):
    frames, slots, coils, depth = weights_ref.shape
    width = depth // 2
    terms = []
    for slot in range(slots):
        holder = jnp.broadcast_to(reads_ref[:, slot : slot + 1] & (frames - 1), (coils, depth))
        chosen = weights_ref[0, slot].astype(F32)
        for frame in range(1, frames):
            chosen = jnp.where(holder == frame, weights_ref[frame, slot].astype(F32), chosen)
        real, imag = chosen[:, :width], chosen[:, width:]
        matrix = jnp.concatenate(
            [jnp.concatenate([real, -imag], axis=1), jnp.concatenate([imag, real], axis=1)], axis=0
        ).astype(BF16)
        filled = jnp.dot(matrix, source_ref[0, slot], preferred_element_type=F32).astype(BF16)
        terms.append(across_rows(filled, interp_ref[0, slot]))
    shape = terms[0].shape
    places = [jnp.broadcast_to(places_ref[:, slot : slot + 1], shape) for slot in range(slots)]
    for block in range(out_ref.shape[0]):
        total = jnp.zeros(shape, F32)
        for place, term in zip(places, terms):
            total = total + jnp.where(place == block, term, 0.0)
        out_ref[block] = total.astype(BF16)


def on_device(cal_source, cal_target, app_source, readers, blocks, interp):
    frames = lax.axis_size("frame")
    segs = lax.axis_size("seg")
    coil_count = lax.axis_size("coil")
    held, samples, depth = cal_source.shape
    coils = cal_target.shape[1]
    width = depth // 2
    part = width // coil_count
    gram_rows = part + part // 2
    rows = gram_rows + 3 * coils + 8
    slots = readers.shape[1]
    cells = interp.shape[2]

    each = held // 2
    block = jax.ShapeDtypeStruct((each, rows, LANES), F32)
    listed = pltpu.with_memory_space_constraint(readers, pltpu.HBM)
    hbm = pl.BlockSpec(memory_space=pltpu.HBM)
    vmem = pl.BlockSpec(memory_space=pltpu.VMEM)
    reading = [pltpu.SMEM(readers.shape, jnp.int32)]
    turned = pltpu.VMEM((each, depth, samples), BF16)
    cost = pl.CostEstimate(
        flops=2 * each * samples * depth * 2 * (part + coils),
        bytes_accessed=2 * each * samples * (depth + 2 * coils),
        transcendentals=0,
    )
    send, row, own_held, own_goal, own_app, own_interp = pl.pallas_call(
        functools.partial(other_gram_kernel, part, frames),
        in_specs=[hbm] * 5,
        out_shape=[
            block,
            jax.ShapeDtypeStruct((8, LANES), F32),
            jax.ShapeDtypeStruct((each, samples, depth), BF16),
            jax.ShapeDtypeStruct((each, coils, 2, samples), BF16),
            jax.ShapeDtypeStruct(app_source.shape, BF16),
            jax.ShapeDtypeStruct(interp.shape, BF16),
        ],
        scratch_shapes=[
            pltpu.VMEM((each, samples, depth), BF16),
            pltpu.VMEM((each, coils, 2, samples), BF16),
            turned,
            *reading,
            pltpu.SemaphoreType.DMA((2, held)),
            pltpu.SemaphoreType.DMA((3,)),
        ],
        compiler_params=SMALL,
        cost_estimate=cost,
    )(
        listed,
        pltpu.with_memory_space_constraint(cal_source, pltpu.HBM),
        pltpu.with_memory_space_constraint(cal_target, pltpu.HBM),
        pltpu.with_memory_space_constraint(app_source, pltpu.HBM),
        pltpu.with_memory_space_constraint(interp, pltpu.HBM),
    )
    keep = pl.pallas_call(
        functools.partial(own_gram_kernel, part),
        in_specs=[vmem, vmem, vmem],
        out_shape=block,
        scratch_shapes=[turned],
        compiler_params=SMALL,
        cost_estimate=cost,
    )(row, own_held, own_goal)
    other = lax.ppermute(send, "frame", [(frame, frame ^ 1) for frame in range(frames)])
    chips = [[2 * chip + core for chip in range(frames // 2)] for core in range(2)]
    received = lax.all_to_all(
        keep + other, "frame", 0, 0, tiled=True, axis_index_groups=chips
    )
    spread, rhs, told = pl.pallas_call(
        functools.partial(sum_kernel, gram_rows),
        out_shape=[
            jax.ShapeDtypeStruct((coil_count, gram_rows, LANES), F32),
            jax.ShapeDtypeStruct((3 * coils, LANES), F32),
            jax.ShapeDtypeStruct((frames, LANES), jnp.int32),
        ],
        compiler_params=SMALL,
    )(received)
    gram = lax.all_to_all(spread, "coil", 0, 0, tiled=True)
    weights, flipped = pl.pallas_call(
        functools.partial(solve_kernel, part),
        out_shape=[
            jax.ShapeDtypeStruct((segs, coils, depth), BF16),
            jax.ShapeDtypeStruct((1, slots, depth, app_source.shape[2]), BF16),
        ],
        scratch_shapes=[
            pltpu.VMEM((width, width), F32),
            pltpu.VMEM((width, width), F32),
            pltpu.VMEM((2 * coils, width), F32),
        ],
        compiler_params=SMALL,
    )(gram, rhs, own_app)
    pieces = lax.all_to_all(weights, "seg", 0, 0, tiled=True)
    sent = pl.pallas_call(
        select_kernel,
        out_shape=jax.ShapeDtypeStruct((frames, slots, coils, depth), BF16),
        compiler_params=SMALL,
    )(told, pieces)
    chosen = lax.all_to_all(sent, "frame", 0, 0, tiled=True)
    grid = pl.pallas_call(
        fill_kernel,
        out_shape=jax.ShapeDtypeStruct((segs, 2 * coils, cells), BF16),
        compiler_params=SMALL,
    )(readers, blocks, chosen, flipped, own_interp)
    terms = lax.all_to_all(grid, "seg", 0, 0, tiled=True)
    total = jnp.sum(terms.astype(F32), axis=0)
    power = lax.all_gather(jnp.sum(total * total, axis=0, keepdims=True), "coil", tiled=True)
    return jnp.sqrt(jnp.sum(power, axis=0, keepdims=True) + epsilon)


def solution(mesh):
    placed = (
        P("seg", "frame", None),
        P("seg", "coil", None, "frame"),
        P("frame", "seg", None, None),
        P("frame", "seg"),
        P("frame", "seg"),
        P("frame", "seg", None, None),
    )
    return jax.shard_map(
        on_device, mesh=mesh, in_specs=placed, out_specs=P("frame", "seg"), check_vma=False
    )
```

```python
import functools

import jax
import jax.numpy as jnp
from jax import lax
from jax.experimental import pallas as pl
from jax.experimental.pallas import tpu as pltpu
from jax.sharding import PartitionSpec as P

regular = 0.02
epsilon = 1e-06
settled = 0.0125
F32 = jnp.float32
BF16 = jnp.bfloat16
LANES = 128
SMALL = pltpu.CompilerParams(vmem_limit_bytes=16 * 1024 * 1024)


def across_rows(left, right):
    return lax.dot_general(left, right, (((1,), (1,)), ((), ())), preferred_element_type=F32)


def pieces_of(value, count):
    out = []
    for _ in range(count):
        piece = value.astype(BF16)
        value = value - piece.astype(F32)
        out.append(piece)
    return out


def product(left, right):
    return product_with(left, pieces_of(right, 2))


def product_with(left, b):
    rows = left.shape[0]
    a = pieces_of(left, 2)
    dot = functools.partial(jnp.dot, preferred_element_type=F32)
    first = dot(jnp.concatenate(a, axis=0), b[0])
    return first[:rows] + (first[rows:] + dot(a[0], b[1]))


def fine_product(left, right):
    rows = left.shape[0]
    a, b = pieces_of(left, 3), pieces_of(right, 3)
    dot = functools.partial(jnp.dot, preferred_element_type=F32)
    first = dot(jnp.concatenate(a, axis=0), b[0])
    second = dot(jnp.concatenate(a[:2], axis=0), b[1])
    return first[:rows] + (
        (first[rows : 2 * rows] + second[:rows])
        + (first[2 * rows :] + (second[rows:] + dot(a[0], b[2])))
    )


def gram_sums(part, groups, picked, held_ref, goal_ref, turned_ref, out_ref, copies):
    coil = lax.axis_index("coil")
    depth = held_ref.shape[2]
    width = depth // 2
    half = part // 2
    base = part + half
    coils = goal_ref.shape[1]
    across = lax.broadcasted_iota(jnp.int32, (part, width), 1)
    down = lax.broadcasted_iota(jnp.int32, (part, width), 0) + coil * part
    first = pl.multiple_of(coil * part, 16)
    second = pl.multiple_of(width + coil * part, 16)
    row = lax.broadcasted_iota(jnp.int32, (2 * part, depth), 0)
    column = lax.broadcasted_iota(jnp.int32, (2 * part, depth), 1)
    wanted = coil * part + jnp.where(row < part, row, row - part + width)
    pick = jnp.where(column == wanted, 1.0, 0.0).astype(BF16)
    for slots in groups:
        for slot in slots:
            for copy in copies[slot]:
                copy.wait()
        lefts = []
        for slot in slots:
            if slot in picked:
                mine = [across_rows(pick, held_ref[slot]).astype(BF16)]
            else:
                turned_ref[slot] = held_ref[slot].T
                mine = [
                    turned_ref[slot, pl.ds(first, part)],
                    turned_ref[slot, pl.ds(second, part)],
                ]
            lefts.append(
                jnp.concatenate([*mine, goal_ref[slot, :, 0, :], goal_ref[slot, :, 1, :]], axis=0)
            )
        products = [
            jnp.dot(left, held_ref[slot], preferred_element_type=F32)
            for left, slot in zip(lefts, slots)
        ]
        for slot, sums in zip(slots, products):
            out = out_ref.at[slot]
            top, bottom = sums[:part], sums[part : 2 * part]
            gram_real = top[:, :width] + bottom[:, width:]
            gram_imag = top[:, width:] - bottom[:, :width]
            packed = jnp.where(across <= down, gram_real, gram_imag)
            proj_real = sums[2 * part : 2 * part + coils]
            proj_imag = sums[2 * part + coils :]
            rhs_real = proj_real[:, :width] + proj_imag[:, width:]
            rhs_imag = proj_imag[:, :width] - proj_real[:, width:]
            out[:part] = packed[:, :LANES]
            out[part:base] = jnp.concatenate(
                [packed[:half, LANES:], packed[half:, LANES:]], axis=1
            )
            out[base : base + coils] = rhs_real[:, :LANES]
            out[base + coils : base + 2 * coils] = rhs_imag[:, :LANES]
            out[base + 2 * coils : base + 3 * coils] = jnp.concatenate(
                [rhs_real[:, LANES:], rhs_imag[:, LANES:]], axis=1
            )


def tell(frames, read_ref):
    core = lax.rem(lax.axis_index("frame"), 2)
    row = lax.broadcasted_iota(jnp.int32, (8, LANES), 0)
    lane = lax.broadcasted_iota(jnp.int32, (8, LANES), 1)
    told = jnp.zeros((8, LANES), jnp.int32)
    for place in range(read_ref.shape[1]):
        told = jnp.where((row == core) & (lane == place), lax.div(read_ref[0, place], frames), told)
    return told.astype(F32)


def other_gram_kernel(
    part,
    frames,
    reads_ref,
    source_ref,
    target_ref,
    app_ref,
    interp_ref,
    out_ref,
    row_ref,
    own_held_ref,
    own_goal_ref,
    own_app_ref,
    own_interp_ref,
    held_ref,
    goal_ref,
    turned_ref,
    read_ref,
    sem,
    late_sem,
):
    core = lax.rem(lax.axis_index("frame"), 2)
    each = out_ref.shape[0]
    copies = []
    for slot in range(2 * each):
        own, place = slot // each, slot % each
        segment = 2 * place + (core if own else 1 - core)
        held = (own_held_ref if own else held_ref).at[place]
        goal = (own_goal_ref if own else goal_ref).at[place]
        copies.append(
            (
                pltpu.make_async_copy(source_ref.at[segment], held, sem.at[0, slot]),
                pltpu.make_async_copy(target_ref.at[segment], goal, sem.at[1, slot]),
            )
        )
    quarter = held_ref.shape[1] // 4
    first = [
        pltpu.make_async_copy(
            source_ref.at[1 - core, pl.ds(run * quarter, quarter)],
            held_ref.at[0, pl.ds(run * quarter, quarter)],
            late_sem.at[3 + run],
        )
        for run in range(4)
    ]
    copies[0] = (*first, copies[0][1])
    for pair in copies:
        for copy in pair:
            copy.start()
    late = [
        pltpu.make_async_copy(reads_ref, read_ref, late_sem.at[0]),
        pltpu.make_async_copy(app_ref, own_app_ref, late_sem.at[1]),
        pltpu.make_async_copy(interp_ref, own_interp_ref, late_sem.at[2]),
    ]
    for copy in late:
        copy.start()
    gram_sums(part, ((0,), (1, 2, 3)), (), held_ref, goal_ref, turned_ref, out_ref, copies)
    late[0].wait()
    told = tell(frames, read_ref)
    row_ref[...] = told
    for slot in range(each):
        out_ref[slot, out_ref.shape[1] - 8 :] = told
    for copy in late[1:]:
        copy.wait()
    for pair in copies[each:]:
        for copy in pair:
            copy.wait()


def own_gram_kernel(part, row_ref, held_ref, goal_ref, out_ref, turned_ref):
    slots = tuple(range(out_ref.shape[0]))
    gram_sums(part, (slots,), (2,), held_ref, goal_ref, turned_ref, out_ref, [() for _ in slots])
    for slot in slots:
        out_ref[slot, out_ref.shape[1] - 8 :] = row_ref[...]


def sum_kernel(gram_rows, partial_ref, spread_ref, rhs_ref, told_ref):
    rows = gram_rows + rhs_ref.shape[0]
    total = partial_ref[0, :rows]
    for chip in range(1, partial_ref.shape[0]):
        total = total + partial_ref[chip, :rows]
    for copy in range(spread_ref.shape[0]):
        spread_ref[copy] = total[:gram_rows]
    rhs_ref[...] = total[gram_rows:]
    for chip in range(partial_ref.shape[0]):
        told_ref[2 * chip : 2 * chip + 2] = partial_ref[chip, rows : rows + 2].astype(jnp.int32)


def solve_kernel(part, gram_ref, rhs_ref, app_ref, out_ref, flipped_ref, real_ref, imag_ref, sol_ref):
    width = 4 * part
    half = part // 2
    coils = rhs_ref.shape[0] // 3
    pieces = []
    for coil in range(4):
        block = gram_ref[coil]
        tail = block[part:]
        pieces.append(
            jnp.concatenate(
                [block[:part], jnp.concatenate([tail[:, :64], tail[:, 64:]], axis=0)], axis=1
            )
        )
    packed = jnp.concatenate(pieces, axis=0)
    flipped = packed.T
    down = lax.broadcasted_iota(jnp.int32, (width, width), 0)
    across = lax.broadcasted_iota(jnp.int32, (width, width), 1)
    diagonal = jnp.where(across == down, packed, 0.0)
    for slot in range(app_ref.shape[1]):
        flipped_ref[0, slot] = app_ref[0, slot].T
    shift = regular / width * jnp.sum(diagonal, keepdims=True)
    norm = jnp.sum(2.0 * (packed * packed) - diagonal * diagonal, keepdims=True)
    high = jnp.sqrt(norm) + shift
    scale = 2.0 / (high + shift)
    real = jnp.where(across <= down, packed, flipped)
    imag = jnp.where(across < down, -flipped, packed)
    real_ref[...] = (real + jnp.where(across == down, shift, 0.0)) * scale
    imag_ref[...] = jnp.where(across == down, 0.0, imag) * scale
    rhs_real = jnp.concatenate([rhs_ref[:coils], rhs_ref[2 * coils :, :64]], axis=1)
    rhs_imag = jnp.concatenate([rhs_ref[coils : 2 * coils], rhs_ref[2 * coils :, 64:]], axis=1)
    sol_ref[...] = jnp.concatenate([rhs_real, rhs_imag], axis=0) * scale

    def step(product, spread):
        square = spread * spread
        factor = 2.0 / (2.0 - square)
        real, imag, sol = real_ref[...], imag_ref[...], sol_ref[...]
        first = product(jnp.concatenate([real, sol], axis=0), imag)
        second = product(jnp.concatenate([real - imag, sol], axis=0), real + imag)
        cross, thin = first[:width], first[width:]
        turned = cross.T
        by_real = second[width:] - thin
        change = jnp.concatenate(
            [by_real[:coils] + thin[coils:], by_real[coils:] - thin[:coils]], axis=0
        )
        sol_ref[...] = factor * (2.0 * sol - change)
        real_ref[...] = factor * (2.0 * real - (second[:width] - cross - turned))
        imag_ref[...] = factor * (2.0 * imag - (cross - turned))
        return square / (2.0 - square)

    spread = jnp.sum((high - shift) / (high + shift))
    spread = lax.while_loop(
        lambda spread: spread > 0.998, functools.partial(step, fine_product), spread
    )
    spread = lax.while_loop(
        lambda spread: spread > settled, functools.partial(step, product), spread
    )
    sol = sol_ref[...]
    total = sol
    real_pieces, imag_pieces = pieces_of(real_ref[...], 2), pieces_of(imag_ref[...], 2)
    for _ in range(2):
        by_real = product_with(total, real_pieces)
        by_imag = product_with(total, imag_pieces)
        change = jnp.concatenate(
            [by_real[:coils] + by_imag[coils:], by_real[coils:] - by_imag[:coils]], axis=0
        )
        total = sol + (total - change)
    sol = total
    weights = jnp.concatenate([sol[:coils], sol[coils:]], axis=1).astype(BF16)
    for copy in range(out_ref.shape[0]):
        out_ref[copy] = weights


def select_kernel(told_ref, piece_ref, out_ref):
    pieces = [piece_ref[place].astype(F32) for place in range(piece_ref.shape[0])]
    for frame in range(out_ref.shape[0]):
        for slot in range(out_ref.shape[1]):
            wanted = jnp.broadcast_to(told_ref[frame : frame + 1, slot : slot + 1], pieces[0].shape)
            chosen = pieces[0]
            for place in range(1, len(pieces)):
                chosen = jnp.where(wanted == place, pieces[place], chosen)
            out_ref[frame, slot] = chosen.astype(BF16)


def fill_kernel(reads_ref, places_ref, weights_ref, source_ref, interp_ref, out_ref):
    frames, slots, coils, depth = weights_ref.shape
    width = depth // 2
    terms = []
    for slot in range(slots):
        holder = jnp.broadcast_to(reads_ref[:, slot : slot + 1] & (frames - 1), (coils, depth))
        chosen = weights_ref[0, slot].astype(F32)
        for frame in range(1, frames):
            chosen = jnp.where(holder == frame, weights_ref[frame, slot].astype(F32), chosen)
        real, imag = chosen[:, :width], chosen[:, width:]
        matrix = jnp.concatenate(
            [jnp.concatenate([real, -imag], axis=1), jnp.concatenate([imag, real], axis=1)], axis=0
        ).astype(BF16)
        filled = jnp.dot(matrix, source_ref[0, slot], preferred_element_type=F32).astype(BF16)
        terms.append(across_rows(filled, interp_ref[0, slot]))
    shape = terms[0].shape
    places = [jnp.broadcast_to(places_ref[:, slot : slot + 1], shape) for slot in range(slots)]
    for block in range(out_ref.shape[0]):
        total = jnp.zeros(shape, F32)
        for place, term in zip(places, terms):
            total = total + jnp.where(place == block, term, 0.0)
        out_ref[block] = total.astype(BF16)


def on_device(cal_source, cal_target, app_source, readers, blocks, interp):
    frames = lax.axis_size("frame")
    segs = lax.axis_size("seg")
    coil_count = lax.axis_size("coil")
    held, samples, depth = cal_source.shape
    coils = cal_target.shape[1]
    width = depth // 2
    part = width // coil_count
    gram_rows = part + part // 2
    rows = gram_rows + 3 * coils + 8
    slots = readers.shape[1]
    cells = interp.shape[2]

    each = held // 2
    block = jax.ShapeDtypeStruct((each, rows, LANES), F32)
    listed = pltpu.with_memory_space_constraint(readers, pltpu.HBM)
    hbm = pl.BlockSpec(memory_space=pltpu.HBM)
    vmem = pl.BlockSpec(memory_space=pltpu.VMEM)
    reading = [pltpu.SMEM(readers.shape, jnp.int32)]
    turned = pltpu.VMEM((each, depth, samples), BF16)
    cost = pl.CostEstimate(
        flops=2 * each * samples * depth * 2 * (part + coils),
        bytes_accessed=2 * each * samples * (depth + 2 * coils),
        transcendentals=0,
    )
    send, row, own_held, own_goal, own_app, own_interp = pl.pallas_call(
        functools.partial(other_gram_kernel, part, frames),
        in_specs=[hbm] * 5,
        out_shape=[
            block,
            jax.ShapeDtypeStruct((8, LANES), F32),
            jax.ShapeDtypeStruct((each, samples, depth), BF16),
            jax.ShapeDtypeStruct((each, coils, 2, samples), BF16),
            jax.ShapeDtypeStruct(app_source.shape, BF16),
            jax.ShapeDtypeStruct(interp.shape, BF16),
        ],
        scratch_shapes=[
            pltpu.VMEM((each, samples, depth), BF16),
            pltpu.VMEM((each, coils, 2, samples), BF16),
            turned,
            *reading,
            pltpu.SemaphoreType.DMA((2, held)),
            pltpu.SemaphoreType.DMA((7,)),
        ],
        compiler_params=SMALL,
        cost_estimate=cost,
    )(
        listed,
        pltpu.with_memory_space_constraint(cal_source, pltpu.HBM),
        pltpu.with_memory_space_constraint(cal_target, pltpu.HBM),
        pltpu.with_memory_space_constraint(app_source, pltpu.HBM),
        pltpu.with_memory_space_constraint(interp, pltpu.HBM),
    )
    keep = pl.pallas_call(
        functools.partial(own_gram_kernel, part),
        in_specs=[vmem, vmem, vmem],
        out_shape=block,
        scratch_shapes=[turned],
        compiler_params=SMALL,
        cost_estimate=cost,
    )(row, own_held, own_goal)
    other = lax.ppermute(send, "frame", [(frame, frame ^ 1) for frame in range(frames)])
    chips = [[2 * chip + core for chip in range(frames // 2)] for core in range(2)]
    received = lax.all_to_all(
        keep + other, "frame", 0, 0, tiled=True, axis_index_groups=chips
    )
    spread, rhs, told = pl.pallas_call(
        functools.partial(sum_kernel, gram_rows),
        out_shape=[
            jax.ShapeDtypeStruct((coil_count, gram_rows, LANES), F32),
            jax.ShapeDtypeStruct((3 * coils, LANES), F32),
            jax.ShapeDtypeStruct((frames, LANES), jnp.int32),
        ],
        compiler_params=SMALL,
    )(received)
    gram = lax.all_to_all(spread, "coil", 0, 0, tiled=True)
    weights, flipped = pl.pallas_call(
        functools.partial(solve_kernel, part),
        out_shape=[
            jax.ShapeDtypeStruct((segs, coils, depth), BF16),
            jax.ShapeDtypeStruct((1, slots, depth, app_source.shape[2]), BF16),
        ],
        scratch_shapes=[
            pltpu.VMEM((width, width), F32),
            pltpu.VMEM((width, width), F32),
            pltpu.VMEM((2 * coils, width), F32),
        ],
        compiler_params=SMALL,
    )(gram, rhs, own_app)
    pieces = lax.all_to_all(weights, "seg", 0, 0, tiled=True)
    sent = pl.pallas_call(
        select_kernel,
        out_shape=jax.ShapeDtypeStruct((frames, slots, coils, depth), BF16),
        compiler_params=SMALL,
    )(told, pieces)
    chosen = lax.all_to_all(sent, "frame", 0, 0, tiled=True)
    grid = pl.pallas_call(
        fill_kernel,
        out_shape=jax.ShapeDtypeStruct((segs, 2 * coils, cells), BF16),
        compiler_params=SMALL,
    )(readers, blocks, chosen, flipped, own_interp)
    terms = lax.all_to_all(grid, "seg", 0, 0, tiled=True)
    total = jnp.sum(terms.astype(F32), axis=0)
    power = lax.all_gather(jnp.sum(total * total, axis=0, keepdims=True), "coil", tiled=True)
    return jnp.sqrt(jnp.sum(power, axis=0, keepdims=True) + epsilon)


def solution(mesh):
    placed = (
        P("seg", "frame", None),
        P("seg", "coil", None, "frame"),
        P("frame", "seg", None, None),
        P("frame", "seg"),
        P("frame", "seg"),
        P("frame", "seg", None, None),
    )
    return jax.shard_map(
        on_device, mesh=mesh, in_specs=placed, out_specs=P("frame", "seg"), check_vma=False
    )
```
